32 devices in a mesh: pipe: 4 (over x, core), wide: 8 (over z, y).
Axes of the slice: x: 2, y: 2, z: 4, core: 2. Of those that a mesh axis runs over, the one named last changes fastest.
Arguments:
- page_tokens: bfloat16 [24, 40, 20, 512], P('wide'), may hold values from -6 to 6
- blank: int32 [24, 200], P('wide'), may hold values 0 or 1
- cotangent: bfloat16 [24, 200, 1024], P('wide'), may hold values from -6 to 6
- first: bfloat16 [4, 1024, 4096], P('pipe')
- second: bfloat16 [4, 4096, 1024], P('pipe'), may hold values from -0.09375 to 0.09375
- gains: float32 [4, 3, 1024], P('pipe'), may hold values from 0.5 to 1.5
- biases: float32 [4, 6, 1024], P('pipe'), may hold values from -1 to 1
- tables: float32 [2, 32, 361], replicated, may hold values from -4 to 4
Outputs:
- output: bfloat16 [24, 200, 1024], P('wide', None, 'pipe')
- input_grad: float32 [24, 40, 20, 512], P('wide', None, None, 'pipe')
- first_grad: float32 [4, 1024, 4096], P('pipe', 'wide')
- second_grad: float32 [4, 4096, 1024], P('pipe', None, 'wide')
- gains_grad: float32 [4, 3, 1024], P('pipe', None, 'wide')
- biases_grad: float32 [4, 6, 1024], P('pipe', None, 'wide')
- tables_grad: float32 [2, 32, 361], replicated
The draws below stay inside these ranges and needn't reach their ends.
Inputs may be any that keep to these rules, and one draw needn't show every extreme that they name: 1 marks a blank cell.
All inputs are finite; a program needn't handle non-finite values. No bound on the sum of `blank` on one device may be relied on, other than what follows from the above.
Results may differ from the reference program's by a relative error of at most 0.024.
Values may be sent and summed in bfloat16 or wider, within the bound.
A program may use at most 320 MiB of HBM per device.

```python
import jax
import jax.numpy as jnp
from jax import lax

D = 1024
HEADS = 32
FF = 4096
WIN = 10
GRID_H = 20
GRID_W = 10
GAIN_ROWS = 3
BIAS_ROWS = 6
MICRO = 3
CIN = 512
TOK = 200
RELS = 361
CROPS = 24
N_PIPE = 4


def draw_first(key, part):
    key = jax.random.fold_in(key, 11)
    shape = (N_PIPE, D, FF)
    sample = jnp.clip(jax.random.normal(key, shape, jnp.float32), -3.0, 3.0)
    section_ids = jnp.arange(N_PIPE).reshape(N_PIPE, 1, 1)
    columns = jnp.arange(FF).reshape(1, 1, FF)
    boost = jnp.where((section_ids % 2 == 0) & (columns >= 3 * D), 3.0, 1.0)
    return (sample * boost * D ** (-0.5)).astype(jnp.bfloat16)


def with_ends(array, key, low, high):
    longest = array.shape.index(max(array.shape))
    spots = []
    for shift in (0, 1):
        where = [jax.random.randint(jax.random.fold_in(key, axis), (), 0, length) for axis, length in enumerate(array.shape)]
        where[longest] = (where[longest] + shift) % array.shape[longest]
        spots.append(tuple(where))
    return array.at[spots[0]].set(low).at[spots[1]].set(high)


def spiked(array, rng, source, target, shards_of, factor):
    owner, partner = [(jnp.arange(array.shape[dim]) // (array.shape[dim] // shards_of)).reshape([-1 if axis == dim else 1 for axis in range(array.ndim)]) for dim in (source, target)]
    chosen = jax.random.permutation(rng, shards_of)[partner]
    strong = (owner == chosen) | (owner == (partner + shards_of // 2) % shards_of)
    return jnp.where(strong, factor * array, array)


def level_of(stream_key, dims, split, low, high):
    def one(dim, shards_of):
        heights = jax.random.uniform(jax.random.fold_in(jax.random.fold_in(stream_key, 6), dim), (shards_of,), jnp.float32, low / len(split), high / len(split))
        return jnp.repeat(jnp.exp(heights), dims[dim] // shards_of).reshape((-1,) + (1,) * (len(dims) - dim - 1))

    level = one(*split[0])
    for cut in split[1:]:
        level = level * one(*cut)
    return level


def centred(key, dims, scale, most, split=(), kind=jnp.bfloat16):
    array = jax.random.normal(key, dims, jnp.float32) * scale
    if len(split) > 0:
        array = level_of(key, dims, split, -0.22, 0.18) * array
    return jnp.clip(array, min=-most, max=most).astype(kind)


def gaussian_with(stream_key, dims, scale, most, pieces, heavy, held_as=jnp.bfloat16):
    entries = scale * jax.random.normal(stream_key, dims, jnp.float32)
    if pieces:
        entries = entries * level_of(stream_key, dims, pieces, -0.22, 0.18)
    return jnp.clip(spiked(entries, jax.random.fold_in(stream_key, 3), *heavy), -most, most).astype(held_as)


def setup_inputs(seed: int = 0) -> dict:
    keys = jax.random.split(jax.random.key(seed), 9)
    page_tokens = centred(keys[0], (CROPS, 2 * GRID_H, 2 * GRID_W, CIN), 1.0, 6.0, ((0, 8),))
    blank = with_ends((jax.random.randint(keys[1], (CROPS, TOK), 0, 4) < 1).astype(jnp.int32), jax.random.fold_in(keys[1], 1), 0, 1)
    cotangent = gaussian_with(keys[2], (CROPS, TOK, D), 1.0, 6.0, ((0, 8),), (0, 2, 8, 2.0))
    first = draw_first(jax.random.fold_in(keys[8], 71), 0)
    second = centred(keys[4], (N_PIPE, FF, D), FF ** -0.5, 0.09375, ((0, 4),))
    gains = jnp.clip(1.0 + 0.1 * jax.random.normal(keys[5], (N_PIPE, GAIN_ROWS, D), jnp.float32), 0.5, 1.5)
    biases = centred(keys[6], (N_PIPE, BIAS_ROWS, D), 0.2, 1.0, ((0, 4),), jnp.float32)
    tables = centred(keys[7], (2, HEADS, RELS), 1.0, 4.0, (), jnp.float32)
    return {"page_tokens": page_tokens, "blank": blank, "cotangent": cotangent, "first": first, "second": second, "gains": gains, "biases": biases, "tables": tables}


EPSILON = 1e-05
NEGATIVE = -1000000000.0

@jax.custom_vjp
def low(v):
    return lax.optimization_barrier(v.astype(jnp.bfloat16)).astype(jnp.float32)

@jax.custom_vjp
def low_back(v):
    return v

def low_keep(v):
    return (low(v), None)

def low_pass(kept, grad):
    return (grad,)

def back_keep(v):
    return (v, None)

def back_low(kept, grad):
    return (low(grad),)
low.defvjp(low_keep, low_pass)
low_back.defvjp(back_keep, back_low)

def round_both(values):
    return low(low_back(values))

def matmul(left, right):
    return jnp.dot(left, right, precision=lax.Precision.HIGHEST, preferred_element_type=jnp.float32)

def layer_norm(values, gain_row, shift_row):
    average = lax.optimization_barrier(jnp.mean(values, -1, keepdims=True))
    centered = values - average
    return centered * lax.rsqrt(lax.optimization_barrier(jnp.mean(centered * centered, -1, keepdims=True)) + EPSILON) * gain_row + shift_row

def gelu(values):
    return 0.5 * values * (1.0 + lax.erf(values * 0.7071067811865476))

def merge_tokens(tokens):
    channels = tokens.shape[-1]
    grid = tokens.reshape(GRID_H, 2, GRID_W, 2, channels)
    grid = jnp.transpose(grid, (0, 2, 3, 1, 4))
    return grid.reshape(GRID_H * GRID_W, 4 * channels)

def to_windows(values):
    channels = values.shape[-1]
    grid = values.reshape(GRID_H // WIN, WIN, GRID_W // WIN, WIN, channels)
    return jnp.transpose(grid, (0, 2, 1, 3, 4)).reshape(GRID_H * GRID_W, channels)

def from_windows(values):
    channels = values.shape[-1]
    grid = values.reshape(GRID_H // WIN, GRID_W // WIN, WIN, WIN, channels)
    return jnp.transpose(grid, (0, 2, 1, 3, 4)).reshape(GRID_H * GRID_W, channels)

def roll_grid(values, amount):
    channels = values.shape[-1]
    grid = values.reshape(GRID_H, GRID_W, channels)
    return jnp.roll(grid, (amount, amount), (0, 1)).reshape(GRID_H * GRID_W, channels)

def window_blank(blank_row, shifted):
    marks = blank_row[:, None]
    if shifted:
        marks = roll_grid(marks, -(WIN // 2))
    return to_windows(marks)[:, 0]

def region_ids(shifted):
    cells = jnp.arange(GRID_H * GRID_W)
    rows_at = cells // GRID_W
    cols_at = cells % GRID_W
    if shifted:
        row_band = (rows_at >= GRID_H - WIN).astype(jnp.int32) + (rows_at >= GRID_H - WIN // 2).astype(jnp.int32)
        col_band = (cols_at >= GRID_W - WIN).astype(jnp.int32) + (cols_at >= GRID_W - WIN // 2).astype(jnp.int32)
        region = row_band * 3 + col_band
    else:
        region = jnp.zeros_like(rows_at)
    return to_windows(region.reshape(-1, 1))[:, 0]

def window_mask(key_blank, shifted):
    area = WIN * WIN
    window_count = key_blank.shape[0] // area
    region = region_ids(shifted).reshape(window_count, area)
    same_region = region[:, :, None] == region[:, None, :]
    open_key = key_blank.reshape(window_count, 1, area) == 0
    own_key = jnp.eye(area, dtype=jnp.bool_)[None]
    return (same_region & (open_key | own_key))[:, None]

def relative_onehot():
    span = 2 * WIN - 1
    cells = jnp.arange(WIN * WIN)
    rows_at = cells // WIN
    cols_at = cells % WIN
    offsets = (rows_at[:, None] - rows_at[None, :] + WIN - 1) * span + (cols_at[:, None] - cols_at[None, :] + WIN - 1)
    return (offsets.reshape(-1, 1) == jnp.arange(span * span)[None, :]).astype(jnp.float32)

def split_heads(rows):
    area = WIN * WIN
    return rows.reshape(rows.shape[0] // area, area, HEADS, rows.shape[1] // HEADS)

def attention(stream, section, shifted, weights, blank_row, onehot):
    first_all, second_all, gain_all, bias_all, table_all = weights
    d_model = stream.shape[1]
    head_dim = d_model // HEADS
    area = WIN * WIN
    normed = low(layer_norm(stream, gain_all[section, 0], bias_all[section, 0]))
    if shifted:
        normed = roll_grid(normed, -(WIN // 2))
    normed = to_windows(normed)
    key_blank = window_blank(blank_row, shifted)
    projected = matmul(normed, first_all[section, :, :3 * d_model])
    queries = round_both(projected[:, :d_model] + bias_all[section, 1])
    key_rows = round_both(projected[:, d_model:2 * d_model])
    value_rows = round_both(projected[:, 2 * d_model:] + bias_all[section, 2])
    raw_scores = low_back(jnp.einsum('wqhd,wkhd->whqk', split_heads(queries), split_heads(key_rows), precision=lax.Precision.HIGHEST))
    relative = matmul(table_all[section // 2], onehot.T).reshape(HEADS, area, area)
    scores = jnp.where(window_mask(key_blank, shifted), raw_scores * head_dim ** (-0.5) + relative[None], NEGATIVE)
    topmost = lax.optimization_barrier(jnp.max(scores, -1, keepdims=True))
    exponent = jnp.exp(scores - topmost)
    probs = low(exponent / lax.optimization_barrier(jnp.sum(exponent, -1, keepdims=True)))
    mixed = jnp.einsum('whqk,wkhd->wqhd', probs, split_heads(value_rows), precision=lax.Precision.HIGHEST)
    mixed = round_both(mixed.reshape(stream.shape[0], d_model))
    result = low_back(matmul(mixed, first_all[section, :, 3 * d_model:])) + bias_all[section, 3]
    result = from_windows(result)
    if shifted:
        result = roll_grid(result, WIN // 2)
    return stream + result

def feed_forward(stream, section, weights):
    first_all, second_all, gain_all, bias_all, table_all = weights
    normed = low(layer_norm(stream, gain_all[section, 0], bias_all[section, 0]))
    preact = low_back(matmul(normed, first_all[section])) + bias_all[section, 1:5].reshape(-1)
    hidden = low(gelu(preact))
    result = low_back(matmul(hidden, second_all[section])) + bias_all[section, 5]
    return stream + result

def crop_forward(weights, tokens, blank_row, onehot):
    first_all, second_all, gain_all, bias_all, table_all = weights
    d_model = first_all.shape[1]
    merged = merge_tokens(tokens)
    normed = low(layer_norm(merged, gain_all[0, 1:3].reshape(-1), bias_all[0, 4:6].reshape(-1)))
    stream = low_back(matmul(normed, second_all[0, :2 * d_model]))
    stream = round_both(attention(stream, 0, False, weights, blank_row, onehot))
    stream = round_both(feed_forward(stream, 1, weights))
    stream = round_both(attention(stream, 2, True, weights, blank_row, onehot))
    return low(feed_forward(stream, 3, weights))

def reference(page_tokens, blank, cotangent, first, second, gains, biases, tables):
    weights = (first.astype(jnp.float32), second.astype(jnp.float32), gains, biases, tables)
    onehot = relative_onehot()
    groups = page_tokens.shape[0] // MICRO
    tokens_all = page_tokens.astype(jnp.float32).reshape((groups, MICRO) + page_tokens.shape[1:])
    blank_all = blank.reshape(groups, MICRO, blank.shape[1])
    grads_all = cotangent.astype(jnp.float32).reshape((groups, MICRO) + cotangent.shape[1:])

    def group_step(totals, inputs):
        crops_in, marks_in, grads_in = inputs

        def run_group(weight_set, crop_set):
            return jax.vmap(lambda crop_one, marks_one: crop_forward(weight_set, crop_one, marks_one, onehot))(crop_set, marks_in)
        results, pullback = jax.vjp(run_group, weights, crops_in)
        weight_grads, crop_grads = pullback(grads_in)
        totals = jax.tree.map(lambda total_now, term_now: total_now + term_now, totals, weight_grads)
        return (totals, (results, crop_grads))
    zero_set = jax.tree.map(jnp.zeros_like, weights)
    totals, (results, crop_grads) = lax.scan(group_step, zero_set, (tokens_all, blank_all, grads_all))
    output = results.reshape(cotangent.shape).astype(jnp.bfloat16)
    input_grad = crop_grads.reshape(page_tokens.shape)
    return (output, input_grad, totals[0], totals[1], totals[2], totals[3], totals[4])
```

```python
import functools
from itertools import zip_longest

import jax
import jax.numpy as jnp
import numpy as np
from jax import lax
from jax.experimental import pallas as pl
from jax.experimental.pallas import tpu as pltpu
from jax.sharding import PartitionSpec as P

HEADS = 32
WIN = 10
GRID_H = 20
GRID_W = 10
AREA = WIN * WIN
TOK = GRID_H * GRID_W
ROWS = 112
WINS = 3
M = ROWS * WINS
D = 1024
FF = 4096
CHUNK = 512
EPSILON = 1e-05
NEGATIVE = -1000000000.0
SCALE = 32 ** (-0.5)
MESH = pl.DeviceIdType.MESH
F32 = jnp.float32
BF16 = jnp.bfloat16


def shape_of(dims, kind):
    return jax.ShapeDtypeStruct(dims, kind)


def dot(left, right):
    return jnp.dot(left, right, preferred_element_type=F32)


def dot_nt(left, right):
    return lax.dot_general(left, right, (((1,), (1,)), ((), ())), preferred_element_type=F32)


def dot_tn(left, right):
    return lax.dot_general(left, right, (((0,), (0,)), ((), ())), preferred_element_type=F32)


def norm_parts(values):
    average = jnp.mean(values, -1, keepdims=True)
    centered = values - average
    inv_std = lax.rsqrt(jnp.mean(centered * centered, -1, keepdims=True) + EPSILON)
    return centered * inv_std, inv_std


def norm_backward(grad_out, values, gain):
    unit, inv_std = norm_parts(values)
    scaled = grad_out * gain
    grad_in = inv_std * (
        scaled
        - jnp.mean(scaled, -1, keepdims=True)
        - unit * jnp.mean(scaled * unit, -1, keepdims=True)
    )
    return (
        grad_in,
        jnp.sum(grad_out * unit, 0, keepdims=True),
        jnp.sum(grad_out, 0, keepdims=True),
    )


def split_dot(left, right, product=dot):
    high = left.astype(BF16)
    low = (left - high.astype(F32)).astype(BF16)
    return product(high, right) + product(low, right)


ANYWHERE = pl.BlockSpec(memory_space=pl.ANY)
IN_VMEM = pl.BlockSpec(memory_space=pltpu.VMEM)
DMA = pltpu.SemaphoreType.DMA
SPAN = 2 * WIN - 1
INNER = 256
OFFSETS = 384
GROUP = 256
GROUP_HEADS = GROUP // 32
STEPS = D // GROUP
CHUNKS = FF // CHUNK
PIECE = 256
HALF = FF // PIECE
PER = D // PIECE
RELAY = 12


class Refs:
    def __init__(self, names, refs):
        self.__dict__.update(zip(names, refs))


def lanes_at(start, size):
    return pl.ds(pl.multiple_of(start, 128), size)


def lane_masks():
    lanes = lax.broadcasted_iota(jnp.int32, (1, 128), 1)
    return [
        jnp.where((lanes >= 32 * h) & (lanes < 32 * h + 32), 1.0, 0.0).astype(BF16)
        for h in range(4)
    ]


def stacked(values, masks, rows):
    if rows > values.shape[0]:
        values = jnp.concatenate(
            [values, jnp.zeros((rows - values.shape[0], values.shape[1]), values.dtype)], 0
        )
    return jnp.concatenate([values * mask for mask in masks], 0)


def beside_ones(values, masks):
    ones = jnp.concatenate([jnp.broadcast_to(mask, (128, 128)) for mask in masks], 0)
    return jnp.concatenate([stacked(values, masks, 128), ones], 1)


def attention_forward(s, vec, weights):
    unit, _ = norm_parts(s.x[...])
    s.normed[...] = (unit * vec[0:1] + vec[3:4]).astype(BF16)
    s.acc[...] = jnp.zeros_like(s.acc)
    masks = lane_masks()

    def step(g, carry):
        weights(g)
        here = lanes_at(g * GROUP, GROUP)
        projected = dot(s.normed[...], s.w_qkv[g])
        s.qkv[0, :, here] = (projected[:, :GROUP] + vec[4:5, here]).astype(BF16)
        s.qkv[1, :, here] = projected[:, GROUP : 2 * GROUP].astype(BF16)
        s.qkv[2, :, here] = (projected[:, 2 * GROUP :] + vec[5:6, here]).astype(BF16)
        for w in range(WINS):
            rows = slice(w * ROWS, (w + 1) * ROWS)
            allowed = s.mask[w] > 0.5
            for part in range(GROUP // 128):
                lanes = lanes_at(g * GROUP + part * 128, 128)
                scores = dot_nt(s.qkv[0, rows, lanes], stacked(s.qkv[1, rows, lanes], masks, 128))
                found = []
                for h in range(4):
                    head = g * GROUP_HEADS + part * 4 + h
                    bias = s.rel[pl.ds(pl.multiple_of(head * ROWS, 8), ROWS)]
                    one = jnp.where(
                        allowed, scores[:, h * 128 : (h + 1) * 128] * SCALE + bias, NEGATIVE
                    )
                    exponent = jnp.exp(one - jnp.max(one, -1, keepdims=True)).astype(BF16)
                    s.exps[w, head] = exponent
                    found.append(exponent)
                sums = dot(jnp.concatenate(found, 1), beside_ones(s.qkv[2, rows, lanes], masks))
                scale = 1.0 / sums[:, 128:]
                s.inverse[rows, lanes] = scale
                s.mixed[rows, lanes] = (sums[:, :128] * scale).astype(BF16)
        s.acc[...] += dot(s.mixed[:, here], s.w_out[g])
        return carry

    lax.fori_loop(0, STEPS, step, 0)
    return s.x[...] + (s.acc[...] + vec[6:7])


def attention_backward(s, vec, right, vecs):
    masks = lane_masks()
    s.acc[...] = jnp.zeros_like(s.acc)

    def step(g, carry):
        here = lanes_at(g * GROUP, GROUP)
        mixed_grad = dot_nt(s.grad_a[...], s.w_out[g])
        scaled_grad = (mixed_grad * s.inverse[:, here]).astype(BF16)
        spread = (scaled_grad.astype(F32) * s.mixed[:, here].astype(F32)).astype(BF16)
        for w in range(WINS):
            rows = slice(w * ROWS, (w + 1) * ROWS)
            for part in range(GROUP // 128):
                inside = slice(part * 128, (part + 1) * 128)
                lanes = lanes_at(g * GROUP + part * 128, 128)
                grad_here = scaled_grad[rows, inside]
                prob_grad = dot_nt(
                    jnp.concatenate([grad_here, -spread[rows, inside]], 1),
                    beside_ones(s.qkv[2, rows, lanes], masks),
                )
                found = []
                draws = []
                for h in range(4):
                    head = g * GROUP_HEADS + part * 4 + h
                    exponent = s.exps[w, head]
                    score_grad = exponent.astype(F32) * prob_grad[:, h * 128 : (h + 1) * 128]
                    at = pl.ds(pl.multiple_of(head * ROWS, 8), ROWS)
                    if w == 0:
                        s.rel[at] = score_grad
                    else:
                        s.rel[at] += score_grad
                    found.append(exponent)
                    draws.append((score_grad * SCALE).astype(BF16))
                query_grad = dot(jnp.concatenate(draws, 1), stacked(s.qkv[1, rows, lanes], masks, 128))
                key_grad = dot_tn(jnp.concatenate(draws, 0), stacked(s.qkv[0, rows, lanes], masks, ROWS))
                value_grad = dot_tn(jnp.concatenate(found, 0), stacked(grad_here, masks, ROWS))
                right[0, rows, lanes] = query_grad.astype(BF16)
                right[1, rows, lanes] = key_grad[:ROWS].astype(BF16)
                right[2, rows, lanes] = value_grad[:ROWS].astype(BF16)
        joined = jnp.concatenate([right[k, :, here] for k in range(3)], 1)
        s.acc[...] += dot_nt(joined, s.w_qkv[g])
        return carry

    lax.fori_loop(0, STEPS, step, 0)
    grad_in, gain_grad, shift_grad = norm_backward(s.acc[...], s.x[...], vec[0:1])
    wide = s.grad_a[...].astype(F32)
    vecs[0:1] = gain_grad
    vecs[1:3] = jnp.zeros((2, D), F32)
    vecs[3:4] = shift_grad
    vecs[4:5] = jnp.sum(right[0].astype(F32), 0, keepdims=True)
    vecs[5:6] = jnp.sum(right[2].astype(F32), 0, keepdims=True)
    vecs[6:7] = jnp.sum(wide, 0, keepdims=True)
    vecs[7:16] = jnp.zeros((9, D), F32)
    return wide + grad_in


def gelu_parts(pre):
    cumulative = 0.5 * (1.0 + lax.erf(pre * 0.7071067811865476))
    density = jnp.exp(-0.5 * pre * pre) * 0.3989422804014327
    return (pre * cumulative).astype(BF16), (cumulative + pre * density).astype(BF16)


def mlp_forward(s, vec, weights):
    x = s.mid[...].astype(F32)
    unit, _ = norm_parts(x)
    s.normed[...] = (unit * vec[0:1] + vec[3:4]).astype(BF16)

    def product(j):
        weights(j)
        start = j % 2 * CHUNK
        bias = vec[4 + j // 2 : 5 + j // 2, start : start + CHUNK]
        s.pre[j % 2] = dot(s.normed[...], s.w1[j]) + bias

    def take(j):
        start = j % 2 * CHUNK
        term = dot(s.hidden[j // 2, :, start : start + CHUNK], s.w2[j])
        if j == 0:
            s.acc[...] = term
        else:
            s.acc[...] += term

    product(0)
    for j in range(CHUNKS):
        start = j % 2 * CHUNK
        if j + 1 < CHUNKS:
            product(j + 1)
        if j > 0:
            take(j - 1)
        values, slopes = gelu_parts(s.pre[j % 2])
        s.hidden[j // 2, :, start : start + CHUNK] = values
        s.slope[j // 2, :, start : start + CHUNK] = slopes
    take(CHUNKS - 1)
    return s.mid[...].astype(F32) + s.acc[...] + vec[8:9]


def mlp_backward(s, vec, vecs):
    def product(j):
        here = slice(j % 2 * CHUNK, (j % 2 + 1) * CHUNK)
        pre_grad = dot_nt(s.grad_m[...], s.w2[j]) * s.slope[j // 2, :, here].astype(F32)
        vecs[4 + j // 2 : 5 + j // 2, here] = jnp.sum(pre_grad, 0, keepdims=True)
        s.slope[j // 2, :, here] = pre_grad.astype(BF16)

    def take(j):
        here = slice(j % 2 * CHUNK, (j % 2 + 1) * CHUNK)
        term = dot_nt(s.slope[j // 2, :, here], s.w1[j])
        if j == 0:
            s.acc[...] = term
        else:
            s.acc[...] += term

    product(0)
    for j in range(CHUNKS):
        if j + 1 < CHUNKS:
            product(j + 1)
        take(j)
    grad_in, gain_grad, shift_grad = norm_backward(s.acc[...], s.mid[...].astype(F32), vec[0:1])
    wide = s.grad_m[...].astype(F32)
    vecs[0:1] = gain_grad
    vecs[1:3] = jnp.zeros((2, D), F32)
    vecs[3:4] = shift_grad
    vecs[8:9] = jnp.sum(wide, 0, keepdims=True)
    vecs[9:16] = jnp.zeros((7, D), F32)
    return wide + grad_in


def main_kernel(ins, outs, scratch, *refs):
    first = len(ins)
    second = first + len(outs)
    i, o, s = Refs(ins, refs[:first]), Refs(outs, refs[first:second]), Refs(scratch, refs[second:])
    p = lax.axis_index("pipe")
    w_at = lax.axis_index("wide")
    side, c = p // 2, lax.rem(p, 2)
    lower, upper = side == 0, side == 1
    pair = (p + 1 - 2 * c, w_at)
    across = (lax.rem(p + 2, 4), w_at)

    def local(source, target, sem):
        return pltpu.make_async_copy(source, target, sem)

    def remote(source, target, sent, got, to):
        return pltpu.make_async_remote_copy(
            source, target, sent, got, device_id=to, device_id_type=MESH
        )

    consts = [local(i.pack.at[k], s.hidden.at[k, :INNER], s.const_sem.at[k]) for k in range(4)]
    consts.append(local(i.pack.at[4], s.slope.at[0, :INNER], s.const_sem.at[4]))
    consts.append(local(i.roll.at[side, c], s.roll, s.const_sem.at[5]))
    picks = []
    for half in range(2):
        for source, target in (
            (i.pick.at[half, : 3 * ROWS], s.slope.at[1 + half]),
            (i.pick.at[half, 3 * ROWS :], s.slope.at[3, half * ROWS : (half + 1) * ROWS]),
        ):
            picks.append(local(source, target, s.pick_sem.at[len(picks)]))
    cot = local(i.cot.at[c], s.mixed, s.const_sem.at[6])

    def token_copy(k):
        return local(i.tokens.at[(c * WINS + k) // 2], s.tokens.at[k % 2], s.token_sem.at[k % 2])

    def cotangent_copy(k):
        return local(i.cotangent.at[k], s.cotangent, s.token_sem.at[0])

    for copy in consts:
        copy.start()

    @pl.when(lower)
    def _():
        token_copy(0).start()
        token_copy(1).start()
        for copy in picks:
            copy.start()

    @pl.when(upper)
    def _():
        cotangent_copy(0).start()
        cot.start()

    for row in range(3):
        s.vec[c, row : row + 1] = i.gains[row]
    for row in range(6):
        s.vec[c, 3 + row : 4 + row] = i.biases[row]
    s.vec[c, 9:16] = jnp.zeros((7, D), F32)
    barrier = pltpu.get_barrier_semaphore()
    for step in range(1, 4):
        pl.semaphore_signal(
            barrier, inc=1, device_id=(lax.rem(p + step, 4), w_at), device_id_type=MESH
        )
    pl.semaphore_wait(barrier, 3)
    vec_copy = remote(s.vec.at[c], s.vec.at[c], s.vec_sem.at[0], s.vec_sem.at[1], pair)
    vec_copy.start()

    attention_parts = []
    for g in range(STEPS):
        for k in range(3):
            start = k * D + g * GROUP
            attention_parts.append(
                (i.first.at[:, start : start + GROUP], s.w_qkv.at[g, :, k * GROUP : (k + 1) * GROUP])
            )
        attention_parts.append((i.first.at[g * GROUP : (g + 1) * GROUP, 3 * D :], s.w_out.at[g]))
    mlp_parts = []
    for j in range(CHUNKS):
        here = slice(j * CHUNK, (j + 1) * CHUNK)
        mlp_parts.append((i.first.at[:, here], s.w1.at[j]))
        mlp_parts.append((i.second.at[here], s.w2.at[j]))
    merge_parts = []
    for g in range(STEPS):
        here = slice(g * GROUP, (g + 1) * GROUP)
        merge_parts.append((i.second.at[: 2 * D, here], s.w_merge.at[:, here]))

    def load(parts, got):
        for k, (source, target) in enumerate(parts):
            local(source, target, got.at[k]).start()

    def gifts(parts, got):
        return [
            remote(source, target, s.give_sem.at[k], got.at[k], pair)
            for k, (source, target) in enumerate(parts)
        ]

    def give(parts, got):
        for copy in gifts(parts, got):
            copy.start()

    def merge_gifts():
        return [
            remote(source, target, s.merge_sem.at[1, k], s.merge_sem.at[0, k], pair)
            for k, (source, target) in enumerate(merge_parts)
        ]

    mine = pl.ds(pl.multiple_of(c * M, 16), M)

    class Delivery:
        def __init__(self, section, item, source, target):
            self.here = c == section
            self.ends = source, target
            self.sems = s.give_out.at[section, item], s.give_in.at[section, item]

        def local(self):
            return local(*self.ends, self.sems[0])

        def remote(self):
            return remote(*self.ends, *self.sems, pair)

        def start(self):
            pl.when(self.here)(lambda: self.local().start())
            pl.when(jnp.logical_not(self.here))(lambda: self.remote().start())

        def wait(self):
            pl.when(self.here)(lambda: self.local().wait())
            pl.when(jnp.logical_not(self.here))(lambda: self.remote().wait_send())

        def wait_recv(self):
            pl.when(self.here)(lambda: self.remote().wait_recv())

    def deliver_rows(section, item, source):
        target = (o.left, o.left_b, o.right_b)[item]
        return Delivery(section, item, source, target.at[mine])

    def deliver_vecs(section, source):
        return Delivery(section, 3, source, o.vecs.at[c])

    def deliver_right(section, source, where=range(4)):
        return [Delivery(section, 4 + k, source.at[k], o.right.at[k, mine]) for k in where]

    def deliver_hidden(section, source, where):
        return [Delivery(section, 8 + k, source.at[k], o.hidden.at[k, mine]) for k in where]

    def start_all(copies):
        for copy in copies:
            copy.start()

    def wait_all(copies):
        for copy in copies:
            copy.wait()

    @pl.when(c == 0)
    def _():
        @pl.when(lower)
        def _():
            start_all(merge_gifts())
            for k, (source, target) in enumerate(merge_parts):
                local(source, target, s.merge_sem.at[0, k]).start()

        @pl.when(upper)
        def _():
            give(attention_parts, s.attention_sem)

        load(attention_parts, s.attention_sem)

    @pl.when(c == 1)
    def _():
        give(mlp_parts, s.mlp_sem)
        load(mlp_parts, s.mlp_sem)

    def arrived(target, sem):
        local(target, target, sem).wait()

    def attention_weights(g):
        for k in range(3):
            arrived(s.w_qkv.at[g, :, k * GROUP : (k + 1) * GROUP], s.attention_sem.at[4 * g + k])
        arrived(s.w_out.at[g], s.attention_sem.at[4 * g + 3])

    def mlp_weights(j):
        arrived(s.w1.at[j], s.mlp_sem.at[2 * j])
        arrived(s.w2.at[j], s.mlp_sem.at[2 * j + 1])

    for copy in consts:
        copy.wait()

    def outer(ri):
        block = s.hidden.at[ri // 2] if ri < 8 else s.slope.at[0]
        return block[:INNER, ri % 2 * OFFSETS : (ri % 2 + 1) * OFFSETS]

    def inner(ci):
        block = s.hidden.at[ci // 2] if ci < 8 else s.slope.at[0]
        return block[ci % 2 * 128 : (ci % 2 + 1) * 128, 2 * OFFSETS :]

    s.table[...] = jnp.zeros_like(s.table)
    s.table[:, : SPAN * SPAN] = jnp.where(lower, i.tables[0], i.tables[1])
    table = s.table[...]
    wide = jnp.concatenate([split_dot(table, outer(ri), dot_nt) for ri in range(WIN)], 0)
    s.rel[...] = jnp.zeros_like(s.rel)
    for ci in range(WIN):
        rows = split_dot(wide, inner(ci), dot_nt)
        for ri in range(WIN):
            s.rel[pl.ds(ri * WIN + ci, HEADS, stride=ROWS), :] = rows[ri * HEADS : (ri + 1) * HEADS]

    closed = dot(i.blank[...].astype(F32).astype(BF16), i.keys[...])
    at_row = lax.broadcasted_iota(jnp.int32, (ROWS, 128), 0)
    at_lane = lax.broadcasted_iota(jnp.int32, (ROWS, 128), 1)
    own = jnp.where(at_row == at_lane, 1.0, 0.0)
    for k in range(WINS):
        found = []
        for rolled in range(2):
            for core in range(2):
                crop, part = (WINS * core + k) // 2, (WINS * core + k) % 2
                start = (2 * rolled + part) * 128
                found.append((closed[crop : crop + 1, start : start + 128], i.regions[2 * rolled + part]))
        near = [[jnp.where(c == 0, found[2 * t][u], found[2 * t + 1][u]) for u in range(2)] for t in range(2)]
        row, region = [jnp.where(lower, near[0][u], near[1][u]) for u in range(2)]
        s.mask[k] = region * jnp.maximum(1.0 - row, own)

    @pl.when(upper)
    def _():
        cot.wait()
        for crop in range(WINS):
            cotangent_copy(crop).wait()
            term = dot(s.mixed[:, crop * 256 : crop * 256 + TOK], s.cotangent[...])
            if crop == 0:
                s.acc[...] = term
            else:
                s.acc[...] += term
            if crop + 1 < WINS:
                cotangent_copy(crop + 1).start()
        s.grad_m[...] = s.acc[...].astype(BF16)
        deliver_rows(1, 2, s.grad_m).start()

    arrived(s.vec.at[1 - c], s.vec_sem.at[1])
    vec_a, vec_m = s.vec.at[0], s.vec.at[1]

    def merge_saved():
        return [
            local(s.hidden.at[2 + k], o.tokens.at[k], s.out_sem.at[1 + k]) for k in range(2)
        ] + deliver_hidden(0, s.hidden, range(2))

    @pl.when(lower)
    def _():
        for copy in picks:
            copy.wait()
        gain = jnp.concatenate([vec_a[1:2], vec_a[2:3]], 1)
        shift = jnp.concatenate([vec_a[7:8], vec_a[8:9]], 1)
        area = 4 * TOK
        for k in range(WINS):
            rows = slice(k * ROWS, (k + 1) * ROWS)
            half = lax.rem(c + k, 2)
            token_copy(k).wait()
            picked = dot(s.slope[1 + half, :, :area], s.tokens[k % 2])
            last = s.slope[3, pl.ds(pl.multiple_of(half * ROWS, 16), ROWS), :area]
            picked = [picked[t * ROWS : (t + 1) * ROWS] for t in range(3)] + [dot(last, s.tokens[k % 2])]
            if k + 2 < WINS:
                token_copy(k + 2).start()
            merged = jnp.concatenate(picked, 1)
            s.hidden[2, rows] = merged[:, :D].astype(BF16)
            s.hidden[3, rows] = merged[:, D:].astype(BF16)
            unit, _ = norm_parts(merged)
            normed = (unit * gain + shift).astype(BF16)
            s.hidden[0, rows] = normed[:, :D]
            s.hidden[1, rows] = normed[:, D:]
        start_all(merge_saved())

        @pl.when(c == 0)
        def _():
            give(attention_parts, s.attention_sem)


        for g in range(STEPS):
            here = slice(g * GROUP, (g + 1) * GROUP)
            arrived(s.w_merge.at[:, here], s.merge_sem.at[0, g])
            s.x[:, here] = dot(s.hidden[0], s.w_merge[:D, here]) + dot(s.hidden[1], s.w_merge[D:, here])

    shared = pl.ds(pl.multiple_of((1 - c) * (WINS - 1) * ROWS, 16), ROWS)
    shared_copy = remote(
        s.hop_out.at[shared], s.hop_out.at[M:], s.hop_sem.at[0], s.hop_sem.at[1], pair
    )

    def hop_copy(target):
        return remote(s.grad_a, target, s.hop_sem.at[2], s.hop_sem.at[3], across)

    def hop(target):
        shared_copy.start()
        near = dot(s.roll[:, :M], s.hop_out[:M])
        shared_copy.wait_recv()
        s.grad_a[...] = (near + dot(s.roll[:, M:], s.hop_out[M:])).astype(BF16)
        hop_copy(target).start()
        shared_copy.wait_send()

    @pl.when(upper)
    def _():
        hop_copy(s.grad_a).wait_recv()
        s.x[...] = s.grad_a[...].astype(F32)

    s.mid[...] = attention_forward(s, vec_a, attention_weights).astype(BF16)
    normed_out = deliver_rows(0, 0, s.normed)
    mixed_out = deliver_rows(0, 1, s.mixed)
    normed_out.start()
    mixed_out.start()
    normed_out.wait()

    @pl.when(lower)
    def _():
        wait_all(merge_saved())

    s.hop_out[:M] = mlp_forward(s, vec_m, mlp_weights).astype(BF16)
    normed_out = deliver_rows(1, 0, s.normed)
    normed_out.start()

    over = range(RELAY // PER)

    def hidden_over(k, core):
        rows = pl.ds(pl.multiple_of(core * M, 16), M)
        return remote(
            s.hidden.at[k], o.hidden.at[k, rows], s.over_sem.at[k], s.over_in.at[core, k], (2, w_at)
        )

    def output_copy(owner):
        wide = D // 4
        source = s.hop_out.at[:M, owner * wide : (owner + 1) * wide]
        return (
            local(source, o.outs.at[c], s.piece_sem.at[owner]),
            remote(source, o.outs.at[c], s.piece_sem.at[owner], s.outs_in.at[c], (owner, w_at)),
        )

    hidden_upper = deliver_hidden(1, s.hidden, range(4))
    hidden_lower = deliver_hidden(1, s.hidden, range(RELAY // PER, 4))
    grad_m_out = deliver_rows(1, 2, s.grad_m)

    @pl.when(lower)
    def _():
        hop(s.grad_a)
        start_all(hidden_lower)
        hop_copy(s.grad_a).wait_send()
        for k in over:
            hidden_over(k, c).start()
        hop_copy(s.grad_m).wait_recv()
        grad_m_out.start()

    @pl.when(upper)
    def _():
        start_all(hidden_upper)
        for owner in range(4):
            here, there = output_copy(owner)
            pl.when(p == owner)(here.start)
            pl.when(p != owner)(there.start)

    s.grad_a[...] = mlp_backward(s, vec_m, s.vecs_m).astype(BF16)
    right_m_out = deliver_right(1, s.slope)
    vecs_m_out = deliver_vecs(1, s.vecs_m)
    start_all(right_m_out)
    vecs_m_out.start()

    @pl.when(lower)
    def _():
        wait_all(hidden_lower)
        for k in over:
            hidden_over(k, c).wait_send()

    @pl.when(upper)
    def _():
        wait_all(hidden_upper)

    grad_a_out = Delivery(0, 4 + 3, s.grad_a, o.right.at[3, mine])
    grad_a_out.start()
    grad_out = attention_backward(s, vec_a, s.hidden, s.vecs_a)
    grad_a_out.wait()

    @pl.when(upper)
    def _():
        for owner in range(4):
            here, there = output_copy(owner)
            pl.when(p == owner)(here.wait)
            pl.when(p != owner)(there.wait_send)

    s.hop_out[:M] = grad_out.astype(BF16)
    table_out = local(s.rel, o.table, s.out_sem.at[3])
    right_a_out = [deliver_rows(0, 2, s.hop_out.at[:M])] + deliver_right(0, s.hidden, range(3))
    vecs_a_out = deliver_vecs(0, s.vecs_a)

    def merged_copy(owner):
        return local(s.slope.at[owner, :, : D // 2], o.merged.at[owner], s.piece_sem.at[owner])

    @pl.when(upper)
    def _():
        hop(s.grad_m)
        start_all(right_a_out)
        table_out.start()
        vecs_a_out.start()
        hop_copy(s.grad_m).wait_send()

    @pl.when(lower)
    def _():
        saved = [
            local(o.tokens.at[k], s.qkv.at[k], s.out_sem.at[1 + k]) for k in range(2)
        ]
        start_all(saved)
        start_all(right_a_out)
        table_out.start()
        wait_all(right_m_out)
        halves = [s.acc, s.inverse]
        for k in range(4):
            rows = slice(k * CHUNK, (k + 1) * CHUNK)
            here = slice(k % 2 * CHUNK, (k % 2 + 1) * CHUNK)
            halves[k // 2][:, here] = dot_nt(s.hop_out[:M], s.w_merge[rows])
        wait_all(saved)
        gain = jnp.concatenate([vec_a[1:2], vec_a[2:3]], 1)
        values = jnp.concatenate([s.qkv[0], s.qkv[1]], 1).astype(F32)
        grad_in, gain_grad, shift_grad = norm_backward(
            jnp.concatenate([s.acc[...], s.inverse[...]], 1), values, gain
        )
        wide = D // 8
        for owner in range(4):
            for part in range(4):
                start = part * (D // 2) + owner * wide
                s.slope[owner, :, part * wide : (part + 1) * wide] = grad_in[
                    :, start : start + wide
                ].astype(BF16)
            merged_copy(owner).start()
        s.vecs_a[1:2] = gain_grad[:, :D]
        s.vecs_a[2:3] = gain_grad[:, D:]
        s.vecs_a[7:8] = shift_grad[:, :D]
        s.vecs_a[8:9] = shift_grad[:, D:]
        vecs_a_out.start()
        for owner in range(4):
            merged_copy(owner).wait()

    @pl.when(upper)
    def _():
        wait_all(right_m_out)

    wait_all(right_a_out + [table_out, vecs_a_out, vecs_m_out, normed_out, mixed_out, grad_m_out])
    given = [deliver_rows(0, 0, s.normed), mixed_out, vecs_a_out, grad_a_out] + right_a_out
    given += [normed_out, grad_m_out, vecs_m_out] + right_m_out
    for copy in given:
        copy.wait_recv()

    @pl.when(lower)
    def _():
        for copy in deliver_hidden(0, s.hidden, range(2)) + hidden_lower:
            copy.wait_recv()

    @pl.when(upper)
    def _():
        for copy in hidden_upper:
            copy.wait_recv()

    @pl.when(p == 2)
    def _():
        for k in over:
            for core in range(2):
                hidden_over(k, core).wait_recv()

    for source in (2, 3):

        @pl.when(p != source)
        def _(source=source):
            wide = D // 4
            remote(
                s.hop_out.at[:M, :wide], o.outs.at[source % 2], s.piece_sem.at[0], s.outs_in.at[source % 2], (source, w_at)
            ).wait_recv()

    vec_copy.wait_send()

    @pl.when(c == 0)
    def _():
        for copy in gifts(attention_parts, s.attention_sem):
            copy.wait_send()

        @pl.when(lower)
        def _():
            for copy in merge_gifts():
                copy.wait_send()

    @pl.when(c == 1)
    def _():
        for copy in gifts(mlp_parts, s.mlp_sem):
            copy.wait_send()


def forward_backward(page_tokens, blank, cotangent, first, second, gains, biases, tables):
    channels = page_tokens.shape[-1]
    crops = blank.shape[0]
    rolls = np.stack([hop_matrix(False), hop_matrix(True)])
    operands = {
        "tokens": jnp.transpose(page_tokens, (0, 2, 1, 3)).reshape(crops, 4 * TOK, channels),
        "cotangent": cotangent,
        "first": first,
        "second": second,
        "pack": jnp.asarray(offset_pack(), BF16),
        "roll": jnp.asarray(rolls, BF16),
        "pick": jnp.asarray(np.pad(merge_matrix(), ((0, 0), (0, 0), (0, D - 4 * TOK))), BF16),
        "cot": jnp.asarray(cotangent_matrix(), BF16),
        "gains": jnp.transpose(gains, (1, 0, 2)),
        "biases": jnp.transpose(biases, (1, 0, 2)),
        "blank": blank,
        "tables": tables,
        "keys": jnp.asarray(key_matrix(), BF16),
        "regions": jnp.asarray(region_masks(), F32),
    }
    in_vmem = ("gains", "biases", "blank", "tables", "keys", "regions")
    four = (4, M, D)
    outs = {
        "left": ((2 * M, D), BF16),
        "left_b": ((2 * M, D), BF16),
        "right_b": ((2 * M, D), BF16),
        "right": ((4, 2 * M, D), BF16),
        "hidden": ((4, 2 * M, D), BF16),
        "vecs": ((2, 16, D), F32),
        "table": ((HEADS * ROWS, 128), F32),
        "outs": ((2, M, D // 4), BF16),
        "merged": ((4, M, D // 2), BF16),
        "tokens": ((2, M, D), BF16),
    }
    scratch = {
        "w_qkv": pltpu.VMEM((STEPS, D, 3 * GROUP), BF16),
        "w_out": pltpu.VMEM((STEPS, GROUP, D), BF16),
        "w1": pltpu.VMEM((CHUNKS, D, CHUNK), BF16),
        "w2": pltpu.VMEM((CHUNKS, CHUNK, D), BF16),
        "w_merge": pltpu.VMEM((2 * D, D), BF16),
        "x": pltpu.VMEM((M, D), F32),
        "normed": pltpu.VMEM((M, D), BF16),
        "mixed": pltpu.VMEM((M, D), BF16),
        "qkv": pltpu.VMEM((3, M, D), BF16),
        "exps": pltpu.VMEM((WINS, HEADS, ROWS, 128), BF16),
        "inverse": pltpu.VMEM((M, D), F32),
        "mid": pltpu.VMEM((M, D), BF16),
        "hidden": pltpu.VMEM(four, BF16),
        "slope": pltpu.VMEM(four, BF16),
        "pre": pltpu.VMEM((2, M, CHUNK), F32),
        "acc": pltpu.VMEM((M, D), F32),
        "hop_out": pltpu.VMEM((M + ROWS, D), BF16),
        "grad_m": pltpu.VMEM((M, D), BF16),
        "grad_a": pltpu.VMEM((M, D), BF16),
        "rel": pltpu.VMEM((HEADS * ROWS, 128), F32),
        "mask": pltpu.VMEM((WINS, ROWS, 128), F32),
        "vec": pltpu.VMEM((2, 16, D), F32),
        "vecs_a": pltpu.VMEM((16, D), F32),
        "vecs_m": pltpu.VMEM((16, D), F32),
        "tokens": pltpu.VMEM((2, 4 * TOK, channels), BF16),
        "table": pltpu.VMEM((HEADS, OFFSETS), F32),
        "cotangent": pltpu.VMEM((TOK, D), BF16),
        "roll": pltpu.VMEM((M, M + ROWS), BF16),
        "const_sem": DMA((7,)),
        "pick_sem": DMA((4,)),
        "token_sem": DMA((2,)),
        "vec_sem": DMA((2,)),
        "attention_sem": DMA((4 * STEPS,)),
        "mlp_sem": DMA((2 * CHUNKS,)),
        "merge_sem": DMA((2, STEPS)),
        "give_sem": DMA((16,)),
        "out_sem": DMA((4,)),
        "give_out": DMA((2, 12)),
        "give_in": DMA((2, 12)),
        "over_sem": DMA((4,)),
        "over_in": DMA((2, 4)),
        "outs_in": DMA((2,)),
        "piece_sem": DMA((4,)),
        "hop_sem": DMA((6,)),
    }
    found = pl.pallas_call(
        functools.partial(main_kernel, tuple(operands), tuple(outs), tuple(scratch)),
        in_specs=[IN_VMEM if k in in_vmem else ANYWHERE for k in operands],
        out_specs=[ANYWHERE] * len(outs),
        out_shape=[shape_of(*value) for value in outs.values()],
        scratch_shapes=list(scratch.values()),
        compiler_params=pltpu.CompilerParams(
            collective_id=1, has_side_effects=True, vmem_limit_bytes=61 * 1024 * 1024
        ),
        name="forward_backward",
    )(*operands.values())
    return dict(zip(outs, found))


PIECES = 2 * HALF
AHEAD = 4
RING = AHEAD + 2
LAG = 2
LEFT = PIECES
SLOTS = PIECES + 4
OWN_PIECES = (HALF + HALF // 2, 2 * HALF - RELAY, HALF + RELAY, 2 * HALF)
EARLY = AHEAD + 1


def bit_reversed(index, bits):
    return sum(((index >> b) & 1) << (bits - 1 - b) for b in range(bits))


def by_device(p, values):
    found = values[-1]
    for index in range(len(values) - 2, -1, -1):
        found = jnp.where(p == index, values[index], found)
    return found


def reduce_kernel(bits, names, *refs):
    refs = list(refs)
    count = 1 << bits
    share = D // count
    quarter = count // 4
    i = Refs(names, refs[: len(names)])
    refs = refs[len(names) :]
    first_ref, second_ref, vecs_ref, tokens_ref, tables_ref = refs[:5]
    refs = refs[5:]
    lhs_in, lhs, rhs, vec_in, vec_own, relay, score, unroll, inner, outer, table, table_recv, send, keep, whole, merged = refs[:16]
    refs = refs[16:]
    recv = refs[:bits]
    vec_recv = refs[bits : 2 * bits]
    (
        row_sem,
        stage_send,
        stage_recv,
        vec_send_sem,
        vec_recv_sem,
        table_send_sem,
        table_recv_sem,
        const_sem,
        cross_local,
        cross_send,
        cross_recv,
        relay_send,
        relay_recv,
        ready,
    ) = refs[2 * bits :]

    p = lax.axis_index("pipe")
    w = lax.axis_index("wide")
    c = lax.rem(p, 2)
    upper = p >= 2
    pair = p + 1 - 2 * c
    across = lax.rem(p + 2, 4)
    partner = []
    mine = []
    for s in range(bits):
        bit = lax.rem(w // (1 << s), 2)
        mine.append(bit)
        partner.append(w + (1 << s) * (1 - 2 * bit))

    barrier = pltpu.get_barrier_semaphore()
    pl.semaphore_signal(barrier, inc=1, device_id=(pair, w), device_id_type=MESH)
    for s in range(bits):
        pl.semaphore_signal(barrier, inc=1, device_id=(p, partner[s]), device_id_type=MESH)

    @pl.when(upper)
    def _():
        for other in (0, 1):
            pl.semaphore_signal(barrier, inc=1, device_id=(other, w), device_id_type=MESH)
        pl.semaphore_wait(barrier, 1 + bits)

    @pl.when(jnp.logical_not(upper))
    def _():
        pl.semaphore_wait(barrier, 3 + bits)
        for other in (2, 3):
            pl.semaphore_signal(ready, inc=1, device_id=(other, w), device_id_type=MESH)

    pieces = by_device(p, OWN_PIECES)

    def columns(ref, j):
        return ref.at[j // PER, :, j % PER * PIECE : (j % PER + 1) * PIECE]

    def sources(index):
        found = [(LEFT, i.left, lhs_in.at[0])]
        found += [(j, columns(i.right, j), rhs.at[j]) for j in range(HALF)]
        if index % 2 == 0:
            found.insert(AHEAD + 1, (LEFT + 1, i.left_b, lhs_in.at[1]))
        where = ((0, HALF // 2), (RELAY, HALF), (0, RELAY), (0, HALF))[index]
        more = [(LEFT + 2, i.right_b, lhs_in.at[2])]
        more += [(HALF + j, columns(i.hidden, j), rhs.at[HALF + j]) for j in range(*where)]
        return more + found if index == 2 else found + more

    def issue(early):
        part = slice(0, EARLY) if early else slice(EARLY, None)
        for index in range(4):

            @pl.when(p == index)
            def _(index=index):
                for slot, source, target in sources(index)[part]:
                    pltpu.make_async_copy(source, target, row_sem.at[slot]).start()

    issue(True)
    pltpu.make_async_copy(i.vecs, vec_in, row_sem.at[LEFT + 3]).start()
    pltpu.make_async_copy(i.table, score, const_sem.at[0]).start()
    pltpu.make_async_copy(i.inner, inner, const_sem.at[1]).start()
    pltpu.make_async_copy(i.outer, outer, const_sem.at[2]).start()

    @pl.when(p == 2)
    def _():
        pltpu.make_async_copy(i.unroll, unroll, const_sem.at[3]).start()

    def token_copy(source, target, to):
        return pltpu.make_async_remote_copy(
            merged.at[target],
            tokens_ref.at[source],
            cross_send.at[target],
            cross_recv.at[source],
            device_id=(to, w),
            device_id_type=MESH,
        )

    def token_own(index):
        return pltpu.make_async_copy(merged.at[index], tokens_ref.at[index], cross_local)

    merged_in = pltpu.make_async_copy(i.merged, merged, const_sem.at[4])

    @pl.when(jnp.logical_not(upper))
    def _():
        merged_in.start()

    def rows_wait(slot, target):
        pltpu.make_async_copy(target, target, row_sem.at[slot]).wait()

    def turn(k, unrolled):
        rows_wait(LEFT + k, lhs_in.at[k])
        if unrolled:
            pltpu.make_async_copy(i.unroll, unroll, const_sem.at[3]).wait()
        per = max(1, 128 // share)
        at_row = lax.broadcasted_iota(jnp.int32, (128, 128), 0)
        at_lane = lax.broadcasted_iota(jnp.int32, (128, 128), 1)
        unit = jnp.where(at_row == at_lane, 1.0, 0.0).astype(BF16)
        for block in range(D // 128):
            flipped = dot_nt(unit, lhs_in[k, :, block * 128 : (block + 1) * 128]).astype(BF16)
            if unrolled:
                flipped = dot(flipped, unroll[...]).astype(BF16)
            if share >= 128:
                at = bit_reversed(block * 128 // share, bits)
                start = block * 128 % share
                lhs[k, at // quarter, at % quarter, start : start + 128] = flipped
            else:
                for q in range(per):
                    at = bit_reversed(block * per + q, bits)
                    lhs[k, at // quarter, at % quarter] = flipped[q * share : (q + 1) * share]

    def swapped(t):
        return (4 - lax.rem(t, 4)) // 4

    def stage_of(s, t):
        if s >= 2:
            return mine[s], partner[s]
        odd = swapped(t)
        return (
            mine[s] + odd * (mine[1 - s] - mine[s]),
            partner[s] + odd * (partner[1 - s] - partner[s]),
        )

    def stage_copy(s, t):
        j = piece(t)
        half, to = stage_of(s, t)
        if s == 0:
            source = send.at[lax.rem(t, RING)]
        elif s == 1:
            source = recv[0].at[j, 1 - half]
        else:
            width = count >> (s + 1)
            source = recv[s - 1].at[j, pl.ds((1 - half) * width, width)]
        return pltpu.make_async_remote_copy(
            source,
            recv[s].at[j],
            stage_send.at[s, j],
            stage_recv.at[s, j],
            device_id=(p, to),
            device_id_type=MESH,
        )

    def send_first(t):
        j = piece(t)
        slot = lax.rem(t, RING)

        @pl.when((j == 0) & (p == 2))
        def _():
            turn(0, False)

        @pl.when((j == HALF - PER) & (c == 0))
        def _():
            turn(1, False)

        @pl.when(j == by_device(p, (HALF, HALF + RELAY, PIECES, HALF)))
        def _():
            turn(2, False)

        @pl.when(t >= RING)
        def _():
            stage_copy(0, t - RING).wait_send()

        rows_wait(j, rhs.at[j])
        odd = swapped(t)
        sel = jnp.where(j < HALF - PER, 0, jnp.where(j < HALF, 1 - c, 2))
        product = dot(lhs[sel].reshape(D, 2 * M), rhs[j])
        for high in range(2):
            for low in range(2):
                bit = (1 - odd) * high + odd * low
                part = (1 - odd) * low + odd * high
                keeps = 1 - (bit - mine_first(odd)) * (bit - mine_first(odd))
                rows = (2 * high + low) * (D // 4)
                whole[2 * keeps + part] = product[rows : rows + D // 4].reshape(quarter, share, PIECE)
        send[slot] = whole[:2].astype(BF16)
        keep[slot] = whole[2:]
        stage_copy(0, t).start()

    def mine_first(odd):
        return mine[0] + odd * (mine[1] - mine[0])

    def store_out(j, values):
        @pl.when(j < HALF)
        def _():
            first_ref[:, pl.ds(pl.multiple_of(j * PIECE, PIECE), PIECE)] = values

        @pl.when(j >= HALF)
        def _():
            turned = jnp.transpose(values)

            @pl.when(p == 2)
            def _():
                relay[j - HALF] = turned

            @pl.when(p != 2)
            def _():
                second_ref[pl.ds(pl.multiple_of((j - HALF) * PIECE, PIECE), PIECE)] = turned

    def take(s, t):
        j = piece(t)
        stage_copy(s, t).wait_recv()
        half, _ = stage_of(s, t)
        if s == 0:
            kept = keep[lax.rem(t, RING)]
        elif s == 1:
            kept = recv[0][j, half].astype(F32)
        else:
            width = count >> (s + 1)
            kept = recv[s - 1][j, pl.ds(half * width, width)].astype(F32)
        total = kept + recv[s][j].astype(F32)
        if s == bits - 1:
            store_out(j, total[0])
        else:
            recv[s][j] = total.astype(BF16)
            stage_copy(s + 1, t).start()

    def piece(t):
        return by_device(
            p,
            (
                t,
                jnp.where(t < HALF, t, t + RELAY),
                jnp.where(t < RELAY, t + HALF, t - RELAY),
                t,
            ),
        )

    @pl.when(p == 2)
    def _():
        turn(2, True)

    @pl.when(p != 2)
    def _():
        turn(0, False)

    issue(False)

    for index in range(2):

        @pl.when(p == index)
        def _(index=index):
            merged_in.wait()
            token_own(index).start()
            for target in range(4):
                if target != index:
                    token_copy(index, target, target).start()

    lax.fori_loop(0, AHEAD, lambda t, _: (send_first(t), 0)[1], 0)

    def vec_copy(s):
        width = count >> (s + 1)
        held = vec_own if s == 0 else vec_recv[s - 1]
        return pltpu.make_async_remote_copy(
            held.at[pl.ds((1 - mine[s]) * width, width)],
            vec_recv[s],
            vec_send_sem.at[s],
            vec_recv_sem.at[s],
            device_id=(p, partner[s]),
            device_id_type=MESH,
        )

    def vec_start():
        rows_wait(LEFT + 3, vec_in)
        both = jnp.concatenate([vec_in[0] + vec_in[1], jnp.zeros((112, D), F32)], 0)
        per = max(1, 128 // share)
        for block in range(D // 128):
            flipped = jnp.transpose(both[:, block * 128 : (block + 1) * 128])
            if share >= 128:
                at = bit_reversed(block * 128 // share, bits)
                inside = block * 128 % share
                vec_own[at, inside : inside + 128] = flipped
            else:
                for q in range(per):
                    at = bit_reversed(block * per + q, bits)
                    vec_own[at] = flipped[q * share : (q + 1) * share]
        vec_copy(0).start()

    def vec_step(s):
        width = count >> (s + 1)
        vec_copy(s).wait_recv()
        held = vec_own if s == 0 else vec_recv[s - 1]
        total = held[pl.ds(mine[s] * width, width)] + vec_recv[s][...]
        if s == bits - 1:
            vecs_ref[...] = total[0]
        else:
            vec_recv[s][...] = total
            vec_copy(s + 1).start()

    def table_copy(s):
        to = (pair, w) if s == 0 else (p, partner[s - 1])
        return pltpu.make_async_remote_copy(
            table.at[s],
            table_recv.at[s],
            table_send_sem.at[s],
            table_recv_sem.at[s],
            device_id=to,
            device_id_type=MESH,
        )

    def table_start():
        pltpu.make_async_copy(i.table, score, const_sem.at[0]).wait()
        pltpu.make_async_copy(i.inner, inner, const_sem.at[1]).wait()
        pltpu.make_async_copy(i.outer, outer, const_sem.at[2]).wait()
        by_row = None
        for ci in range(WIN):
            rows = jnp.concatenate(
                [score[pl.ds(ri * WIN + ci, HEADS, stride=ROWS), :] for ri in range(WIN)], 0
            )
            term = split_dot(rows, inner[ci])
            by_row = term if by_row is None else by_row + term
        total = None
        for ri in range(WIN):
            term = split_dot(by_row[ri * HEADS : (ri + 1) * HEADS], outer[ri])
            total = term if total is None else total + term
        table[0] = total
        table_copy(0).start()

    def table_cross():
        x = p // 2
        return pltpu.make_async_remote_copy(
            table.at[bits + 1],
            tables_ref.at[x],
            table_send_sem.at[bits + 1],
            table_recv_sem.at[bits + 1],
            device_id=(across, w),
            device_id_type=MESH,
        )

    def table_step(s):
        table_copy(s).wait_recv()
        table[s + 1] = table[s] + table_recv[s]
        if s < bits:
            table_copy(s + 1).start()
        else:
            tables_ref[p // 2] = table[s + 1]

            @pl.when(jnp.logical_not(upper))
            def _():
                table_cross().start()

    def relay_copy(k):
        return pltpu.make_async_remote_copy(
            relay.at[k],
            second_ref.at[k * PIECE : (k + 1) * PIECE],
            relay_send.at[k],
            relay_recv.at[k],
            device_id=(1, w),
            device_id_type=MESH,
        )

    vec_start()
    table_start()

    def body(t, carry):
        for s in range(bits):
            at = t - LAG * s

            @pl.when((at >= 0) & (at < pieces))
            def _(s=s, at=at):
                take(s, at)
                if s == 0:

                    @pl.when(t + AHEAD < pieces)
                    def _():
                        send_first(t + AHEAD)

        for s in range(bits):

            @pl.when(t == 2 * s + 2)
            def _(s=s):
                vec_step(s)

        for s in range(bits + 1):

            @pl.when(t == 2 * s + 2)
            def _(s=s):
                table_step(s)

        @pl.when(upper & (t == RELAY + LAG * (bits - 1)))
        def _():
            pl.semaphore_wait(ready, 2)
            table_cross().start()

            @pl.when(p == 2)
            def _():
                for k in range(RELAY):
                    relay_copy(k).start()

        return carry

    lax.fori_loop(0, pieces + LAG * (bits - 1), body, 0)

    def clear(j, carry):
        second_ref[pl.ds(pl.multiple_of(j * PIECE, PIECE), PIECE)] = jnp.zeros((PIECE, share), F32)
        return carry

    lax.fori_loop(by_device(p, (HALF // 2, HALF, 0, HALF)), HALF, clear, 0)

    def drain(t, carry):
        @pl.when(t >= pieces - RING)
        def _():
            stage_copy(0, t).wait_send()

        for s in range(1, bits):
            stage_copy(s, t).wait_send()
        return carry

    lax.fori_loop(0, pieces, drain, 0)
    for s in range(bits):
        vec_copy(s).wait_send()
    for s in range(bits + 1):
        table_copy(s).wait_send()
    table_cross().wait()

    for index in range(4):

        @pl.when(p == index)
        def _(index=index):
            if index < 2:
                token_own(index).wait()
                for target in range(4):
                    if target != index:
                        token_copy(index, target, target).wait_send()
            for source in range(2):
                if source != index:
                    token_copy(source, index, source).wait_recv()
            if index == 2:
                for k in range(RELAY):
                    relay_copy(k).wait_send()
            if index == 1:
                for k in range(RELAY):
                    relay_copy(k).wait_recv()


def reduce_gradients(made, count):
    bits = count.bit_length() - 1
    share = D // count
    anywhere = pl.BlockSpec(memory_space=pl.ANY)
    in_vmem = pl.BlockSpec(memory_space=pltpu.VMEM)
    inner, outer = offset_blocks()
    flat = (HEADS * ROWS, 128)
    operands = {name: made[name] for name in made if name not in ("tokens", "outs")}
    operands["unroll"] = jnp.asarray(unroll_matrix(), BF16)
    operands["inner"] = jnp.asarray(inner, BF16)
    operands["outer"] = jnp.asarray(outer, BF16)
    merged = made["merged"]
    dma = pltpu.SemaphoreType.DMA
    halves = [(2, count // 4)] + [(count >> (s + 1),) for s in range(1, bits)]
    return pl.pallas_call(
        functools.partial(reduce_kernel, bits, tuple(operands)),
        in_specs=[anywhere] * len(operands),
        out_specs=[in_vmem] * 3 + [anywhere] + [in_vmem],
        out_shape=[
            shape_of((share, FF), F32),
            shape_of((FF, share), F32),
            shape_of((share, 128), F32),
            shape_of((2,) + merged.shape[1:], BF16),
            shape_of((2, HEADS, OFFSETS), F32),
        ],
        scratch_shapes=[
            pltpu.VMEM((3, 2 * M, D), BF16),
            pltpu.VMEM((3, 4, count // 4, share, 2 * M), BF16),
            pltpu.VMEM((PIECES, 2 * M, PIECE), BF16),
            pltpu.VMEM((2, 16, D), F32),
            pltpu.VMEM((count, share, 128), F32),
            pltpu.VMEM((RELAY, PIECE, share), F32),
            pltpu.VMEM(flat, F32),
            pltpu.VMEM((2 * M, 2 * M), BF16),
            pltpu.VMEM(inner.shape, BF16),
            pltpu.VMEM(outer.shape, BF16),
            pltpu.VMEM((bits + 2, HEADS, OFFSETS), F32),
            pltpu.VMEM((bits + 1, HEADS, OFFSETS), F32),
            pltpu.VMEM((RING, 2, count // 4, share, PIECE), BF16),
            pltpu.VMEM((RING, 2, count // 4, share, PIECE), F32),
            pltpu.VMEM((4, count // 4, share, PIECE), F32),
            pltpu.VMEM(merged.shape, BF16),
            *[pltpu.VMEM((PIECES,) + half + (share, PIECE), BF16) for half in halves],
            *[pltpu.VMEM((count >> (s + 1), share, 128), F32) for s in range(bits)],
            dma((SLOTS,)),
            dma((bits, PIECES)),
            dma((bits, PIECES)),
            dma((bits,)),
            dma((bits,)),
            dma((bits + 2,)),
            dma((bits + 2,)),
            dma((5,)),
            dma,
            dma((4,)),
            dma((2,)),
            dma((RELAY,)),
            dma((RELAY,)),
            pltpu.SemaphoreType.REGULAR,
        ],
        compiler_params=pltpu.CompilerParams(
            collective_id=0, has_side_effects=True, vmem_limit_bytes=60 * 1024 * 1024
        ),
        name="reduce_gradients",
    )(*operands.values())


def finish_kernel(
    first_in, second_in, vecs_in, outs_in, parts_in, tables_in, order_in, split_in,
    output_ref, tokens_ref, first_out, second_out, gains_ref, biases_ref, tables_out,
    vecs_ref, outs_ref, parts_ref, tables_ref, order_ref, split_ref, first_ref, second_ref, sems,
):
    copies = [
        pltpu.make_async_copy(source, target, sems.at[k])
        for k, (source, target) in enumerate(
            (
                (parts_in, parts_ref),
                (split_in, split_ref),
                (outs_in, outs_ref),
                (order_in, order_ref),
                (tables_in, tables_ref),
                (vecs_in, vecs_ref),
                (first_in, first_ref),
                (second_in, second_ref),
            )
        )
    ]
    for copy in copies:
        copy.start()
    for copy in copies[:6]:
        copy.wait()
    on = []
    for copy, source, target in ((copies[6], first_ref, first_out), (copies[7], second_ref, second_out)):
        copy.wait()
        on.append(pltpu.make_async_copy(source, target, sems.at[8 + len(on)]))
        on[-1].start()
    tables_out[...] = tables_ref[:, :, : SPAN * SPAN]
    vecs = jnp.transpose(vecs_ref[...])
    for row in range(3):
        gains_ref[row] = vecs[row : row + 1]
    for row in range(6):
        biases_ref[row] = vecs[3 + row : 4 + row]
    channels = tokens_ref.shape[-1]
    for crop in range(WINS):
        windows = []
        for half in range(2):
            window = 2 * crop + half
            core, k = window // WINS, window % WINS
            windows.append((core, slice(k * ROWS, (k + 1) * ROWS)))
        rolled = jnp.concatenate([outs_ref[core, rows] for core, rows in windows], 0)
        output_ref[crop] = dot(order_ref[...], rolled).astype(BF16)
        total = None
        for half, (core, rows) in enumerate(windows):
            cells = jnp.concatenate(
                [parts_ref[core, rows, t * channels : (t + 1) * channels] for t in range(4)], 0
            )
            term = dot(split_ref[half], cells)
            total = term if total is None else total + term
        tokens_ref[crop] = total
    for copy in on:
        copy.wait()


def finish(out_parts, first_part, second_part, vec_part, token_parts, table_parts):
    share = first_part.shape[0]
    split = np.transpose(merge_matrix(), (0, 2, 1))
    channels = token_parts.shape[-1] // 4
    return pl.pallas_call(
        finish_kernel,
        in_specs=[ANYWHERE] * 8,
        out_specs=[IN_VMEM] * 2 + [ANYWHERE] * 2 + [IN_VMEM] * 3,
        out_shape=[
            shape_of((WINS, TOK, out_parts.shape[-1]), BF16),
            shape_of((WINS, 4 * TOK, channels), F32),
            shape_of(first_part.shape, F32),
            shape_of(second_part.shape, F32),
            shape_of((3, 1, share), F32),
            shape_of((6, 1, share), F32),
            shape_of((2, HEADS, SPAN * SPAN), F32),
        ],
        scratch_shapes=[
            pltpu.VMEM(vec_part.shape, F32),
            pltpu.VMEM(out_parts.shape, BF16),
            pltpu.VMEM(token_parts.shape, BF16),
            pltpu.VMEM(table_parts.shape, F32),
            pltpu.VMEM((TOK, 2 * ROWS), BF16),
            pltpu.VMEM(split.shape, BF16),
            pltpu.VMEM(first_part.shape, F32),
            pltpu.VMEM(second_part.shape, F32),
            DMA((10,)),
        ],
        compiler_params=pltpu.CompilerParams(vmem_limit_bytes=61 * 1024 * 1024),
        name="finish",
    )(
        first_part,
        second_part,
        vec_part,
        out_parts,
        token_parts,
        table_parts,
        jnp.asarray(output_matrix(), BF16),
        jnp.asarray(split, BF16),
    )


def padded_row(token):
    return (token // AREA) * ROWS + token % AREA


def rolled_source():
    cells = np.arange(TOK)
    rows, columns = cells // GRID_W, cells % GRID_W
    return ((rows + WIN // 2) % GRID_H) * GRID_W + (columns + WIN // 2) % GRID_W


def hop_matrix(inverse):
    source = rolled_source()
    if inverse:
        source = np.argsort(source)
    result = np.zeros((2, M, (WINS + 1) * ROWS), np.float32)
    for core in range(2):
        for k in range(WINS):
            window = WINS * core + k
            crop, part = window // 2, window % 2
            for t in range(AREA):
                token = source[part * AREA + t]
                taken = crop * 2 + token // AREA
                slot = taken - WINS * core
                if not 0 <= slot < WINS:
                    slot = WINS
                result[core, k * ROWS + t, slot * ROWS + token % AREA] = 1.0
    return result


def cotangent_matrix():
    source = rolled_source()
    result = np.zeros((2, M, 4 * 256), np.float32)
    for core in range(2):
        for k in range(WINS):
            window = WINS * core + k
            crop, part = window // 2, window % 2
            for t in range(AREA):
                result[core, k * ROWS + t, crop * 256 + source[part * AREA + t]] = 1.0
    return result


def output_matrix():
    source = rolled_source()
    result = np.zeros((TOK, 2 * ROWS), np.float32)
    for t in range(TOK):
        result[source[t], padded_row(t)] = 1.0
    return result


def offset_matrices():
    span = 2 * WIN - 1
    inner = np.zeros((WIN, 128, WIN, span), np.float32)
    outer = np.zeros((WIN, WIN, span, span, span), np.float32)
    for ci in range(WIN):
        for j in range(AREA):
            inner[ci, j, j // WIN, ci - j % WIN + WIN - 1] = 1.0
    for ri in range(WIN):
        for rj in range(WIN):
            for dc in range(span):
                outer[ri, rj, dc, ri - rj + WIN - 1, dc] = 1.0
    return (
        inner.reshape(WIN * 128, WIN * span),
        outer.reshape(WIN * WIN * span, span * span),
    )


def offset_blocks():
    inner, outer = offset_matrices()
    inner = np.pad(inner.reshape(WIN, 128, WIN * SPAN), ((0, 0), (0, 0), (0, INNER - WIN * SPAN)))
    outer = np.pad(
        outer.reshape(WIN, WIN * SPAN, SPAN * SPAN),
        ((0, 0), (0, INNER - WIN * SPAN), (0, OFFSETS - SPAN * SPAN)),
    )
    return inner, outer


def offset_pack():
    inner, outer = offset_blocks()
    result = np.zeros((WIN // 2, INNER, D), np.float32)
    for k in range(WIN):
        half = k % 2
        result[k // 2, :, half * OFFSETS : (half + 1) * OFFSETS] = outer[k]
        result[k // 2, half * 128 : (half + 1) * 128, 2 * OFFSETS :] = inner[k]
    return result


def unroll_matrix():
    source = rolled_source()
    result = np.zeros((2 * M, 2 * M), np.float32)
    for crop in range(WINS):
        for t in range(TOK):
            start = crop * 2 * ROWS
            result[start + padded_row(t), start + padded_row(source[t])] = 1.0
    return result


def merge_matrix():
    result = np.zeros((2, 4, ROWS, 2 * GRID_W, 2 * GRID_H), np.float32)
    for half in range(2):
        for part in range(4):
            right, down = part // 2, part % 2
            for t in range(AREA):
                result[half, part, t, 2 * (t % WIN) + right, 2 * (half * WIN + t // WIN) + down] = 1.0
    return result.reshape(2, 4 * ROWS, 4 * TOK)


def region_masks():
    cells = np.arange(TOK)
    rows_at, cols_at = cells // GRID_W, cells % GRID_W
    row_band = (rows_at >= GRID_H - WIN).astype(int) + (rows_at >= GRID_H - WIN // 2)
    col_band = (cols_at >= GRID_W - WIN).astype(int) + (cols_at >= GRID_W - WIN // 2)
    rolled = (row_band * 3 + col_band).reshape(2, AREA)
    result = np.zeros((4, ROWS, 128), np.float32)
    for part in range(2):
        result[part, :AREA, :AREA] = 1.0
        result[2 + part, :AREA, :AREA] = rolled[part][:, None] == rolled[part][None, :]
    return result


def key_matrix():
    source = rolled_source()
    result = np.zeros((TOK, 4, 128), np.float32)
    for part in range(2):
        for t in range(AREA):
            result[part * AREA + t, part, t] = 1.0
            result[source[part * AREA + t], 2 + part, t] = 1.0
    return result.reshape(TOK, 4 * 128)


def local(page_tokens, blank, cotangent, first, second, gains, biases, tables):
    count = lax.axis_size("wide")
    made = forward_backward(
        page_tokens, blank, cotangent, first[0], second[0], gains, biases, tables
    )
    output, token_grad, first_grad, second_grad, gain_grad, bias_grad, table_grad = finish(
        made["outs"], *reduce_gradients(made, count)
    )
    crops, rows, columns, channels = page_tokens.shape
    token_grad = token_grad.reshape(crops, columns, rows, channels // 4)
    return (
        output,
        jnp.transpose(token_grad, (0, 2, 1, 3)),
        first_grad[None],
        second_grad[None],
        jnp.transpose(gain_grad, (1, 0, 2)),
        jnp.transpose(bias_grad, (1, 0, 2)),
        table_grad,
    )


def solution(mesh):
    placed = (
        P("wide", None, None, None),
        P("wide", None),
        P("wide", None, None),
        P("pipe", None, None),
        P("pipe", None, None),
        P("pipe", None, None),
        P("pipe", None, None),
        P(),
    )
    return jax.shard_map(
        local,
        mesh=mesh,
        in_specs=placed,
        out_specs=(
            P("wide", None, "pipe"),
            P("wide", None, None, "pipe"),
            P("pipe", "wide", None),
            P("pipe", None, "wide"),
            P("pipe", None, "wide"),
            P("pipe", None, "wide"),
            P(),
        ),
        check_vma=False,
    )
```

```python
import functools
from itertools import zip_longest

import jax
import jax.numpy as jnp
import numpy as np
from jax import lax
from jax.experimental import pallas as pl
from jax.experimental.pallas import tpu as pltpu
from jax.sharding import PartitionSpec as P

HEADS = 32
WIN = 10
GRID_H = 20
GRID_W = 10
AREA = WIN * WIN
TOK = GRID_H * GRID_W
ROWS = 112
WINS = 3
M = ROWS * WINS
D = 1024
FF = 4096
CHUNK = 512
EPSILON = 1e-05
NEGATIVE = -1000000000.0
SCALE = 32 ** (-0.5)
MESH = pl.DeviceIdType.MESH
F32 = jnp.float32
BF16 = jnp.bfloat16


def shape_of(dims, kind):
    return jax.ShapeDtypeStruct(dims, kind)


def dot(left, right):
    return jnp.dot(left, right, preferred_element_type=F32)


def dot_nt(left, right):
    return lax.dot_general(left, right, (((1,), (1,)), ((), ())), preferred_element_type=F32)


def dot_tn(left, right):
    return lax.dot_general(left, right, (((0,), (0,)), ((), ())), preferred_element_type=F32)


def norm_parts(values):
    average = jnp.mean(values, -1, keepdims=True)
    centered = values - average
    inv_std = lax.rsqrt(jnp.mean(centered * centered, -1, keepdims=True) + EPSILON)
    return centered * inv_std, inv_std


def norm_backward(grad_out, values, gain):
    unit, inv_std = norm_parts(values)
    scaled = grad_out * gain
    grad_in = inv_std * (
        scaled
        - jnp.mean(scaled, -1, keepdims=True)
        - unit * jnp.mean(scaled * unit, -1, keepdims=True)
    )
    return (
        grad_in,
        jnp.sum(grad_out * unit, 0, keepdims=True),
        jnp.sum(grad_out, 0, keepdims=True),
    )


def split_dot(left, right, product=dot):
    high = left.astype(BF16)
    low = (left - high.astype(F32)).astype(BF16)
    return product(high, right) + product(low, right)


ANYWHERE = pl.BlockSpec(memory_space=pl.ANY)
IN_VMEM = pl.BlockSpec(memory_space=pltpu.VMEM)
DMA = pltpu.SemaphoreType.DMA
SPAN = 2 * WIN - 1
INNER = 256
OFFSETS = 384
GROUP = 256
GROUP_HEADS = GROUP // 32
STEPS = D // GROUP
CHUNKS = FF // CHUNK
PIECE = 256
HALF = FF // PIECE
PER = D // PIECE
RELAY = 12


class Refs:
    def __init__(self, names, refs):
        self.__dict__.update(zip(names, refs))


def lanes_at(start, size):
    return pl.ds(pl.multiple_of(start, 128), size)


def lane_masks():
    lanes = lax.broadcasted_iota(jnp.int32, (1, 128), 1)
    return [
        jnp.where((lanes >= 32 * h) & (lanes < 32 * h + 32), 1.0, 0.0).astype(BF16)
        for h in range(4)
    ]


def stacked(values, masks, rows):
    if rows > values.shape[0]:
        values = jnp.concatenate(
            [values, jnp.zeros((rows - values.shape[0], values.shape[1]), values.dtype)], 0
        )
    return jnp.concatenate([values * mask for mask in masks], 0)


def beside_ones(values, masks):
    ones = jnp.concatenate([jnp.broadcast_to(mask, (128, 128)) for mask in masks], 0)
    return jnp.concatenate([stacked(values, masks, 128), ones], 1)


def attention_forward(s, vec, weights):
    unit, _ = norm_parts(s.x[...])
    s.normed[...] = (unit * vec[0:1] + vec[3:4]).astype(BF16)
    s.acc[...] = jnp.zeros_like(s.acc)
    masks = lane_masks()

    def step(g, carry):
        weights(g)
        here = lanes_at(g * GROUP, GROUP)
        projected = dot(s.normed[...], s.w_qkv[g])
        query = (projected[:, :GROUP] + vec[4:5, here]).astype(BF16)
        key = projected[:, GROUP : 2 * GROUP].astype(BF16)
        value = (projected[:, 2 * GROUP :] + vec[5:6, here]).astype(BF16)
        for k, values in enumerate((query, key, value)):
            s.qkv[k, :, here] = values
        mixed = []
        for w in range(WINS):
            rows = slice(w * ROWS, (w + 1) * ROWS)
            allowed = s.mask[w] > 0.5
            parts = []
            for part in range(GROUP // 128):
                inside = slice(part * 128, (part + 1) * 128)
                lanes = lanes_at(g * GROUP + part * 128, 128)
                scores = dot_nt(query[rows, inside], stacked(key[rows, inside], masks, 128))
                found = []
                for h in range(4):
                    head = g * GROUP_HEADS + part * 4 + h
                    bias = s.rel[pl.ds(pl.multiple_of(head * ROWS, 8), ROWS)]
                    one = jnp.where(
                        allowed, scores[:, h * 128 : (h + 1) * 128] * SCALE + bias, NEGATIVE
                    )
                    exponent = jnp.exp(one - jnp.max(one, -1, keepdims=True)).astype(BF16)
                    s.exps[w, head] = exponent
                    found.append(exponent)
                sums = dot(jnp.concatenate(found, 1), beside_ones(value[rows, inside], masks))
                scale = 1.0 / sums[:, 128:]
                s.inverse[rows, lanes] = scale
                parts.append((sums[:, :128] * scale).astype(BF16))
            mixed.append(jnp.concatenate(parts, 1))
        mixed = jnp.concatenate(mixed, 0)
        s.mixed[:, here] = mixed
        s.acc[...] += dot(mixed, s.w_out[g])
        return carry

    lax.fori_loop(0, STEPS, step, 0)
    return s.x[...] + (s.acc[...] + vec[6:7])


def attention_backward(s, vec, right, vecs):
    masks = lane_masks()
    s.acc[...] = jnp.zeros_like(s.acc)

    def step(g, carry):
        here = lanes_at(g * GROUP, GROUP)
        mixed_grad = dot_nt(s.grad_a[...], s.w_out[g])
        scaled_grad = (mixed_grad * s.inverse[:, here]).astype(BF16)
        spread = (scaled_grad.astype(F32) * s.mixed[:, here].astype(F32)).astype(BF16)
        query, key, value = [s.qkv[k, :, here] for k in range(3)]
        made = []
        for w in range(WINS):
            rows = slice(w * ROWS, (w + 1) * ROWS)
            parts = []
            for part in range(GROUP // 128):
                inside = slice(part * 128, (part + 1) * 128)
                grad_here = scaled_grad[rows, inside]
                prob_grad = dot_nt(
                    jnp.concatenate([grad_here, -spread[rows, inside]], 1),
                    beside_ones(value[rows, inside], masks),
                )
                found = []
                draws = []
                for h in range(4):
                    head = g * GROUP_HEADS + part * 4 + h
                    exponent = s.exps[w, head]
                    score_grad = exponent.astype(F32) * prob_grad[:, h * 128 : (h + 1) * 128]
                    at = pl.ds(pl.multiple_of(head * ROWS, 8), ROWS)
                    if w == 0:
                        s.rel[at] = score_grad
                    else:
                        s.rel[at] += score_grad
                    found.append(exponent)
                    draws.append((score_grad * SCALE).astype(BF16))
                query_grad = dot(jnp.concatenate(draws, 1), stacked(key[rows, inside], masks, 128))
                key_grad = dot_tn(jnp.concatenate(draws, 0), stacked(query[rows, inside], masks, ROWS))
                value_grad = dot_tn(jnp.concatenate(found, 0), stacked(grad_here, masks, ROWS))
                parts.append([t[:ROWS].astype(BF16) for t in (query_grad, key_grad, value_grad)])
            made.append([jnp.concatenate([part[k] for part in parts], 1) for k in range(3)])
        made = [jnp.concatenate([window[k] for window in made], 0) for k in range(3)]
        for k in range(3):
            right[k, :, here] = made[k]
        s.acc[...] += dot_nt(jnp.concatenate(made, 1), s.w_qkv[g])
        return carry

    lax.fori_loop(0, STEPS, step, 0)
    grad_in, gain_grad, shift_grad = norm_backward(s.acc[...], s.x[...], vec[0:1])
    wide = s.grad_a[...].astype(F32)
    vecs[0:1] = gain_grad
    vecs[1:3] = jnp.zeros((2, D), F32)
    vecs[3:4] = shift_grad
    vecs[4:5] = jnp.sum(right[0].astype(F32), 0, keepdims=True)
    vecs[5:6] = jnp.sum(right[2].astype(F32), 0, keepdims=True)
    vecs[6:7] = jnp.sum(wide, 0, keepdims=True)
    vecs[7:16] = jnp.zeros((9, D), F32)
    return wide + grad_in


def gelu_parts(pre):
    cumulative = 0.5 * (1.0 + lax.erf(pre * 0.7071067811865476))
    density = jnp.exp(-0.5 * pre * pre) * 0.3989422804014327
    return (pre * cumulative).astype(BF16), (cumulative + pre * density).astype(BF16)


def mlp_forward(s, vec, weights):
    x = s.mid[...].astype(F32)
    unit, _ = norm_parts(x)
    s.normed[...] = (unit * vec[0:1] + vec[3:4]).astype(BF16)

    def product(j):
        weights(j)
        start = j % 2 * CHUNK
        bias = vec[4 + j // 2 : 5 + j // 2, start : start + CHUNK]
        s.pre[j % 2] = dot(s.normed[...], s.w1[j]) + bias

    def take(j):
        start = j % 2 * CHUNK
        term = dot(s.hidden[j // 2, :, start : start + CHUNK], s.w2[j])
        if j == 0:
            s.acc[...] = term
        else:
            s.acc[...] += term

    product(0)
    for j in range(CHUNKS):
        start = j % 2 * CHUNK
        if j + 1 < CHUNKS:
            product(j + 1)
        if j > 0:
            take(j - 1)
        values, slopes = gelu_parts(s.pre[j % 2])
        s.hidden[j // 2, :, start : start + CHUNK] = values
        s.slope[j // 2, :, start : start + CHUNK] = slopes
    take(CHUNKS - 1)
    return s.mid[...].astype(F32) + s.acc[...] + vec[8:9]


def mlp_backward(s, vec, vecs):
    def product(j):
        here = slice(j % 2 * CHUNK, (j % 2 + 1) * CHUNK)
        pre_grad = dot_nt(s.grad_m[...], s.w2[j]) * s.slope[j // 2, :, here].astype(F32)
        vecs[4 + j // 2 : 5 + j // 2, here] = jnp.sum(pre_grad, 0, keepdims=True)
        s.slope[j // 2, :, here] = pre_grad.astype(BF16)

    def take(j):
        here = slice(j % 2 * CHUNK, (j % 2 + 1) * CHUNK)
        term = dot_nt(s.slope[j // 2, :, here], s.w1[j])
        if j == 0:
            s.acc[...] = term
        else:
            s.acc[...] += term

    product(0)
    for j in range(CHUNKS):
        if j + 1 < CHUNKS:
            product(j + 1)
        take(j)
    grad_in, gain_grad, shift_grad = norm_backward(s.acc[...], s.mid[...].astype(F32), vec[0:1])
    wide = s.grad_m[...].astype(F32)
    vecs[0:1] = gain_grad
    vecs[1:3] = jnp.zeros((2, D), F32)
    vecs[3:4] = shift_grad
    vecs[8:9] = jnp.sum(wide, 0, keepdims=True)
    vecs[9:16] = jnp.zeros((7, D), F32)
    return wide + grad_in


def main_kernel(ins, outs, scratch, *refs):
    first = len(ins)
    second = first + len(outs)
    i, o, s = Refs(ins, refs[:first]), Refs(outs, refs[first:second]), Refs(scratch, refs[second:])
    p = lax.axis_index("pipe")
    w_at = lax.axis_index("wide")
    side, c = p // 2, lax.rem(p, 2)
    lower, upper = side == 0, side == 1
    pair = (p + 1 - 2 * c, w_at)
    across = (lax.rem(p + 2, 4), w_at)

    def local(source, target, sem):
        return pltpu.make_async_copy(source, target, sem)

    def remote(source, target, sent, got, to):
        return pltpu.make_async_remote_copy(
            source, target, sent, got, device_id=to, device_id_type=MESH
        )

    consts = [local(i.pack.at[k], s.hidden.at[k, :INNER], s.const_sem.at[k]) for k in range(4)]
    consts.append(local(i.pack.at[4], s.slope.at[0, :INNER], s.const_sem.at[4]))
    consts.append(local(i.roll.at[side, c], s.roll, s.const_sem.at[5]))
    picks = []
    for half in range(2):
        for source, target in (
            (i.pick.at[half, : 3 * ROWS], s.slope.at[1 + half]),
            (i.pick.at[half, 3 * ROWS :], s.slope.at[3, half * ROWS : (half + 1) * ROWS]),
        ):
            picks.append(local(source, target, s.pick_sem.at[len(picks)]))
    cot = local(i.cot.at[c], s.mixed, s.const_sem.at[6])

    def token_copy(k):
        return local(i.tokens.at[(c * WINS + k) // 2], s.tokens.at[k % 2], s.token_sem.at[k % 2])

    def cotangent_copy(k):
        return local(i.cotangent.at[k], s.cotangent, s.token_sem.at[0])

    for copy in consts:
        copy.start()

    @pl.when(lower)
    def _():
        token_copy(0).start()
        token_copy(1).start()
        for copy in picks:
            copy.start()

    @pl.when(upper)
    def _():
        cotangent_copy(0).start()
        cot.start()

    for row in range(3):
        s.vec[c, row : row + 1] = i.gains[row]
    for row in range(6):
        s.vec[c, 3 + row : 4 + row] = i.biases[row]
    s.vec[c, 9:16] = jnp.zeros((7, D), F32)
    barrier = pltpu.get_barrier_semaphore()
    for step in range(1, 4):
        pl.semaphore_signal(
            barrier, inc=1, device_id=(lax.rem(p + step, 4), w_at), device_id_type=MESH
        )
    beside = []
    for b in range(2):
        bit = lax.rem(w_at // (1 << b), 2)
        beside.append((pair[0], w_at + (1 << b) * (1 - 2 * bit)))
        pl.semaphore_signal(barrier, inc=1, device_id=beside[b], device_id_type=MESH)
    pl.semaphore_wait(barrier, 5)
    vec_copy = remote(s.vec.at[c], s.vec.at[c], s.vec_sem.at[0], s.vec_sem.at[1], pair)
    vec_copy.start()

    attention_parts = []
    for g in range(STEPS):
        for k in range(3):
            start = k * D + g * GROUP
            attention_parts.append(
                (i.first.at[:, start : start + GROUP], s.w_qkv.at[g, :, k * GROUP : (k + 1) * GROUP])
            )
        attention_parts.append((i.first.at[g * GROUP : (g + 1) * GROUP, 3 * D :], s.w_out.at[g]))
    mlp_parts = []
    for j in range(CHUNKS):
        here = slice(j * CHUNK, (j + 1) * CHUNK)
        mlp_parts.append((i.first.at[:, here], s.w1.at[j]))
        mlp_parts.append((i.second.at[here], s.w2.at[j]))
    merge_parts = []
    for g in range(STEPS):
        here = slice(g * GROUP, (g + 1) * GROUP)
        merge_parts.append((i.second.at[: 2 * D, here], s.w_merge.at[:, here]))

    def load(parts, got):
        for k, (source, target) in enumerate(parts):
            local(source, target, got.at[k]).start()

    def gifts(parts, got):
        found = []
        for k, (source, target) in enumerate(parts):
            to = beside[k // 8] if parts is attention_parts and k % 4 == 3 else pair
            found.append(remote(source, target, s.give_sem.at[k], got.at[k], to))
        return found

    def give(parts, got):
        for copy in gifts(parts, got):
            copy.start()

    def merge_gifts():
        return [
            remote(source, target, s.merge_sem.at[1, k], s.merge_sem.at[0, k], pair)
            for k, (source, target) in enumerate(merge_parts)
        ]

    mine = pl.ds(pl.multiple_of(c * M, 16), M)

    class Delivery:
        def __init__(self, section, item, source, target):
            self.here = c == section
            self.ends = source, target
            self.sems = s.give_out.at[section, item], s.give_in.at[section, item]

        def local(self):
            return local(*self.ends, self.sems[0])

        def remote(self):
            return remote(*self.ends, *self.sems, pair)

        def start(self):
            pl.when(self.here)(lambda: self.local().start())
            pl.when(jnp.logical_not(self.here))(lambda: self.remote().start())

        def wait(self):
            pl.when(self.here)(lambda: self.local().wait())
            pl.when(jnp.logical_not(self.here))(lambda: self.remote().wait_send())

        def wait_recv(self):
            pl.when(self.here)(lambda: self.remote().wait_recv())

    def deliver_rows(section, item, source):
        target = (o.left, o.left_b, o.right_b)[item]
        return Delivery(section, item, source, target.at[mine])

    def deliver_vecs(section, source):
        return Delivery(section, 3, source, o.vecs.at[c])

    def deliver_right(section, source, where=range(4)):
        return [Delivery(section, 4 + k, source.at[k], o.right.at[k, mine]) for k in where]

    def deliver_hidden(section, source, where):
        return [Delivery(section, 8 + k, source.at[k], o.hidden.at[k, mine]) for k in where]

    def start_all(copies):
        for copy in copies:
            copy.start()

    def wait_all(copies):
        for copy in copies:
            copy.wait()

    @pl.when(c == 0)
    def _():
        @pl.when(lower)
        def _():
            start_all(merge_gifts())
            for k, (source, target) in enumerate(merge_parts):
                local(source, target, s.merge_sem.at[0, k]).start()

        @pl.when(upper)
        def _():
            give(attention_parts, s.attention_sem)

        load(attention_parts, s.attention_sem)

    @pl.when(c == 1)
    def _():
        give(mlp_parts, s.mlp_sem)
        load(mlp_parts, s.mlp_sem)

    def arrived(target, sem):
        local(target, target, sem).wait()

    def attention_weights(g):
        for k in range(3):
            arrived(s.w_qkv.at[g, :, k * GROUP : (k + 1) * GROUP], s.attention_sem.at[4 * g + k])
        arrived(s.w_out.at[g], s.attention_sem.at[4 * g + 3])

    def mlp_weights(j):
        arrived(s.w1.at[j], s.mlp_sem.at[2 * j])
        arrived(s.w2.at[j], s.mlp_sem.at[2 * j + 1])

    for copy in consts:
        copy.wait()

    def outer(ri):
        block = s.hidden.at[ri // 2] if ri < 8 else s.slope.at[0]
        return block[:INNER, ri % 2 * OFFSETS : (ri % 2 + 1) * OFFSETS]

    def inner(ci):
        block = s.hidden.at[ci // 2] if ci < 8 else s.slope.at[0]
        return block[ci % 2 * 128 : (ci % 2 + 1) * 128, 2 * OFFSETS :]

    s.table[...] = jnp.zeros_like(s.table)
    s.table[:, : SPAN * SPAN] = jnp.where(lower, i.tables[0], i.tables[1])
    table = s.table[...]
    wide = jnp.concatenate([split_dot(table, outer(ri), dot_nt) for ri in range(WIN)], 0)
    s.rel[...] = jnp.zeros_like(s.rel)
    for ci in range(WIN):
        rows = split_dot(wide, inner(ci), dot_nt)
        for ri in range(WIN):
            s.rel[pl.ds(ri * WIN + ci, HEADS, stride=ROWS), :] = rows[ri * HEADS : (ri + 1) * HEADS]

    @pl.when(lower & (c == 0))
    def _():
        give(attention_parts, s.attention_sem)

    closed = dot(i.blank[...].astype(F32).astype(BF16), i.keys[...])
    at_row = lax.broadcasted_iota(jnp.int32, (ROWS, 128), 0)
    at_lane = lax.broadcasted_iota(jnp.int32, (ROWS, 128), 1)
    own = jnp.where(at_row == at_lane, 1.0, 0.0)
    for k in range(WINS):
        found = []
        for rolled in range(2):
            for core in range(2):
                crop, part = (WINS * core + k) // 2, (WINS * core + k) % 2
                start = (2 * rolled + part) * 128
                found.append((closed[crop : crop + 1, start : start + 128], i.regions[2 * rolled + part]))
        near = [[jnp.where(c == 0, found[2 * t][u], found[2 * t + 1][u]) for u in range(2)] for t in range(2)]
        row, region = [jnp.where(lower, near[0][u], near[1][u]) for u in range(2)]
        s.mask[k] = region * jnp.maximum(1.0 - row, own)

    @pl.when(upper)
    def _():
        cot.wait()
        for crop in range(WINS):
            cotangent_copy(crop).wait()
            term = dot(s.mixed[:, crop * 256 : crop * 256 + TOK], s.cotangent[...])
            if crop == 0:
                s.acc[...] = term
            else:
                s.acc[...] += term
            if crop + 1 < WINS:
                cotangent_copy(crop + 1).start()
        s.grad_m[...] = s.acc[...].astype(BF16)
        deliver_rows(1, 2, s.grad_m).start()

    arrived(s.vec.at[1 - c], s.vec_sem.at[1])
    vec_a, vec_m = s.vec.at[0], s.vec.at[1]

    def merge_saved():
        return [local(s.hidden.at[k], o.tokens.at[k], s.save_sem.at[k]) for k in range(4)]

    @pl.when(lower)
    def _():
        for copy in picks:
            copy.wait()
        gain = jnp.concatenate([vec_a[1:2], vec_a[2:3]], 1)
        shift = jnp.concatenate([vec_a[7:8], vec_a[8:9]], 1)
        area = 4 * TOK
        for k in range(WINS):
            rows = slice(k * ROWS, (k + 1) * ROWS)
            half = lax.rem(c + k, 2)
            token_copy(k).wait()
            picked = dot(s.slope[1 + half, :, :area], s.tokens[k % 2])
            last = s.slope[3, pl.ds(pl.multiple_of(half * ROWS, 16), ROWS), :area]
            picked = [picked[t * ROWS : (t + 1) * ROWS] for t in range(3)] + [dot(last, s.tokens[k % 2])]
            if k + 2 < WINS:
                token_copy(k + 2).start()
            merged = jnp.concatenate(picked, 1)
            s.hidden[2, rows] = merged[:, :D].astype(BF16)
            s.hidden[3, rows] = merged[:, D:].astype(BF16)
            unit, _ = norm_parts(merged)
            normed = (unit * gain + shift).astype(BF16)
            s.hidden[0, rows] = normed[:, :D]
            s.hidden[1, rows] = normed[:, D:]
        start_all(merge_saved())

        for g in range(STEPS):
            here = slice(g * GROUP, (g + 1) * GROUP)
            arrived(s.w_merge.at[:, here], s.merge_sem.at[0, g])
            s.x[:, here] = dot(s.hidden[0], s.w_merge[:D, here]) + dot(s.hidden[1], s.w_merge[D:, here])

    shared = pl.ds(pl.multiple_of((1 - c) * (WINS - 1) * ROWS, 16), ROWS)
    shared_copy = remote(
        s.hop_out.at[shared], s.hop_out.at[M:], s.hop_sem.at[0], s.hop_sem.at[1], pair
    )

    early = pl.ds(pl.multiple_of(c * ROWS, 16), 2 * ROWS)
    late = pl.ds(pl.multiple_of((1 - c) * 2 * ROWS, 16), ROWS)

    def hop_copies(target):
        return [
            remote(s.grad_a.at[rows], target.at[rows], s.hop_sem.at[2 * k], s.hop_sem.at[2 * k + 1], across)
            for k, rows in ((1, early), (2, late))
        ]

    def hop(target):
        first, last = hop_copies(target)
        shared_copy.start()
        s.grad_a[early] = dot(s.roll[early, :M], s.hop_out[:M]).astype(BF16)
        first.start()
        near = dot(s.roll[late, :M], s.hop_out[:M])
        shared_copy.wait_recv()
        s.grad_a[late] = (near + dot(s.roll[late, M:], s.hop_out[M:])).astype(BF16)
        last.start()
        shared_copy.wait_send()

    @pl.when(upper)
    def _():
        for copy in hop_copies(s.grad_a):
            copy.wait_recv()
        s.x[...] = s.grad_a[...].astype(F32)

    s.mid[...] = attention_forward(s, vec_a, attention_weights).astype(BF16)
    normed_out = deliver_rows(0, 0, s.normed)
    mixed_out = deliver_rows(0, 1, s.mixed)

    @pl.when(lower)
    def _():
        aside = local(s.normed, o.tokens.at[4], s.save_sem.at[4])
        aside.start()
        wait_all(merge_saved())
        aside.wait()

    @pl.when(upper)
    def _():
        normed_out.start()
        normed_out.wait()

    s.hop_out[:M] = mlp_forward(s, vec_m, mlp_weights).astype(BF16)
    mixed_out.start()
    normed_out = deliver_rows(1, 0, s.normed)

    over = range(RELAY // PER)

    def hidden_over(k, core):
        rows = pl.ds(pl.multiple_of(core * M, 16), M)
        return remote(
            s.hidden.at[k], o.hidden.at[k, rows], s.over_sem.at[k], s.over_in.at[core, k], (2, w_at)
        )

    def output_copy(owner):
        wide = D // 4
        source = s.hop_out.at[:M, owner * wide : (owner + 1) * wide]
        return (
            local(source, o.outs.at[c], s.piece_sem.at[owner]),
            remote(source, o.outs.at[c], s.piece_sem.at[owner], s.outs_in.at[c], (owner, w_at)),
        )

    hidden_upper = deliver_hidden(1, s.hidden, range(4))
    hidden_lower = deliver_hidden(1, s.hidden, range(RELAY // PER, 4))
    grad_m_out = deliver_rows(1, 2, s.grad_m)

    @pl.when(lower)
    def _():
        hop(s.grad_a)
        start_all(hidden_lower)
        for copy in hop_copies(s.grad_a):
            copy.wait_send()
        for k in over:
            hidden_over(k, c).start()
        normed_out.start()
        normed_out.wait()

        def bring(at, buffer):
            back = local(o.tokens.at[at], buffer, s.save_sem.at[at])
            back.start()
            back.wait()

        late = [Delivery(0, 8 + k, b, o.hidden.at[k, mine]) for k, b in enumerate((s.normed, s.grad_a))]
        for k, copy in enumerate(late):
            bring(k, (s.normed, s.grad_a)[k])
            copy.start()
        wait_all(late)
        bring(4, s.normed)
        copy = deliver_rows(0, 0, s.normed)
        copy.start()
        copy.wait()
        for copy in hop_copies(s.grad_m):
            copy.wait_recv()
        grad_m_out.start()

    @pl.when(upper)
    def _():
        normed_out.start()
        start_all(hidden_upper)
        for owner in range(4):
            here, there = output_copy(owner)
            pl.when(p == owner)(here.start)
            pl.when(p != owner)(there.start)

    s.grad_a[...] = mlp_backward(s, vec_m, s.vecs_m).astype(BF16)
    right_m_out = deliver_right(1, s.slope)
    vecs_m_out = deliver_vecs(1, s.vecs_m)
    start_all(right_m_out)
    vecs_m_out.start()

    @pl.when(lower)
    def _():
        wait_all(hidden_lower)
        for k in over:
            hidden_over(k, c).wait_send()

    @pl.when(upper)
    def _():
        wait_all(hidden_upper)

    grad_a_out = Delivery(0, 4 + 3, s.grad_a, o.right.at[3, mine])
    grad_a_out.start()
    grad_out = attention_backward(s, vec_a, s.hidden, s.vecs_a)
    grad_a_out.wait()

    @pl.when(upper)
    def _():
        for owner in range(4):
            here, there = output_copy(owner)
            pl.when(p == owner)(here.wait)
            pl.when(p != owner)(there.wait_send)

    s.hop_out[:M] = grad_out.astype(BF16)
    table_out = local(s.rel, o.table, s.out_sem.at[3])
    right_a_out = [deliver_rows(0, 2, s.hop_out.at[:M])] + deliver_right(0, s.hidden, range(3))
    vecs_a_out = deliver_vecs(0, s.vecs_a)

    def merged_copy(owner):
        return local(s.slope.at[owner, :, : D // 2], o.merged.at[owner], s.piece_sem.at[owner])

    @pl.when(upper)
    def _():
        hop(s.grad_m)
        start_all(right_a_out)
        table_out.start()
        vecs_a_out.start()
        for copy in hop_copies(s.grad_m):
            copy.wait_send()

    @pl.when(lower)
    def _():
        saved = [
            local(o.tokens.at[2 + k], s.qkv.at[k], s.out_sem.at[1 + k]) for k in range(2)
        ]
        start_all(saved)
        start_all(right_a_out)
        table_out.start()
        wait_all(right_m_out)
        halves = [s.acc, s.inverse]
        for k in range(4):
            rows = slice(k * CHUNK, (k + 1) * CHUNK)
            here = slice(k % 2 * CHUNK, (k % 2 + 1) * CHUNK)
            halves[k // 2][:, here] = dot_nt(s.hop_out[:M], s.w_merge[rows])
        wait_all(saved)
        gain = jnp.concatenate([vec_a[1:2], vec_a[2:3]], 1)
        values = jnp.concatenate([s.qkv[0], s.qkv[1]], 1).astype(F32)
        grad_in, gain_grad, shift_grad = norm_backward(
            jnp.concatenate([s.acc[...], s.inverse[...]], 1), values, gain
        )
        wide = D // 8
        for owner in range(4):
            for part in range(4):
                start = part * (D // 2) + owner * wide
                s.slope[owner, :, part * wide : (part + 1) * wide] = grad_in[
                    :, start : start + wide
                ].astype(BF16)
            merged_copy(owner).start()
        s.vecs_a[1:2] = gain_grad[:, :D]
        s.vecs_a[2:3] = gain_grad[:, D:]
        s.vecs_a[7:8] = shift_grad[:, :D]
        s.vecs_a[8:9] = shift_grad[:, D:]
        vecs_a_out.start()
        for owner in range(4):
            merged_copy(owner).wait()

    @pl.when(upper)
    def _():
        wait_all(right_m_out)

    wait_all(right_a_out + [table_out, vecs_a_out, vecs_m_out, mixed_out, grad_m_out])
    pl.when(upper)(normed_out.wait)
    given = [deliver_rows(0, 0, s.normed), mixed_out, vecs_a_out, grad_a_out] + right_a_out
    given += [normed_out, grad_m_out, vecs_m_out] + right_m_out
    for copy in given:
        copy.wait_recv()

    @pl.when(lower)
    def _():
        for copy in deliver_hidden(0, s.hidden, range(2)) + hidden_lower:
            copy.wait_recv()

    @pl.when(upper)
    def _():
        for copy in hidden_upper:
            copy.wait_recv()

    @pl.when(p == 2)
    def _():
        for k in over:
            for core in range(2):
                hidden_over(k, core).wait_recv()

    for source in (2, 3):

        @pl.when(p != source)
        def _(source=source):
            wide = D // 4
            remote(
                s.hop_out.at[:M, :wide], o.outs.at[source % 2], s.piece_sem.at[0], s.outs_in.at[source % 2], (source, w_at)
            ).wait_recv()

    vec_copy.wait_send()

    @pl.when(c == 0)
    def _():
        for copy in gifts(attention_parts, s.attention_sem):
            copy.wait_send()

        @pl.when(lower)
        def _():
            for copy in merge_gifts():
                copy.wait_send()

    @pl.when(c == 1)
    def _():
        for copy in gifts(mlp_parts, s.mlp_sem):
            copy.wait_send()


def forward_backward(page_tokens, blank, cotangent, first, second, gains, biases, tables):
    channels = page_tokens.shape[-1]
    crops = blank.shape[0]
    rolls = np.stack([hop_matrix(False), hop_matrix(True)])
    operands = {
        "tokens": jnp.transpose(page_tokens, (0, 2, 1, 3)).reshape(crops, 4 * TOK, channels),
        "cotangent": cotangent,
        "first": first,
        "second": second,
        "pack": jnp.asarray(offset_pack(), BF16),
        "roll": jnp.asarray(rolls, BF16),
        "pick": jnp.asarray(np.pad(merge_matrix(), ((0, 0), (0, 0), (0, D - 4 * TOK))), BF16),
        "cot": jnp.asarray(cotangent_matrix(), BF16),
        "gains": jnp.transpose(gains, (1, 0, 2)),
        "biases": jnp.transpose(biases, (1, 0, 2)),
        "blank": blank,
        "tables": tables,
        "keys": jnp.asarray(key_matrix(), BF16),
        "regions": jnp.asarray(region_masks(), F32),
    }
    in_vmem = ("gains", "biases", "blank", "tables", "keys", "regions")
    four = (4, M, D)
    outs = {
        "left": ((2 * M, D), BF16),
        "left_b": ((2 * M, D), BF16),
        "right_b": ((2 * M, D), BF16),
        "right": ((4, 2 * M, D), BF16),
        "hidden": ((4, 2 * M, D), BF16),
        "vecs": ((2, 16, D), F32),
        "table": ((HEADS * ROWS, 128), F32),
        "outs": ((2, M, D // 4), BF16),
        "merged": ((4, M, D // 2), BF16),
        "tokens": ((5, M, D), BF16),
    }
    scratch = {
        "w_qkv": pltpu.VMEM((STEPS, D, 3 * GROUP), BF16),
        "w_out": pltpu.VMEM((STEPS, GROUP, D), BF16),
        "w1": pltpu.VMEM((CHUNKS, D, CHUNK), BF16),
        "w2": pltpu.VMEM((CHUNKS, CHUNK, D), BF16),
        "w_merge": pltpu.VMEM((2 * D, D), BF16),
        "x": pltpu.VMEM((M, D), F32),
        "normed": pltpu.VMEM((M, D), BF16),
        "mixed": pltpu.VMEM((M, D), BF16),
        "qkv": pltpu.VMEM((3, M, D), BF16),
        "exps": pltpu.VMEM((WINS, HEADS, ROWS, 128), BF16),
        "inverse": pltpu.VMEM((M, D), F32),
        "mid": pltpu.VMEM((M, D), BF16),
        "hidden": pltpu.VMEM(four, BF16),
        "slope": pltpu.VMEM(four, BF16),
        "pre": pltpu.VMEM((2, M, CHUNK), F32),
        "acc": pltpu.VMEM((M, D), F32),
        "hop_out": pltpu.VMEM((M + ROWS, D), BF16),
        "grad_m": pltpu.VMEM((M, D), BF16),
        "grad_a": pltpu.VMEM((M, D), BF16),
        "rel": pltpu.VMEM((HEADS * ROWS, 128), F32),
        "mask": pltpu.VMEM((WINS, ROWS, 128), F32),
        "vec": pltpu.VMEM((2, 16, D), F32),
        "vecs_a": pltpu.VMEM((16, D), F32),
        "vecs_m": pltpu.VMEM((16, D), F32),
        "tokens": pltpu.VMEM((2, 4 * TOK, channels), BF16),
        "table": pltpu.VMEM((HEADS, OFFSETS), F32),
        "cotangent": pltpu.VMEM((TOK, D), BF16),
        "roll": pltpu.VMEM((M, M + ROWS), BF16),
        "const_sem": DMA((7,)),
        "pick_sem": DMA((4,)),
        "token_sem": DMA((2,)),
        "vec_sem": DMA((2,)),
        "attention_sem": DMA((4 * STEPS,)),
        "mlp_sem": DMA((2 * CHUNKS,)),
        "merge_sem": DMA((2, STEPS)),
        "give_sem": DMA((16,)),
        "out_sem": DMA((4,)),
        "give_out": DMA((2, 12)),
        "give_in": DMA((2, 12)),
        "save_sem": DMA((5,)),
        "over_sem": DMA((4,)),
        "over_in": DMA((2, 4)),
        "outs_in": DMA((2,)),
        "piece_sem": DMA((4,)),
        "hop_sem": DMA((6,)),
    }
    found = pl.pallas_call(
        functools.partial(main_kernel, tuple(operands), tuple(outs), tuple(scratch)),
        in_specs=[IN_VMEM if k in in_vmem else ANYWHERE for k in operands],
        out_specs=[ANYWHERE] * len(outs),
        out_shape=[shape_of(*value) for value in outs.values()],
        scratch_shapes=list(scratch.values()),
        compiler_params=pltpu.CompilerParams(
            collective_id=1, has_side_effects=True, vmem_limit_bytes=61 * 1024 * 1024
        ),
        name="forward_backward",
    )(*operands.values())
    return dict(zip(outs, found))


PIECES = 2 * HALF
AHEAD = 3
RING = AHEAD + 2
LAG = 2
LEFT = PIECES
SLOTS = PIECES + 4
OWN_PIECES = (HALF + HALF // 2, 2 * HALF - RELAY, HALF + RELAY, 2 * HALF)
EARLY = AHEAD + 1


def bit_reversed(index, bits):
    return sum(((index >> b) & 1) << (bits - 1 - b) for b in range(bits))


def by_device(p, values):
    found = values[-1]
    for index in range(len(values) - 2, -1, -1):
        found = jnp.where(p == index, values[index], found)
    return found


def reduce_kernel(bits, names, *refs):
    refs = list(refs)
    count = 1 << bits
    share = D // count
    quarter = count // 4
    i = Refs(names, refs[: len(names)])
    refs = refs[len(names) :]
    first_ref, second_ref, vecs_ref, tokens_ref, tables_ref = refs[:5]
    refs = refs[5:]
    lhs_in, lhs, rhs, vec_in, vec_own, relay, score, unroll, inner, outer, table, table_recv, send, keep, whole, merged = refs[:16]
    refs = refs[16:]
    recv = refs[:bits]
    vec_recv = refs[bits : 2 * bits]
    (
        row_sem,
        stage_send,
        stage_recv,
        vec_send_sem,
        vec_recv_sem,
        table_send_sem,
        table_recv_sem,
        const_sem,
        cross_local,
        cross_send,
        cross_recv,
        relay_send,
        relay_recv,
        ready,
    ) = refs[2 * bits :]

    p = lax.axis_index("pipe")
    w = lax.axis_index("wide")
    c = lax.rem(p, 2)
    upper = p >= 2
    pair = p + 1 - 2 * c
    across = lax.rem(p + 2, 4)
    partner = []
    mine = []
    for s in range(bits):
        bit = lax.rem(w // (1 << s), 2)
        mine.append(bit)
        partner.append(w + (1 << s) * (1 - 2 * bit))

    barrier = pltpu.get_barrier_semaphore()
    pl.semaphore_signal(barrier, inc=1, device_id=(pair, w), device_id_type=MESH)
    for s in range(bits):
        pl.semaphore_signal(barrier, inc=1, device_id=(p, partner[s]), device_id_type=MESH)

    @pl.when(upper)
    def _():
        for other in (0, 1):
            pl.semaphore_signal(barrier, inc=1, device_id=(other, w), device_id_type=MESH)
        pl.semaphore_wait(barrier, 1 + bits)

    @pl.when(jnp.logical_not(upper))
    def _():
        pl.semaphore_wait(barrier, 3 + bits)
        for other in (2, 3):
            pl.semaphore_signal(ready, inc=1, device_id=(other, w), device_id_type=MESH)

    pieces = by_device(p, OWN_PIECES)

    def columns(ref, j):
        return ref.at[j // PER, :, j % PER * PIECE : (j % PER + 1) * PIECE]

    def sources(index):
        found = [(LEFT, i.left, lhs_in.at[0])]
        found += [(j, columns(i.right, j), rhs.at[j]) for j in range(HALF)]
        if index % 2 == 0:
            found.insert(AHEAD + 1, (LEFT + 1, i.left_b, lhs_in.at[1]))
        where = ((0, HALF // 2), (RELAY, HALF), (0, RELAY), (0, HALF))[index]
        more = [(LEFT + 2, i.right_b, lhs_in.at[2])]
        more += [(HALF + j, columns(i.hidden, j), rhs.at[HALF + j]) for j in range(*where)]
        return more + found if index == 2 else found + more

    def issue(early):
        part = slice(0, EARLY) if early else slice(EARLY, None)
        for index in range(4):

            @pl.when(p == index)
            def _(index=index):
                for slot, source, target in sources(index)[part]:
                    pltpu.make_async_copy(source, target, row_sem.at[slot]).start()

    issue(True)
    pltpu.make_async_copy(i.vecs, vec_in, row_sem.at[LEFT + 3]).start()
    pltpu.make_async_copy(i.table, score, const_sem.at[0]).start()
    pltpu.make_async_copy(i.inner, inner, const_sem.at[1]).start()
    pltpu.make_async_copy(i.outer, outer, const_sem.at[2]).start()

    @pl.when(p == 2)
    def _():
        pltpu.make_async_copy(i.unroll, unroll, const_sem.at[3]).start()

    def token_copy(source, target, to):
        return pltpu.make_async_remote_copy(
            merged.at[target],
            tokens_ref.at[source],
            cross_send.at[target],
            cross_recv.at[source],
            device_id=(to, w),
            device_id_type=MESH,
        )

    def token_own(index):
        return pltpu.make_async_copy(merged.at[index], tokens_ref.at[index], cross_local)

    merged_in = pltpu.make_async_copy(i.merged, merged, const_sem.at[4])

    @pl.when(jnp.logical_not(upper))
    def _():
        merged_in.start()

    def rows_wait(slot, target):
        pltpu.make_async_copy(target, target, row_sem.at[slot]).wait()

    def turn(k, unrolled):
        rows_wait(LEFT + k, lhs_in.at[k])
        if unrolled:
            pltpu.make_async_copy(i.unroll, unroll, const_sem.at[3]).wait()
        per = max(1, 128 // share)
        at_row = lax.broadcasted_iota(jnp.int32, (128, 128), 0)
        at_lane = lax.broadcasted_iota(jnp.int32, (128, 128), 1)
        unit = jnp.where(at_row == at_lane, 1.0, 0.0).astype(BF16)
        for block in range(D // 128):
            flipped = dot_nt(unit, lhs_in[k, :, block * 128 : (block + 1) * 128]).astype(BF16)
            if unrolled:
                flipped = dot(flipped, unroll[...]).astype(BF16)
            if share >= 128:
                at = bit_reversed(block * 128 // share, bits)
                start = block * 128 % share
                lhs[k, at // quarter, at % quarter, start : start + 128] = flipped
            else:
                for q in range(per):
                    at = bit_reversed(block * per + q, bits)
                    lhs[k, at // quarter, at % quarter] = flipped[q * share : (q + 1) * share]

    def swapped(t):
        return (4 - lax.rem(t, 4)) // 4

    def stage_of(s, t):
        if s >= 2:
            return mine[s], partner[s]
        odd = swapped(t)
        return (
            mine[s] + odd * (mine[1 - s] - mine[s]),
            partner[s] + odd * (partner[1 - s] - partner[s]),
        )

    def stage_copy(s, t):
        j = piece(t)
        half, to = stage_of(s, t)
        if s == 0:
            source = send.at[lax.rem(t, RING)]
        elif s == 1:
            source = recv[0].at[j, 1 - half]
        else:
            width = count >> (s + 1)
            source = recv[s - 1].at[j, pl.ds((1 - half) * width, width)]
        return pltpu.make_async_remote_copy(
            source,
            recv[s].at[j],
            stage_send.at[s, j],
            stage_recv.at[s, j],
            device_id=(p, to),
            device_id_type=MESH,
        )

    def send_first(t):
        j = piece(t)
        slot = lax.rem(t, RING)

        @pl.when((j == 0) & (p == 2))
        def _():
            turn(0, False)

        @pl.when((j == HALF - PER) & (c == 0))
        def _():
            turn(1, False)

        @pl.when(j == by_device(p, (HALF, HALF + RELAY, PIECES, HALF)))
        def _():
            turn(2, False)

        @pl.when(t >= RING)
        def _():
            stage_copy(0, t - RING).wait_send()

        rows_wait(j, rhs.at[j])
        odd = swapped(t)
        sel = jnp.where(j < HALF - PER, 0, jnp.where(j < HALF, 1 - c, 2))
        product = dot(lhs[sel].reshape(D, 2 * M), rhs[j])
        for high in range(2):
            for low in range(2):
                bit = (1 - odd) * high + odd * low
                part = (1 - odd) * low + odd * high
                keeps = 1 - (bit - mine_first(odd)) * (bit - mine_first(odd))
                rows = (2 * high + low) * (D // 4)
                whole[2 * keeps + part] = product[rows : rows + D // 4].reshape(quarter, share, PIECE)
        send[slot] = whole[:2].astype(BF16)
        keep[slot] = whole[2:]
        stage_copy(0, t).start()

    def mine_first(odd):
        return mine[0] + odd * (mine[1] - mine[0])

    def store_out(j, values):
        @pl.when(j < HALF)
        def _():
            first_ref[:, pl.ds(pl.multiple_of(j * PIECE, PIECE), PIECE)] = values

        @pl.when(j >= HALF)
        def _():
            turned = jnp.transpose(values)

            @pl.when(p == 2)
            def _():
                relay[j - HALF] = turned

            @pl.when(p != 2)
            def _():
                second_ref[pl.ds(pl.multiple_of((j - HALF) * PIECE, PIECE), PIECE)] = turned

    def take(s, t):
        j = piece(t)
        stage_copy(s, t).wait_recv()
        half, _ = stage_of(s, t)
        if s == 0:
            kept = keep[lax.rem(t, RING)]
        elif s == 1:
            kept = recv[0][j, half].astype(F32)
        else:
            width = count >> (s + 1)
            kept = recv[s - 1][j, pl.ds(half * width, width)].astype(F32)
        total = kept + recv[s][j].astype(F32)
        if s == bits - 1:
            store_out(j, total[0])
        else:
            recv[s][j] = total.astype(BF16)
            stage_copy(s + 1, t).start()

    def piece(t):
        return by_device(
            p,
            (
                t,
                jnp.where(t < HALF, t, t + RELAY),
                jnp.where(t < RELAY, t + HALF, t - RELAY),
                t,
            ),
        )

    @pl.when(p == 2)
    def _():
        turn(2, True)

    @pl.when(p != 2)
    def _():
        turn(0, False)

    issue(False)

    for index in range(2):

        @pl.when(p == index)
        def _(index=index):
            merged_in.wait()
            token_own(index).start()
            for target in range(4):
                if target != index:
                    token_copy(index, target, target).start()

    lax.fori_loop(0, AHEAD, lambda t, _: (send_first(t), 0)[1], 0)

    def vec_copy(s):
        width = count >> (s + 1)
        held = vec_own if s == 0 else vec_recv[s - 1]
        return pltpu.make_async_remote_copy(
            held.at[pl.ds((1 - mine[s]) * width, width)],
            vec_recv[s],
            vec_send_sem.at[s],
            vec_recv_sem.at[s],
            device_id=(p, partner[s]),
            device_id_type=MESH,
        )

    def vec_start():
        rows_wait(LEFT + 3, vec_in)
        both = jnp.concatenate([vec_in[0] + vec_in[1], jnp.zeros((112, D), F32)], 0)
        per = max(1, 128 // share)
        for block in range(D // 128):
            flipped = jnp.transpose(both[:, block * 128 : (block + 1) * 128])
            if share >= 128:
                at = bit_reversed(block * 128 // share, bits)
                inside = block * 128 % share
                vec_own[at, inside : inside + 128] = flipped
            else:
                for q in range(per):
                    at = bit_reversed(block * per + q, bits)
                    vec_own[at] = flipped[q * share : (q + 1) * share]
        vec_copy(0).start()

    def vec_step(s):
        width = count >> (s + 1)
        vec_copy(s).wait_recv()
        held = vec_own if s == 0 else vec_recv[s - 1]
        total = held[pl.ds(mine[s] * width, width)] + vec_recv[s][...]
        if s == bits - 1:
            vecs_ref[...] = total[0]
        else:
            vec_recv[s][...] = total
            vec_copy(s + 1).start()

    def table_copy(s):
        to = (pair, w) if s == 0 else (p, partner[s - 1])
        return pltpu.make_async_remote_copy(
            table.at[s],
            table_recv.at[s],
            table_send_sem.at[s],
            table_recv_sem.at[s],
            device_id=to,
            device_id_type=MESH,
        )

    def table_start():
        pltpu.make_async_copy(i.table, score, const_sem.at[0]).wait()
        pltpu.make_async_copy(i.inner, inner, const_sem.at[1]).wait()
        pltpu.make_async_copy(i.outer, outer, const_sem.at[2]).wait()
        by_row = None
        for ci in range(WIN):
            rows = jnp.concatenate(
                [score[pl.ds(ri * WIN + ci, HEADS, stride=ROWS), :] for ri in range(WIN)], 0
            )
            term = split_dot(rows, inner[ci])
            by_row = term if by_row is None else by_row + term
        total = None
        for ri in range(WIN):
            term = split_dot(by_row[ri * HEADS : (ri + 1) * HEADS], outer[ri])
            total = term if total is None else total + term
        table[0] = total
        table_copy(0).start()

    def table_cross():
        x = p // 2
        return pltpu.make_async_remote_copy(
            table.at[bits + 1],
            tables_ref.at[x],
            table_send_sem.at[bits + 1],
            table_recv_sem.at[bits + 1],
            device_id=(across, w),
            device_id_type=MESH,
        )

    def table_step(s):
        table_copy(s).wait_recv()
        table[s + 1] = table[s] + table_recv[s]
        if s < bits:
            table_copy(s + 1).start()
        else:
            tables_ref[p // 2] = table[s + 1]

            @pl.when(jnp.logical_not(upper))
            def _():
                table_cross().start()

    def relay_copy(k):
        return pltpu.make_async_remote_copy(
            relay.at[k],
            second_ref.at[k * PIECE : (k + 1) * PIECE],
            relay_send.at[k],
            relay_recv.at[k],
            device_id=(1, w),
            device_id_type=MESH,
        )

    vec_start()
    table_start()

    def body(t, carry):
        for s in range(bits):
            at = t - LAG * s

            @pl.when((at >= 0) & (at < pieces))
            def _(s=s, at=at):
                take(s, at)
                if s == 0:

                    @pl.when(t + AHEAD < pieces)
                    def _():
                        send_first(t + AHEAD)

        for s in range(bits):

            @pl.when(t == 2 * s + 2)
            def _(s=s):
                vec_step(s)

        for s in range(bits + 1):

            @pl.when(t == 2 * s + 2)
            def _(s=s):
                table_step(s)

        @pl.when(upper & (t == RELAY + LAG * (bits - 1)))
        def _():
            pl.semaphore_wait(ready, 2)
            table_cross().start()

            @pl.when(p == 2)
            def _():
                for k in range(RELAY):
                    relay_copy(k).start()

        return carry

    lax.fori_loop(0, pieces + LAG * (bits - 1), body, 0)

    def clear(j, carry):
        second_ref[pl.ds(pl.multiple_of(j * PIECE, PIECE), PIECE)] = jnp.zeros((PIECE, share), F32)
        return carry

    lax.fori_loop(by_device(p, (HALF // 2, HALF, 0, HALF)), HALF, clear, 0)

    def drain(t, carry):
        @pl.when(t >= pieces - RING)
        def _():
            stage_copy(0, t).wait_send()

        for s in range(1, bits):
            stage_copy(s, t).wait_send()
        return carry

    lax.fori_loop(0, pieces, drain, 0)
    for s in range(bits):
        vec_copy(s).wait_send()
    for s in range(bits + 1):
        table_copy(s).wait_send()
    table_cross().wait()

    for index in range(4):

        @pl.when(p == index)
        def _(index=index):
            if index < 2:
                token_own(index).wait()
                for target in range(4):
                    if target != index:
                        token_copy(index, target, target).wait_send()
            for source in range(2):
                if source != index:
                    token_copy(source, index, source).wait_recv()
            if index == 2:
                for k in range(RELAY):
                    relay_copy(k).wait_send()
            if index == 1:
                for k in range(RELAY):
                    relay_copy(k).wait_recv()


def reduce_gradients(made, count):
    bits = count.bit_length() - 1
    share = D // count
    anywhere = pl.BlockSpec(memory_space=pl.ANY)
    in_vmem = pl.BlockSpec(memory_space=pltpu.VMEM)
    inner, outer = offset_blocks()
    flat = (HEADS * ROWS, 128)
    operands = {name: made[name] for name in made if name not in ("tokens", "outs")}
    operands["unroll"] = jnp.asarray(unroll_matrix(), BF16)
    operands["inner"] = jnp.asarray(inner, BF16)
    operands["outer"] = jnp.asarray(outer, BF16)
    merged = made["merged"]
    dma = pltpu.SemaphoreType.DMA
    halves = [(2, count // 4)] + [(count >> (s + 1),) for s in range(1, bits)]
    return pl.pallas_call(
        functools.partial(reduce_kernel, bits, tuple(operands)),
        in_specs=[anywhere] * len(operands),
        out_specs=[in_vmem] * 3 + [anywhere] + [in_vmem],
        out_shape=[
            shape_of((share, FF), F32),
            shape_of((FF, share), F32),
            shape_of((share, 128), F32),
            shape_of((2,) + merged.shape[1:], BF16),
            shape_of((2, HEADS, OFFSETS), F32),
        ],
        scratch_shapes=[
            pltpu.VMEM((3, 2 * M, D), BF16),
            pltpu.VMEM((3, 4, count // 4, share, 2 * M), BF16),
            pltpu.VMEM((PIECES, 2 * M, PIECE), BF16),
            pltpu.VMEM((2, 16, D), F32),
            pltpu.VMEM((count, share, 128), F32),
            pltpu.VMEM((RELAY, PIECE, share), F32),
            pltpu.VMEM(flat, F32),
            pltpu.VMEM((2 * M, 2 * M), BF16),
            pltpu.VMEM(inner.shape, BF16),
            pltpu.VMEM(outer.shape, BF16),
            pltpu.VMEM((bits + 2, HEADS, OFFSETS), F32),
            pltpu.VMEM((bits + 1, HEADS, OFFSETS), F32),
            pltpu.VMEM((RING, 2, count // 4, share, PIECE), BF16),
            pltpu.VMEM((RING, 2, count // 4, share, PIECE), F32),
            pltpu.VMEM((4, count // 4, share, PIECE), F32),
            pltpu.VMEM(merged.shape, BF16),
            *[pltpu.VMEM((PIECES,) + half + (share, PIECE), BF16) for half in halves],
            *[pltpu.VMEM((count >> (s + 1), share, 128), F32) for s in range(bits)],
            dma((SLOTS,)),
            dma((bits, PIECES)),
            dma((bits, PIECES)),
            dma((bits,)),
            dma((bits,)),
            dma((bits + 2,)),
            dma((bits + 2,)),
            dma((5,)),
            dma,
            dma((4,)),
            dma((2,)),
            dma((RELAY,)),
            dma((RELAY,)),
            pltpu.SemaphoreType.REGULAR,
        ],
        compiler_params=pltpu.CompilerParams(
            collective_id=0, has_side_effects=True, vmem_limit_bytes=60 * 1024 * 1024
        ),
        name="reduce_gradients",
    )(*operands.values())


def finish_kernel(
    first_in, second_in, vecs_in, outs_in, parts_in, tables_in, order_in, split_in,
    output_ref, tokens_ref, first_out, second_out, gains_ref, biases_ref, tables_out,
    vecs_ref, outs_ref, parts_ref, tables_ref, order_ref, split_ref, first_ref, second_ref, sems,
):
    copies = [
        pltpu.make_async_copy(source, target, sems.at[k])
        for k, (source, target) in enumerate(
            (
                (parts_in, parts_ref),
                (split_in, split_ref),
                (outs_in, outs_ref),
                (order_in, order_ref),
                (tables_in, tables_ref),
                (vecs_in, vecs_ref),
                (first_in, first_ref),
                (second_in, second_ref),
            )
        )
    ]
    for copy in copies:
        copy.start()
    for copy in copies[:6]:
        copy.wait()
    on = []
    for copy, source, target in ((copies[6], first_ref, first_out), (copies[7], second_ref, second_out)):
        copy.wait()
        on.append(pltpu.make_async_copy(source, target, sems.at[8 + len(on)]))
        on[-1].start()
    tables_out[...] = tables_ref[:, :, : SPAN * SPAN]
    vecs = jnp.transpose(vecs_ref[...])
    for row in range(3):
        gains_ref[row] = vecs[row : row + 1]
    for row in range(6):
        biases_ref[row] = vecs[3 + row : 4 + row]
    channels = tokens_ref.shape[-1]
    for crop in range(WINS):
        windows = []
        for half in range(2):
            window = 2 * crop + half
            core, k = window // WINS, window % WINS
            windows.append((core, slice(k * ROWS, (k + 1) * ROWS)))
        rolled = jnp.concatenate([outs_ref[core, rows] for core, rows in windows], 0)
        output_ref[crop] = dot(order_ref[...], rolled).astype(BF16)
        total = None
        for half, (core, rows) in enumerate(windows):
            cells = jnp.concatenate(
                [parts_ref[core, rows, t * channels : (t + 1) * channels] for t in range(4)], 0
            )
            term = dot(split_ref[half], cells)
            total = term if total is None else total + term
        tokens_ref[crop] = total
    for copy in on:
        copy.wait()


def finish(out_parts, first_part, second_part, vec_part, token_parts, table_parts):
    share = first_part.shape[0]
    split = np.transpose(merge_matrix(), (0, 2, 1))
    channels = token_parts.shape[-1] // 4
    return pl.pallas_call(
        finish_kernel,
        in_specs=[ANYWHERE] * 8,
        out_specs=[IN_VMEM] * 2 + [ANYWHERE] * 2 + [IN_VMEM] * 3,
        out_shape=[
            shape_of((WINS, TOK, out_parts.shape[-1]), BF16),
            shape_of((WINS, 4 * TOK, channels), F32),
            shape_of(first_part.shape, F32),
            shape_of(second_part.shape, F32),
            shape_of((3, 1, share), F32),
            shape_of((6, 1, share), F32),
            shape_of((2, HEADS, SPAN * SPAN), F32),
        ],
        scratch_shapes=[
            pltpu.VMEM(vec_part.shape, F32),
            pltpu.VMEM(out_parts.shape, BF16),
            pltpu.VMEM(token_parts.shape, BF16),
            pltpu.VMEM(table_parts.shape, F32),
            pltpu.VMEM((TOK, 2 * ROWS), BF16),
            pltpu.VMEM(split.shape, BF16),
            pltpu.VMEM(first_part.shape, F32),
            pltpu.VMEM(second_part.shape, F32),
            DMA((10,)),
        ],
        compiler_params=pltpu.CompilerParams(vmem_limit_bytes=61 * 1024 * 1024),
        name="finish",
    )(
        first_part,
        second_part,
        vec_part,
        out_parts,
        token_parts,
        table_parts,
        jnp.asarray(output_matrix(), BF16),
        jnp.asarray(split, BF16),
    )


def padded_row(token):
    return (token // AREA) * ROWS + token % AREA


def rolled_source():
    cells = np.arange(TOK)
    rows, columns = cells // GRID_W, cells % GRID_W
    return ((rows + WIN // 2) % GRID_H) * GRID_W + (columns + WIN // 2) % GRID_W


def hop_matrix(inverse):
    source = rolled_source()
    if inverse:
        source = np.argsort(source)
    result = np.zeros((2, M, (WINS + 1) * ROWS), np.float32)
    for core in range(2):
        for k in range(WINS):
            window = WINS * core + k
            crop, part = window // 2, window % 2
            for t in range(AREA):
                token = source[part * AREA + t]
                taken = crop * 2 + token // AREA
                slot = taken - WINS * core
                if not 0 <= slot < WINS:
                    slot = WINS
                result[core, k * ROWS + t, slot * ROWS + token % AREA] = 1.0
    return result


def cotangent_matrix():
    source = rolled_source()
    result = np.zeros((2, M, 4 * 256), np.float32)
    for core in range(2):
        for k in range(WINS):
            window = WINS * core + k
            crop, part = window // 2, window % 2
            for t in range(AREA):
                result[core, k * ROWS + t, crop * 256 + source[part * AREA + t]] = 1.0
    return result


def output_matrix():
    source = rolled_source()
    result = np.zeros((TOK, 2 * ROWS), np.float32)
    for t in range(TOK):
        result[source[t], padded_row(t)] = 1.0
    return result


def offset_matrices():
    span = 2 * WIN - 1
    inner = np.zeros((WIN, 128, WIN, span), np.float32)
    outer = np.zeros((WIN, WIN, span, span, span), np.float32)
    for ci in range(WIN):
        for j in range(AREA):
            inner[ci, j, j // WIN, ci - j % WIN + WIN - 1] = 1.0
    for ri in range(WIN):
        for rj in range(WIN):
            for dc in range(span):
                outer[ri, rj, dc, ri - rj + WIN - 1, dc] = 1.0
    return (
        inner.reshape(WIN * 128, WIN * span),
        outer.reshape(WIN * WIN * span, span * span),
    )


def offset_blocks():
    inner, outer = offset_matrices()
    inner = np.pad(inner.reshape(WIN, 128, WIN * SPAN), ((0, 0), (0, 0), (0, INNER - WIN * SPAN)))
    outer = np.pad(
        outer.reshape(WIN, WIN * SPAN, SPAN * SPAN),
        ((0, 0), (0, INNER - WIN * SPAN), (0, OFFSETS - SPAN * SPAN)),
    )
    return inner, outer


def offset_pack():
    inner, outer = offset_blocks()
    result = np.zeros((WIN // 2, INNER, D), np.float32)
    for k in range(WIN):
        half = k % 2
        result[k // 2, :, half * OFFSETS : (half + 1) * OFFSETS] = outer[k]
        result[k // 2, half * 128 : (half + 1) * 128, 2 * OFFSETS :] = inner[k]
    return result


def unroll_matrix():
    source = rolled_source()
    result = np.zeros((2 * M, 2 * M), np.float32)
    for crop in range(WINS):
        for t in range(TOK):
            start = crop * 2 * ROWS
            result[start + padded_row(t), start + padded_row(source[t])] = 1.0
    return result


def merge_matrix():
    result = np.zeros((2, 4, ROWS, 2 * GRID_W, 2 * GRID_H), np.float32)
    for half in range(2):
        for part in range(4):
            right, down = part // 2, part % 2
            for t in range(AREA):
                result[half, part, t, 2 * (t % WIN) + right, 2 * (half * WIN + t // WIN) + down] = 1.0
    return result.reshape(2, 4 * ROWS, 4 * TOK)


def region_masks():
    cells = np.arange(TOK)
    rows_at, cols_at = cells // GRID_W, cells % GRID_W
    row_band = (rows_at >= GRID_H - WIN).astype(int) + (rows_at >= GRID_H - WIN // 2)
    col_band = (cols_at >= GRID_W - WIN).astype(int) + (cols_at >= GRID_W - WIN // 2)
    rolled = (row_band * 3 + col_band).reshape(2, AREA)
    result = np.zeros((4, ROWS, 128), np.float32)
    for part in range(2):
        result[part, :AREA, :AREA] = 1.0
        result[2 + part, :AREA, :AREA] = rolled[part][:, None] == rolled[part][None, :]
    return result


def key_matrix():
    source = rolled_source()
    result = np.zeros((TOK, 4, 128), np.float32)
    for part in range(2):
        for t in range(AREA):
            result[part * AREA + t, part, t] = 1.0
            result[source[part * AREA + t], 2 + part, t] = 1.0
    return result.reshape(TOK, 4 * 128)


def local(page_tokens, blank, cotangent, first, second, gains, biases, tables):
    count = lax.axis_size("wide")
    made = forward_backward(
        page_tokens, blank, cotangent, first[0], second[0], gains, biases, tables
    )
    output, token_grad, first_grad, second_grad, gain_grad, bias_grad, table_grad = finish(
        made["outs"], *reduce_gradients(made, count)
    )
    crops, rows, columns, channels = page_tokens.shape
    token_grad = token_grad.reshape(crops, columns, rows, channels // 4)
    return (
        output,
        jnp.transpose(token_grad, (0, 2, 1, 3)),
        first_grad[None],
        second_grad[None],
        jnp.transpose(gain_grad, (1, 0, 2)),
        jnp.transpose(bias_grad, (1, 0, 2)),
        table_grad,
    )


def solution(mesh):
    placed = (
        P("wide", None, None, None),
        P("wide", None),
        P("wide", None, None),
        P("pipe", None, None),
        P("pipe", None, None),
        P("pipe", None, None),
        P("pipe", None, None),
        P(),
    )
    return jax.shard_map(
        local,
        mesh=mesh,
        in_specs=placed,
        out_specs=(
            P("wide", None, "pipe"),
            P("wide", None, None, "pipe"),
            P("pipe", "wide", None),
            P("pipe", None, "wide"),
            P("pipe", None, "wide"),
            P("pipe", None, "wide"),
            P(),
        ),
        check_vma=False,
    )
```

```python
import functools
from itertools import zip_longest

import jax
import jax.numpy as jnp
import numpy as np
from jax import lax
from jax.experimental import pallas as pl
from jax.experimental.pallas import tpu as pltpu
from jax.sharding import PartitionSpec as P

HEADS = 32
WIN = 10
GRID_H = 20
GRID_W = 10
AREA = WIN * WIN
TOK = GRID_H * GRID_W
ROWS = 112
WINS = 3
M = ROWS * WINS
D = 1024
FF = 4096
CHUNK = 512
EPSILON = 1e-05
NEGATIVE = -1000000000.0
SCALE = 32 ** (-0.5)
MESH = pl.DeviceIdType.MESH
F32 = jnp.float32
BF16 = jnp.bfloat16


def shape_of(dims, kind):
    return jax.ShapeDtypeStruct(dims, kind)


def dot(left, right):
    return jnp.dot(left, right, preferred_element_type=F32)


def dot_nt(left, right):
    return lax.dot_general(left, right, (((1,), (1,)), ((), ())), preferred_element_type=F32)


def dot_tn(left, right):
    return lax.dot_general(left, right, (((0,), (0,)), ((), ())), preferred_element_type=F32)


def norm_parts(values):
    average = jnp.mean(values, -1, keepdims=True)
    centered = values - average
    inv_std = lax.rsqrt(jnp.mean(centered * centered, -1, keepdims=True) + EPSILON)
    return centered * inv_std, inv_std


def norm_backward(grad_out, values, gain):
    unit, inv_std = norm_parts(values)
    scaled = grad_out * gain
    grad_in = inv_std * (
        scaled
        - jnp.mean(scaled, -1, keepdims=True)
        - unit * jnp.mean(scaled * unit, -1, keepdims=True)
    )
    return (
        grad_in,
        jnp.sum(grad_out * unit, 0, keepdims=True),
        jnp.sum(grad_out, 0, keepdims=True),
    )


def split_dot(left, right, product=dot):
    high = left.astype(BF16)
    low = (left - high.astype(F32)).astype(BF16)
    return product(high, right) + product(low, right)


ANYWHERE = pl.BlockSpec(memory_space=pl.ANY)
IN_VMEM = pl.BlockSpec(memory_space=pltpu.VMEM)
DMA = pltpu.SemaphoreType.DMA
SPAN = 2 * WIN - 1
INNER = 256
OFFSETS = 384
GROUP = 256
GROUP_HEADS = GROUP // 32
STEPS = D // GROUP
CHUNKS = FF // CHUNK
PIECE = 256
HALF = FF // PIECE
PER = D // PIECE
RELAY = 12


class Refs:
    def __init__(self, names, refs):
        self.__dict__.update(zip(names, refs))


def lanes_at(start, size):
    return pl.ds(pl.multiple_of(start, 128), size)


def lane_masks():
    lanes = lax.broadcasted_iota(jnp.int32, (1, 128), 1)
    return [
        jnp.where((lanes >= 32 * h) & (lanes < 32 * h + 32), 1.0, 0.0).astype(BF16)
        for h in range(4)
    ]


def stacked(values, masks, rows):
    if rows > values.shape[0]:
        values = jnp.concatenate(
            [values, jnp.zeros((rows - values.shape[0], values.shape[1]), values.dtype)], 0
        )
    return jnp.concatenate([values * mask for mask in masks], 0)


def beside_ones(values, masks):
    ones = jnp.concatenate([jnp.broadcast_to(mask, (128, 128)) for mask in masks], 0)
    return jnp.concatenate([stacked(values, masks, 128), ones], 1)


def attention_forward(s, vec, weights):
    unit, _ = norm_parts(s.x[...])
    s.normed[...] = (unit * vec[0:1] + vec[3:4]).astype(BF16)
    s.acc[...] = jnp.zeros_like(s.acc)
    masks = lane_masks()

    def step(g, carry):
        weights(g)
        here = lanes_at(g * GROUP, GROUP)
        projected = dot(s.normed[...], s.w_qkv[g])
        query = (projected[:, :GROUP] + vec[4:5, here]).astype(BF16)
        key = projected[:, GROUP : 2 * GROUP].astype(BF16)
        value = (projected[:, 2 * GROUP :] + vec[5:6, here]).astype(BF16)
        for k, values in enumerate((query, key, value)):
            s.qkv[k, :, here] = values
        mixed = []
        for w in range(WINS):
            rows = slice(w * ROWS, (w + 1) * ROWS)
            allowed = s.mask[w] > 0.5
            parts = []
            for part in range(GROUP // 128):
                inside = slice(part * 128, (part + 1) * 128)
                lanes = lanes_at(g * GROUP + part * 128, 128)
                scores = dot_nt(query[rows, inside], stacked(key[rows, inside], masks, 128))
                found = []
                for h in range(4):
                    head = g * GROUP_HEADS + part * 4 + h
                    bias = s.rel[pl.ds(pl.multiple_of(head * ROWS, 8), ROWS)]
                    one = jnp.where(
                        allowed, scores[:, h * 128 : (h + 1) * 128] * SCALE + bias, NEGATIVE
                    )
                    exponent = jnp.exp(one - jnp.max(one, -1, keepdims=True)).astype(BF16)
                    s.exps[w, head] = exponent
                    found.append(exponent)
                sums = dot(jnp.concatenate(found, 1), beside_ones(value[rows, inside], masks))
                scale = 1.0 / sums[:, 128:]
                s.inverse[rows, lanes] = scale
                parts.append((sums[:, :128] * scale).astype(BF16))
            mixed.append(jnp.concatenate(parts, 1))
        mixed = jnp.concatenate(mixed, 0)
        s.mixed[:, here] = mixed
        s.acc[...] += dot(mixed, s.w_out[g])
        return carry

    lax.fori_loop(0, STEPS, step, 0)
    return s.x[...] + (s.acc[...] + vec[6:7])


def attention_backward(s, vec, right, vecs):
    masks = lane_masks()
    s.acc[...] = jnp.zeros_like(s.acc)

    def step(g, carry):
        here = lanes_at(g * GROUP, GROUP)
        mixed_grad = dot_nt(s.grad_a[...], s.w_out[g])
        scaled_grad = (mixed_grad * s.inverse[:, here]).astype(BF16)
        spread = (scaled_grad.astype(F32) * s.mixed[:, here].astype(F32)).astype(BF16)
        query, key, value = [s.qkv[k, :, here] for k in range(3)]
        made = []
        for w in range(WINS):
            rows = slice(w * ROWS, (w + 1) * ROWS)
            parts = []
            for part in range(GROUP // 128):
                inside = slice(part * 128, (part + 1) * 128)
                grad_here = scaled_grad[rows, inside]
                prob_grad = dot_nt(
                    jnp.concatenate([grad_here, -spread[rows, inside]], 1),
                    beside_ones(value[rows, inside], masks),
                )
                found = []
                draws = []
                for h in range(4):
                    head = g * GROUP_HEADS + part * 4 + h
                    exponent = s.exps[w, head]
                    score_grad = exponent.astype(F32) * prob_grad[:, h * 128 : (h + 1) * 128]
                    at = pl.ds(pl.multiple_of(head * ROWS, 8), ROWS)
                    if w == 0:
                        s.rel[at] = score_grad
                    else:
                        s.rel[at] += score_grad
                    found.append(exponent)
                    draws.append((score_grad * SCALE).astype(BF16))
                query_grad = dot(jnp.concatenate(draws, 1), stacked(key[rows, inside], masks, 128))
                key_grad = dot_tn(jnp.concatenate(draws, 0), stacked(query[rows, inside], masks, ROWS))
                value_grad = dot_tn(jnp.concatenate(found, 0), stacked(grad_here, masks, ROWS))
                parts.append([t[:ROWS].astype(BF16) for t in (query_grad, key_grad, value_grad)])
            made.append([jnp.concatenate([part[k] for part in parts], 1) for k in range(3)])
        made = [jnp.concatenate([window[k] for window in made], 0) for k in range(3)]
        for k in range(3):
            right[k, :, here] = made[k]
        s.acc[...] += dot_nt(jnp.concatenate(made, 1), s.w_qkv[g])
        return carry

    lax.fori_loop(0, STEPS, step, 0)
    grad_in, gain_grad, shift_grad = norm_backward(s.acc[...], s.x[...], vec[0:1])
    wide = s.grad_a[...].astype(F32)
    vecs[0:1] = gain_grad
    vecs[1:3] = jnp.zeros((2, D), F32)
    vecs[3:4] = shift_grad
    vecs[4:5] = jnp.sum(right[0].astype(F32), 0, keepdims=True)
    vecs[5:6] = jnp.sum(right[2].astype(F32), 0, keepdims=True)
    vecs[6:7] = jnp.sum(wide, 0, keepdims=True)
    vecs[7:16] = jnp.zeros((9, D), F32)
    return wide + grad_in


def gelu_parts(pre):
    cumulative = 0.5 * (1.0 + lax.erf(pre * 0.7071067811865476))
    density = jnp.exp(-0.5 * pre * pre) * 0.3989422804014327
    return (pre * cumulative).astype(BF16), (cumulative + pre * density).astype(BF16)


def mlp_forward(s, vec, weights):
    x = s.mid[...].astype(F32)
    unit, _ = norm_parts(x)
    s.normed[...] = (unit * vec[0:1] + vec[3:4]).astype(BF16)

    def product(j):
        weights(j)
        start = j % 2 * CHUNK
        bias = vec[4 + j // 2 : 5 + j // 2, start : start + CHUNK]
        s.pre[j % 2] = dot(s.normed[...], s.w1[j]) + bias

    def take(j):
        start = j % 2 * CHUNK
        term = dot(s.hidden[j // 2, :, start : start + CHUNK], s.w2[j])
        if j == 0:
            s.acc[...] = term
        else:
            s.acc[...] += term

    product(0)
    for j in range(CHUNKS):
        start = j % 2 * CHUNK
        if j + 1 < CHUNKS:
            product(j + 1)
        if j > 0:
            take(j - 1)
        values, slopes = gelu_parts(s.pre[j % 2])
        s.hidden[j // 2, :, start : start + CHUNK] = values
        s.slope[j // 2, :, start : start + CHUNK] = slopes
    take(CHUNKS - 1)
    return s.mid[...].astype(F32) + s.acc[...] + vec[8:9]


def mlp_backward(s, vec, vecs):
    def product(j):
        here = slice(j % 2 * CHUNK, (j % 2 + 1) * CHUNK)
        pre_grad = dot_nt(s.grad_m[...], s.w2[j]) * s.slope[j // 2, :, here].astype(F32)
        vecs[4 + j // 2 : 5 + j // 2, here] = jnp.sum(pre_grad, 0, keepdims=True)
        s.slope[j // 2, :, here] = pre_grad.astype(BF16)

    def take(j):
        here = slice(j % 2 * CHUNK, (j % 2 + 1) * CHUNK)
        term = dot_nt(s.slope[j // 2, :, here], s.w1[j])
        if j == 0:
            s.acc[...] = term
        else:
            s.acc[...] += term

    product(0)
    for j in range(CHUNKS):
        if j + 1 < CHUNKS:
            product(j + 1)
        take(j)
    grad_in, gain_grad, shift_grad = norm_backward(s.acc[...], s.mid[...].astype(F32), vec[0:1])
    wide = s.grad_m[...].astype(F32)
    vecs[0:1] = gain_grad
    vecs[1:3] = jnp.zeros((2, D), F32)
    vecs[3:4] = shift_grad
    vecs[8:9] = jnp.sum(wide, 0, keepdims=True)
    vecs[9:16] = jnp.zeros((7, D), F32)
    return wide + grad_in


def main_kernel(ins, outs, scratch, *refs):
    first = len(ins)
    second = first + len(outs)
    i, o, s = Refs(ins, refs[:first]), Refs(outs, refs[first:second]), Refs(scratch, refs[second:])
    p = lax.axis_index("pipe")
    w_at = lax.axis_index("wide")
    side, c = p // 2, lax.rem(p, 2)
    lower, upper = side == 0, side == 1
    pair = (p + 1 - 2 * c, w_at)
    across = (lax.rem(p + 2, 4), w_at)

    def local(source, target, sem):
        return pltpu.make_async_copy(source, target, sem)

    def remote(source, target, sent, got, to):
        return pltpu.make_async_remote_copy(
            source, target, sent, got, device_id=to, device_id_type=MESH
        )

    consts = [local(i.pack.at[k], s.hidden.at[k, :INNER], s.const_sem.at[k]) for k in range(4)]
    consts.append(local(i.pack.at[4], s.slope.at[0, :INNER], s.const_sem.at[4]))
    consts.append(local(i.roll.at[side, c], s.roll, s.const_sem.at[5]))
    picks = []
    for half in range(2):
        for source, target in (
            (i.pick.at[half, : 3 * ROWS], s.slope.at[1 + half]),
            (i.pick.at[half, 3 * ROWS :], s.slope.at[3, half * ROWS : (half + 1) * ROWS]),
        ):
            picks.append(local(source, target, s.pick_sem.at[len(picks)]))
    cot = local(i.cot.at[c], s.mixed, s.const_sem.at[6])

    def token_copy(k):
        return local(i.tokens.at[(c * WINS + k) // 2], s.tokens.at[k % 2], s.token_sem.at[k % 2])

    def cotangent_copy(k):
        return local(i.cotangent.at[k], s.cotangent, s.token_sem.at[0])

    for copy in consts:
        copy.start()

    @pl.when(lower)
    def _():
        token_copy(0).start()
        token_copy(1).start()
        for copy in picks:
            copy.start()

    @pl.when(upper)
    def _():
        cotangent_copy(0).start()
        cot.start()

    for row in range(3):
        s.vec[c, row : row + 1] = i.gains[row]
    for row in range(6):
        s.vec[c, 3 + row : 4 + row] = i.biases[row]
    s.vec[c, 9:16] = jnp.zeros((7, D), F32)
    barrier = pltpu.get_barrier_semaphore()
    for step in range(1, 4):
        pl.semaphore_signal(
            barrier, inc=1, device_id=(lax.rem(p + step, 4), w_at), device_id_type=MESH
        )
    beside = []
    for b in range(2):
        bit = lax.rem(w_at // (1 << b), 2)
        beside.append((pair[0], w_at + (1 << b) * (1 - 2 * bit)))
        pl.semaphore_signal(barrier, inc=1, device_id=beside[b], device_id_type=MESH)
    pl.semaphore_wait(barrier, 5)
    vec_copy = remote(s.vec.at[c], s.vec.at[c], s.vec_sem.at[0], s.vec_sem.at[1], pair)
    vec_copy.start()

    attention_parts = []
    for g in range(STEPS):
        for k in range(3):
            start = k * D + g * GROUP
            attention_parts.append(
                (i.first.at[:, start : start + GROUP], s.w_qkv.at[g, :, k * GROUP : (k + 1) * GROUP])
            )
        attention_parts.append((i.first.at[g * GROUP : (g + 1) * GROUP, 3 * D :], s.w_out.at[g]))
    mlp_parts = []
    for j in range(CHUNKS):
        here = slice(j * CHUNK, (j + 1) * CHUNK)
        mlp_parts.append((i.first.at[:, here], s.w1.at[j]))
        mlp_parts.append((i.second.at[here], s.w2.at[j]))
    merge_parts = []
    for g in range(STEPS):
        here = slice(g * GROUP, (g + 1) * GROUP)
        merge_parts.append((i.second.at[: 2 * D, here], s.w_merge.at[:, here]))

    def load(parts, got):
        for k, (source, target) in enumerate(parts):
            local(source, target, got.at[k]).start()

    def gifts(parts, got):
        found = []
        for k, (source, target) in enumerate(parts):
            to = beside[k // 8] if parts is attention_parts and k % 4 == 3 else pair
            found.append(remote(source, target, s.give_sem.at[k], got.at[k], to))
        return found

    def give(parts, got):
        for copy in gifts(parts, got):
            copy.start()

    def merge_gifts():
        return [
            remote(source, target, s.merge_sem.at[1, k], s.merge_sem.at[0, k], pair)
            for k, (source, target) in enumerate(merge_parts)
        ]

    mine = pl.ds(pl.multiple_of(c * M, 16), M)

    class Delivery:
        def __init__(self, section, item, source, target):
            self.here = c == section
            self.ends = source, target
            self.sems = s.give_out.at[section, item], s.give_in.at[section, item]

        def local(self):
            return local(*self.ends, self.sems[0])

        def remote(self):
            return remote(*self.ends, *self.sems, pair)

        def start(self):
            pl.when(self.here)(lambda: self.local().start())
            pl.when(jnp.logical_not(self.here))(lambda: self.remote().start())

        def wait(self):
            pl.when(self.here)(lambda: self.local().wait())
            pl.when(jnp.logical_not(self.here))(lambda: self.remote().wait_send())

        def wait_recv(self):
            pl.when(self.here)(lambda: self.remote().wait_recv())

    def deliver_rows(section, item, source):
        target = (o.left, o.left_b, o.right_b)[item]
        return Delivery(section, item, source, target.at[mine])

    def deliver_vecs(section, source):
        return Delivery(section, 3, source, o.vecs.at[c])

    def deliver_right(section, source, where=range(4)):
        return [Delivery(section, 4 + k, source.at[k], o.right.at[k, mine]) for k in where]

    def deliver_hidden(section, source, where):
        return [Delivery(section, 8 + k, source.at[k], o.hidden.at[k, mine]) for k in where]

    def start_all(copies):
        for copy in copies:
            copy.start()

    def wait_all(copies):
        for copy in copies:
            copy.wait()

    @pl.when(c == 0)
    def _():
        @pl.when(lower)
        def _():
            start_all(merge_gifts())
            for k, (source, target) in enumerate(merge_parts):
                local(source, target, s.merge_sem.at[0, k]).start()

        @pl.when(upper)
        def _():
            give(attention_parts, s.attention_sem)

        load(attention_parts, s.attention_sem)

    @pl.when(c == 1)
    def _():
        give(mlp_parts, s.mlp_sem)
        load(mlp_parts, s.mlp_sem)

    def arrived(target, sem):
        local(target, target, sem).wait()

    def attention_weights(g):
        for k in range(3):
            arrived(s.w_qkv.at[g, :, k * GROUP : (k + 1) * GROUP], s.attention_sem.at[4 * g + k])
        arrived(s.w_out.at[g], s.attention_sem.at[4 * g + 3])

    def mlp_weights(j):
        arrived(s.w1.at[j], s.mlp_sem.at[2 * j])
        arrived(s.w2.at[j], s.mlp_sem.at[2 * j + 1])

    for copy in consts:
        copy.wait()

    def outer(ri):
        block = s.hidden.at[ri // 2] if ri < 8 else s.slope.at[0]
        return block[:INNER, ri % 2 * OFFSETS : (ri % 2 + 1) * OFFSETS]

    def inner(ci):
        block = s.hidden.at[ci // 2] if ci < 8 else s.slope.at[0]
        return block[ci % 2 * 128 : (ci % 2 + 1) * 128, 2 * OFFSETS :]

    s.table[...] = jnp.zeros_like(s.table)
    s.table[:, : SPAN * SPAN] = jnp.where(lower, i.tables[0], i.tables[1])
    table = s.table[...]
    wide = jnp.concatenate([split_dot(table, outer(ri), dot_nt) for ri in range(WIN)], 0)
    s.rel[...] = jnp.zeros_like(s.rel)
    for ci in range(WIN):
        rows = split_dot(wide, inner(ci), dot_nt)
        for ri in range(WIN):
            s.rel[pl.ds(ri * WIN + ci, HEADS, stride=ROWS), :] = rows[ri * HEADS : (ri + 1) * HEADS]

    @pl.when(lower & (c == 0))
    def _():
        give(attention_parts, s.attention_sem)

    closed = dot(i.blank[...].astype(F32).astype(BF16), i.keys[...])
    at_row = lax.broadcasted_iota(jnp.int32, (ROWS, 128), 0)
    at_lane = lax.broadcasted_iota(jnp.int32, (ROWS, 128), 1)
    own = jnp.where(at_row == at_lane, 1.0, 0.0)
    for k in range(WINS):
        found = []
        for rolled in range(2):
            for core in range(2):
                crop, part = (WINS * core + k) // 2, (WINS * core + k) % 2
                start = (2 * rolled + part) * 128
                found.append((closed[crop : crop + 1, start : start + 128], i.regions[2 * rolled + part]))
        near = [[jnp.where(c == 0, found[2 * t][u], found[2 * t + 1][u]) for u in range(2)] for t in range(2)]
        row, region = [jnp.where(lower, near[0][u], near[1][u]) for u in range(2)]
        s.mask[k] = region * jnp.maximum(1.0 - row, own)

    @pl.when(upper)
    def _():
        cot.wait()
        for crop in range(WINS):
            cotangent_copy(crop).wait()
            term = dot(s.mixed[:, crop * 256 : crop * 256 + TOK], s.cotangent[...])
            if crop == 0:
                s.acc[...] = term
            else:
                s.acc[...] += term
            if crop + 1 < WINS:
                cotangent_copy(crop + 1).start()
        s.grad_m[...] = s.acc[...].astype(BF16)
        deliver_rows(1, 2, s.grad_m).start()

    arrived(s.vec.at[1 - c], s.vec_sem.at[1])
    vec_a, vec_m = s.vec.at[0], s.vec.at[1]

    def merge_saved():
        return [local(s.hidden.at[k], o.tokens.at[k], s.save_sem.at[k]) for k in range(4)]

    @pl.when(lower)
    def _():
        for copy in picks:
            copy.wait()
        gain = jnp.concatenate([vec_a[1:2], vec_a[2:3]], 1)
        shift = jnp.concatenate([vec_a[7:8], vec_a[8:9]], 1)
        area = 4 * TOK
        for k in range(WINS):
            rows = slice(k * ROWS, (k + 1) * ROWS)
            half = lax.rem(c + k, 2)
            token_copy(k).wait()
            picked = dot(s.slope[1 + half, :, :area], s.tokens[k % 2])
            last = s.slope[3, pl.ds(pl.multiple_of(half * ROWS, 16), ROWS), :area]
            picked = [picked[t * ROWS : (t + 1) * ROWS] for t in range(3)] + [dot(last, s.tokens[k % 2])]
            if k + 2 < WINS:
                token_copy(k + 2).start()
            merged = jnp.concatenate(picked, 1)
            s.hidden[2, rows] = merged[:, :D].astype(BF16)
            s.hidden[3, rows] = merged[:, D:].astype(BF16)
            unit, _ = norm_parts(merged)
            normed = (unit * gain + shift).astype(BF16)
            s.hidden[0, rows] = normed[:, :D]
            s.hidden[1, rows] = normed[:, D:]
        start_all(merge_saved())

        for g in range(STEPS):
            here = slice(g * GROUP, (g + 1) * GROUP)
            arrived(s.w_merge.at[:, here], s.merge_sem.at[0, g])
            s.x[:, here] = dot(s.hidden[0], s.w_merge[:D, here]) + dot(s.hidden[1], s.w_merge[D:, here])

    shared = pl.ds(pl.multiple_of((1 - c) * (WINS - 1) * ROWS, 16), ROWS)
    shared_copy = remote(
        s.hop_out.at[shared], s.hop_out.at[M:], s.hop_sem.at[0], s.hop_sem.at[1], pair
    )

    early = pl.ds(pl.multiple_of(c * ROWS, 16), 2 * ROWS)
    late = pl.ds(pl.multiple_of((1 - c) * 2 * ROWS, 16), ROWS)

    def hop_copies(target):
        return [
            remote(s.grad_a.at[rows], target.at[rows], s.hop_sem.at[2 * k], s.hop_sem.at[2 * k + 1], across)
            for k, rows in ((1, early), (2, late))
        ]

    def hop(target):
        first, last = hop_copies(target)
        shared_copy.start()
        s.grad_a[early] = dot(s.roll[early, :M], s.hop_out[:M]).astype(BF16)
        first.start()
        near = dot(s.roll[late, :M], s.hop_out[:M])
        shared_copy.wait_recv()
        s.grad_a[late] = (near + dot(s.roll[late, M:], s.hop_out[M:])).astype(BF16)
        last.start()
        shared_copy.wait_send()

    @pl.when(upper)
    def _():
        for copy in hop_copies(s.grad_a):
            copy.wait_recv()
        s.x[...] = s.grad_a[...].astype(F32)

    s.mid[...] = attention_forward(s, vec_a, attention_weights).astype(BF16)
    normed_out = deliver_rows(0, 0, s.normed)
    mixed_out = deliver_rows(0, 1, s.mixed)

    @pl.when(lower)
    def _():
        aside = local(s.normed, o.tokens.at[4], s.save_sem.at[4])
        aside.start()
        wait_all(merge_saved())
        aside.wait()

    @pl.when(upper)
    def _():
        normed_out.start()
        normed_out.wait()

    s.hop_out[:M] = mlp_forward(s, vec_m, mlp_weights).astype(BF16)
    mixed_out.start()
    normed_out = deliver_rows(1, 0, s.normed)

    over = range(RELAY // PER)

    def hidden_over(k, core):
        rows = pl.ds(pl.multiple_of(core * M, 16), M)
        return remote(
            s.hidden.at[k], o.hidden.at[k, rows], s.over_sem.at[k], s.over_in.at[core, k], (2, w_at)
        )

    def output_copy(owner):
        wide = D // 4
        source = s.hop_out.at[:M, owner * wide : (owner + 1) * wide]
        return (
            local(source, o.outs.at[c], s.piece_sem.at[owner]),
            remote(source, o.outs.at[c], s.piece_sem.at[owner], s.outs_in.at[c], (owner, w_at)),
        )

    hidden_upper = deliver_hidden(1, s.hidden, range(4))
    hidden_lower = deliver_hidden(1, s.hidden, range(RELAY // PER, 4))
    grad_m_out = deliver_rows(1, 2, s.grad_m)

    @pl.when(lower)
    def _():
        hop(s.grad_a)
        start_all(hidden_lower)
        for copy in hop_copies(s.grad_a):
            copy.wait_send()
        for k in over:
            hidden_over(k, c).start()
        normed_out.start()
        normed_out.wait()

        def bring(at, buffer):
            back = local(o.tokens.at[at], buffer, s.save_sem.at[at])
            back.start()
            back.wait()

        late = [Delivery(0, 8 + k, b, o.hidden.at[k, mine]) for k, b in enumerate((s.normed, s.grad_a))]
        for k, copy in enumerate(late):
            bring(k, (s.normed, s.grad_a)[k])
            copy.start()
        wait_all(late)
        bring(4, s.normed)
        copy = deliver_rows(0, 0, s.normed)
        copy.start()
        copy.wait()
        for copy in hop_copies(s.grad_m):
            copy.wait_recv()
        grad_m_out.start()

    @pl.when(upper)
    def _():
        normed_out.start()
        start_all(hidden_upper)
        for owner in range(4):
            here, there = output_copy(owner)
            pl.when(p == owner)(here.start)
            pl.when(p != owner)(there.start)

    s.grad_a[...] = mlp_backward(s, vec_m, s.vecs_m).astype(BF16)
    right_m_out = deliver_right(1, s.slope)
    vecs_m_out = deliver_vecs(1, s.vecs_m)
    start_all(right_m_out)
    vecs_m_out.start()

    @pl.when(lower)
    def _():
        wait_all(hidden_lower)
        for k in over:
            hidden_over(k, c).wait_send()

    @pl.when(upper)
    def _():
        wait_all(hidden_upper)

    grad_a_out = Delivery(0, 4 + 3, s.grad_a, o.right.at[3, mine])
    grad_a_out.start()
    grad_out = attention_backward(s, vec_a, s.hidden, s.vecs_a)
    grad_a_out.wait()

    @pl.when(upper)
    def _():
        for owner in range(4):
            here, there = output_copy(owner)
            pl.when(p == owner)(here.wait)
            pl.when(p != owner)(there.wait_send)

    s.hop_out[:M] = grad_out.astype(BF16)
    table_out = local(s.rel, o.table, s.out_sem.at[3])
    right_a_out = [deliver_rows(0, 2, s.hop_out.at[:M])] + deliver_right(0, s.hidden, range(3))
    vecs_a_out = deliver_vecs(0, s.vecs_a)

    def merged_copy(owner):
        return local(s.slope.at[owner, :, : D // 2], o.merged.at[owner], s.piece_sem.at[owner])

    @pl.when(upper)
    def _():
        hop(s.grad_m)
        start_all(right_a_out)
        table_out.start()
        vecs_a_out.start()
        for copy in hop_copies(s.grad_m):
            copy.wait_send()

    @pl.when(lower)
    def _():
        saved = [
            local(o.tokens.at[2 + k], s.qkv.at[k], s.out_sem.at[1 + k]) for k in range(2)
        ]
        start_all(saved)
        start_all(right_a_out)
        table_out.start()
        wait_all(right_m_out)
        halves = [s.acc, s.inverse]
        for k in range(4):
            rows = slice(k * CHUNK, (k + 1) * CHUNK)
            here = slice(k % 2 * CHUNK, (k % 2 + 1) * CHUNK)
            halves[k // 2][:, here] = dot_nt(s.hop_out[:M], s.w_merge[rows])
        wait_all(saved)
        gain = jnp.concatenate([vec_a[1:2], vec_a[2:3]], 1)
        values = jnp.concatenate([s.qkv[0], s.qkv[1]], 1).astype(F32)
        grad_in, gain_grad, shift_grad = norm_backward(
            jnp.concatenate([s.acc[...], s.inverse[...]], 1), values, gain
        )
        wide = D // 8
        for owner in range(4):
            for part in range(4):
                start = part * (D // 2) + owner * wide
                s.slope[owner, :, part * wide : (part + 1) * wide] = grad_in[
                    :, start : start + wide
                ].astype(BF16)
            merged_copy(owner).start()
        s.vecs_a[1:2] = gain_grad[:, :D]
        s.vecs_a[2:3] = gain_grad[:, D:]
        s.vecs_a[7:8] = shift_grad[:, :D]
        s.vecs_a[8:9] = shift_grad[:, D:]
        vecs_a_out.start()
        for owner in range(4):
            merged_copy(owner).wait()

    @pl.when(upper)
    def _():
        wait_all(right_m_out)

    wait_all(right_a_out + [table_out, vecs_a_out, vecs_m_out, mixed_out, grad_m_out])
    pl.when(upper)(normed_out.wait)
    given = [deliver_rows(0, 0, s.normed), mixed_out, vecs_a_out, grad_a_out] + right_a_out
    given += [normed_out, grad_m_out, vecs_m_out] + right_m_out
    for copy in given:
        copy.wait_recv()

    @pl.when(lower)
    def _():
        for copy in deliver_hidden(0, s.hidden, range(2)) + hidden_lower:
            copy.wait_recv()

    @pl.when(upper)
    def _():
        for copy in hidden_upper:
            copy.wait_recv()

    @pl.when(p == 2)
    def _():
        for k in over:
            for core in range(2):
                hidden_over(k, core).wait_recv()

    for source in (2, 3):

        @pl.when(p != source)
        def _(source=source):
            wide = D // 4
            remote(
                s.hop_out.at[:M, :wide], o.outs.at[source % 2], s.piece_sem.at[0], s.outs_in.at[source % 2], (source, w_at)
            ).wait_recv()

    vec_copy.wait_send()

    @pl.when(c == 0)
    def _():
        for copy in gifts(attention_parts, s.attention_sem):
            copy.wait_send()

        @pl.when(lower)
        def _():
            for copy in merge_gifts():
                copy.wait_send()

    @pl.when(c == 1)
    def _():
        for copy in gifts(mlp_parts, s.mlp_sem):
            copy.wait_send()


def forward_backward(page_tokens, blank, cotangent, first, second, gains, biases, tables):
    channels = page_tokens.shape[-1]
    crops = blank.shape[0]
    rolls = np.stack([hop_matrix(False), hop_matrix(True)])
    operands = {
        "tokens": jnp.transpose(page_tokens, (0, 2, 1, 3)).reshape(crops, 4 * TOK, channels),
        "cotangent": cotangent,
        "first": first,
        "second": second,
        "pack": jnp.asarray(offset_pack(), BF16),
        "roll": jnp.asarray(rolls, BF16),
        "pick": jnp.asarray(np.pad(merge_matrix(), ((0, 0), (0, 0), (0, D - 4 * TOK))), BF16),
        "cot": jnp.asarray(cotangent_matrix(), BF16),
        "gains": jnp.transpose(gains, (1, 0, 2)),
        "biases": jnp.transpose(biases, (1, 0, 2)),
        "blank": blank,
        "tables": tables,
        "keys": jnp.asarray(key_matrix(), BF16),
        "regions": jnp.asarray(region_masks(), F32),
    }
    in_vmem = ("gains", "biases", "blank", "tables", "keys", "regions")
    four = (4, M, D)
    outs = {
        "left": ((2 * M, D), BF16),
        "left_b": ((2 * M, D), BF16),
        "right_b": ((2 * M, D), BF16),
        "right": ((4, 2 * M, D), BF16),
        "hidden": ((4, 2 * M, D), BF16),
        "vecs": ((2, 16, D), F32),
        "table": ((HEADS * ROWS, 128), F32),
        "outs": ((2, M, D // 4), BF16),
        "merged": ((4, M, D // 2), BF16),
        "tokens": ((5, M, D), BF16),
    }
    scratch = {
        "w_qkv": pltpu.VMEM((STEPS, D, 3 * GROUP), BF16),
        "w_out": pltpu.VMEM((STEPS, GROUP, D), BF16),
        "w1": pltpu.VMEM((CHUNKS, D, CHUNK), BF16),
        "w2": pltpu.VMEM((CHUNKS, CHUNK, D), BF16),
        "w_merge": pltpu.VMEM((2 * D, D), BF16),
        "x": pltpu.VMEM((M, D), F32),
        "normed": pltpu.VMEM((M, D), BF16),
        "mixed": pltpu.VMEM((M, D), BF16),
        "qkv": pltpu.VMEM((3, M, D), BF16),
        "exps": pltpu.VMEM((WINS, HEADS, ROWS, 128), BF16),
        "inverse": pltpu.VMEM((M, D), F32),
        "mid": pltpu.VMEM((M, D), BF16),
        "hidden": pltpu.VMEM(four, BF16),
        "slope": pltpu.VMEM(four, BF16),
        "pre": pltpu.VMEM((2, M, CHUNK), F32),
        "acc": pltpu.VMEM((M, D), F32),
        "hop_out": pltpu.VMEM((M + ROWS, D), BF16),
        "grad_m": pltpu.VMEM((M, D), BF16),
        "grad_a": pltpu.VMEM((M, D), BF16),
        "rel": pltpu.VMEM((HEADS * ROWS, 128), F32),
        "mask": pltpu.VMEM((WINS, ROWS, 128), F32),
        "vec": pltpu.VMEM((2, 16, D), F32),
        "vecs_a": pltpu.VMEM((16, D), F32),
        "vecs_m": pltpu.VMEM((16, D), F32),
        "tokens": pltpu.VMEM((2, 4 * TOK, channels), BF16),
        "table": pltpu.VMEM((HEADS, OFFSETS), F32),
        "cotangent": pltpu.VMEM((TOK, D), BF16),
        "roll": pltpu.VMEM((M, M + ROWS), BF16),
        "const_sem": DMA((7,)),
        "pick_sem": DMA((4,)),
        "token_sem": DMA((2,)),
        "vec_sem": DMA((2,)),
        "attention_sem": DMA((4 * STEPS,)),
        "mlp_sem": DMA((2 * CHUNKS,)),
        "merge_sem": DMA((2, STEPS)),
        "give_sem": DMA((16,)),
        "out_sem": DMA((4,)),
        "give_out": DMA((2, 12)),
        "give_in": DMA((2, 12)),
        "save_sem": DMA((5,)),
        "over_sem": DMA((4,)),
        "over_in": DMA((2, 4)),
        "outs_in": DMA((2,)),
        "piece_sem": DMA((4,)),
        "hop_sem": DMA((6,)),
    }
    found = pl.pallas_call(
        functools.partial(main_kernel, tuple(operands), tuple(outs), tuple(scratch)),
        in_specs=[IN_VMEM if k in in_vmem else ANYWHERE for k in operands],
        out_specs=[ANYWHERE] * len(outs),
        out_shape=[shape_of(*value) for value in outs.values()],
        scratch_shapes=list(scratch.values()),
        compiler_params=pltpu.CompilerParams(
            collective_id=1, has_side_effects=True, vmem_limit_bytes=61 * 1024 * 1024
        ),
        name="forward_backward",
    )(*operands.values())
    return dict(zip(outs, found))


PIECES = 2 * HALF
AHEAD = 3
RING = AHEAD + 2
LAG = 2
LEFT = PIECES
SLOTS = PIECES + 4
OWN_PIECES = (HALF + HALF // 2, 2 * HALF - RELAY, HALF + RELAY, 2 * HALF)
EARLY = AHEAD + 1


def bit_reversed(index, bits):
    return sum(((index >> b) & 1) << (bits - 1 - b) for b in range(bits))


def by_device(p, values):
    found = values[-1]
    for index in range(len(values) - 2, -1, -1):
        found = jnp.where(p == index, values[index], found)
    return found


def reduce_kernel(bits, names, *refs):
    refs = list(refs)
    count = 1 << bits
    share = D // count
    quarter = count // 4
    i = Refs(names, refs[: len(names)])
    refs = refs[len(names) :]
    first_ref, second_ref, vecs_ref, tokens_ref, tables_ref = refs[:5]
    refs = refs[5:]
    lhs_in, lhs, rhs, vec_in, vec_own, relay, score, unroll, inner, outer, table, table_recv, send, keep, whole, merged = refs[:16]
    refs = refs[16:]
    recv = refs[:bits]
    vec_recv = refs[bits : 2 * bits]
    (
        row_sem,
        stage_send,
        stage_recv,
        vec_send_sem,
        vec_recv_sem,
        table_send_sem,
        table_recv_sem,
        const_sem,
        cross_local,
        cross_send,
        cross_recv,
        relay_send,
        relay_recv,
        ready,
    ) = refs[2 * bits :]

    p = lax.axis_index("pipe")
    w = lax.axis_index("wide")
    c = lax.rem(p, 2)
    upper = p >= 2
    pair = p + 1 - 2 * c
    across = lax.rem(p + 2, 4)
    partner = []
    mine = []
    for s in range(bits):
        bit = lax.rem(w // (1 << s), 2)
        mine.append(bit)
        partner.append(w + (1 << s) * (1 - 2 * bit))

    barrier = pltpu.get_barrier_semaphore()
    pl.semaphore_signal(barrier, inc=1, device_id=(pair, w), device_id_type=MESH)
    for s in range(bits):
        pl.semaphore_signal(barrier, inc=1, device_id=(p, partner[s]), device_id_type=MESH)

    @pl.when(upper)
    def _():
        for other in (0, 1):
            pl.semaphore_signal(barrier, inc=1, device_id=(other, w), device_id_type=MESH)
        pl.semaphore_wait(barrier, 1 + bits)

    @pl.when(jnp.logical_not(upper))
    def _():
        pl.semaphore_wait(barrier, 3 + bits)
        for other in (2, 3):
            pl.semaphore_signal(ready, inc=1, device_id=(other, w), device_id_type=MESH)

    pieces = by_device(p, OWN_PIECES)

    def columns(ref, j):
        return ref.at[j // PER, :, j % PER * PIECE : (j % PER + 1) * PIECE]

    def sources(index):
        found = [(LEFT, i.left, lhs_in.at[0])]
        found += [(j, columns(i.right, j), rhs.at[j]) for j in range(HALF)]
        if index % 2 == 0:
            found.insert(AHEAD + 1, (LEFT + 1, i.left_b, lhs_in.at[1]))
        where = ((0, HALF // 2), (RELAY, HALF), (0, RELAY), (0, HALF))[index]
        more = [(LEFT + 2, i.right_b, lhs_in.at[2])]
        more += [(HALF + j, columns(i.hidden, j), rhs.at[HALF + j]) for j in range(*where)]
        return more + found if index == 2 else found + more

    def issue(early):
        part = slice(0, EARLY) if early else slice(EARLY, None)
        for index in range(4):

            @pl.when(p == index)
            def _(index=index):
                for slot, source, target in sources(index)[part]:
                    pltpu.make_async_copy(source, target, row_sem.at[slot]).start()

    issue(True)
    pltpu.make_async_copy(i.vecs, vec_in, row_sem.at[LEFT + 3]).start()
    pltpu.make_async_copy(i.table, score, const_sem.at[0]).start()
    pltpu.make_async_copy(i.inner, inner, const_sem.at[1]).start()
    pltpu.make_async_copy(i.outer, outer, const_sem.at[2]).start()

    @pl.when(p == 2)
    def _():
        pltpu.make_async_copy(i.unroll, unroll, const_sem.at[3]).start()

    def token_copy(source, target, to):
        return pltpu.make_async_remote_copy(
            merged.at[target],
            tokens_ref.at[source],
            cross_send.at[target],
            cross_recv.at[source],
            device_id=(to, w),
            device_id_type=MESH,
        )

    def token_own(index):
        return pltpu.make_async_copy(merged.at[index], tokens_ref.at[index], cross_local)

    merged_in = pltpu.make_async_copy(i.merged, merged, const_sem.at[4])

    @pl.when(jnp.logical_not(upper))
    def _():
        merged_in.start()

    def rows_wait(slot, target):
        pltpu.make_async_copy(target, target, row_sem.at[slot]).wait()

    def turn(k, unrolled):
        rows_wait(LEFT + k, lhs_in.at[k])
        if unrolled:
            pltpu.make_async_copy(i.unroll, unroll, const_sem.at[3]).wait()
        per = max(1, 128 // share)
        at_row = lax.broadcasted_iota(jnp.int32, (128, 128), 0)
        at_lane = lax.broadcasted_iota(jnp.int32, (128, 128), 1)
        unit = jnp.where(at_row == at_lane, 1.0, 0.0).astype(BF16)
        for block in range(D // 128):
            flipped = dot_nt(unit, lhs_in[k, :, block * 128 : (block + 1) * 128]).astype(BF16)
            if unrolled:
                flipped = dot(flipped, unroll[...]).astype(BF16)
            if share >= 128:
                at = bit_reversed(block * 128 // share, bits)
                start = block * 128 % share
                lhs[k, at // quarter, at % quarter, start : start + 128] = flipped
            else:
                for q in range(per):
                    at = bit_reversed(block * per + q, bits)
                    lhs[k, at // quarter, at % quarter] = flipped[q * share : (q + 1) * share]

    def swapped(t):
        return (4 - lax.rem(t, 4)) // 4

    def stage_of(s, t):
        if s >= 2:
            return mine[s], partner[s]
        odd = swapped(t)
        return (
            mine[s] + odd * (mine[1 - s] - mine[s]),
            partner[s] + odd * (partner[1 - s] - partner[s]),
        )

    def stage_copy(s, t):
        j = piece(t)
        half, to = stage_of(s, t)
        if s == 0:
            source = send.at[lax.rem(t, RING)]
        elif s == 1:
            source = recv[0].at[j, 1 - half]
        else:
            width = count >> (s + 1)
            source = recv[s - 1].at[j, pl.ds((1 - half) * width, width)]
        return pltpu.make_async_remote_copy(
            source,
            recv[s].at[j],
            stage_send.at[s, j],
            stage_recv.at[s, j],
            device_id=(p, to),
            device_id_type=MESH,
        )

    def send_first(t):
        j = piece(t)
        slot = lax.rem(t, RING)

        @pl.when((j == 0) & (p == 2))
        def _():
            turn(0, False)

        @pl.when((j == HALF - PER) & (c == 0))
        def _():
            turn(1, False)

        @pl.when(j == by_device(p, (HALF, HALF + RELAY, PIECES, HALF)))
        def _():
            turn(2, False)

        @pl.when(t >= RING)
        def _():
            stage_copy(0, t - RING).wait_send()

        rows_wait(j, rhs.at[j])
        odd = swapped(t)
        sel = jnp.where(j < HALF - PER, 0, jnp.where(j < HALF, 1 - c, 2))
        product = dot(lhs[sel].reshape(D, 2 * M), rhs[j])
        for high in range(2):
            for low in range(2):
                bit = (1 - odd) * high + odd * low
                part = (1 - odd) * low + odd * high
                keeps = 1 - (bit - mine_first(odd)) * (bit - mine_first(odd))
                rows = (2 * high + low) * (D // 4)
                whole[2 * keeps + part] = product[rows : rows + D // 4].reshape(quarter, share, PIECE)
        send[slot] = whole[:2].astype(BF16)
        keep[slot] = whole[2:]
        stage_copy(0, t).start()

    def mine_first(odd):
        return mine[0] + odd * (mine[1] - mine[0])

    def store_out(j, values):
        @pl.when(j < HALF)
        def _():
            first_ref[:, pl.ds(pl.multiple_of(j * PIECE, PIECE), PIECE)] = values

        @pl.when(j >= HALF)
        def _():
            turned = jnp.transpose(values)

            @pl.when(p == 2)
            def _():
                relay[j - HALF] = turned

            @pl.when(p != 2)
            def _():
                second_ref[pl.ds(pl.multiple_of((j - HALF) * PIECE, PIECE), PIECE)] = turned

    def take(s, t):
        j = piece(t)
        stage_copy(s, t).wait_recv()
        half, _ = stage_of(s, t)
        if s == 0:
            kept = keep[lax.rem(t, RING)]
        elif s == 1:
            kept = recv[0][j, half].astype(F32)
        else:
            width = count >> (s + 1)
            kept = recv[s - 1][j, pl.ds(half * width, width)].astype(F32)
        total = kept + recv[s][j].astype(F32)
        if s == bits - 1:
            store_out(j, total[0])
        else:
            recv[s][j] = total.astype(BF16)
            stage_copy(s + 1, t).start()

    def piece(t):
        return by_device(
            p,
            (
                t,
                jnp.where(t < HALF, t, t + RELAY),
                jnp.where(t < RELAY, t + HALF, t - RELAY),
                t,
            ),
        )

    @pl.when(p == 2)
    def _():
        turn(2, True)

    @pl.when(p != 2)
    def _():
        turn(0, False)

    lax.fori_loop(0, AHEAD, lambda t, _: (send_first(t), 0)[1], 0)
    issue(False)

    for index in range(2):

        @pl.when(p == index)
        def _(index=index):
            merged_in.wait()
            token_own(index).start()
            for target in range(4):
                if target != index:
                    token_copy(index, target, target).start()

    def vec_copy(s):
        width = count >> (s + 1)
        held = vec_own if s == 0 else vec_recv[s - 1]
        return pltpu.make_async_remote_copy(
            held.at[pl.ds((1 - mine[s]) * width, width)],
            vec_recv[s],
            vec_send_sem.at[s],
            vec_recv_sem.at[s],
            device_id=(p, partner[s]),
            device_id_type=MESH,
        )

    def vec_start():
        rows_wait(LEFT + 3, vec_in)
        both = jnp.concatenate([vec_in[0] + vec_in[1], jnp.zeros((112, D), F32)], 0)
        per = max(1, 128 // share)
        for block in range(D // 128):
            flipped = jnp.transpose(both[:, block * 128 : (block + 1) * 128])
            if share >= 128:
                at = bit_reversed(block * 128 // share, bits)
                inside = block * 128 % share
                vec_own[at, inside : inside + 128] = flipped
            else:
                for q in range(per):
                    at = bit_reversed(block * per + q, bits)
                    vec_own[at] = flipped[q * share : (q + 1) * share]
        vec_copy(0).start()

    def vec_step(s):
        width = count >> (s + 1)
        vec_copy(s).wait_recv()
        held = vec_own if s == 0 else vec_recv[s - 1]
        total = held[pl.ds(mine[s] * width, width)] + vec_recv[s][...]
        if s == bits - 1:
            vecs_ref[...] = total[0]
        else:
            vec_recv[s][...] = total
            vec_copy(s + 1).start()

    def table_copy(s):
        to = (pair, w) if s == 0 else (p, partner[s - 1])
        return pltpu.make_async_remote_copy(
            table.at[s],
            table_recv.at[s],
            table_send_sem.at[s],
            table_recv_sem.at[s],
            device_id=to,
            device_id_type=MESH,
        )

    def table_start():
        pltpu.make_async_copy(i.table, score, const_sem.at[0]).wait()
        pltpu.make_async_copy(i.inner, inner, const_sem.at[1]).wait()
        pltpu.make_async_copy(i.outer, outer, const_sem.at[2]).wait()
        by_row = None
        for ci in range(WIN):
            rows = jnp.concatenate(
                [score[pl.ds(ri * WIN + ci, HEADS, stride=ROWS), :] for ri in range(WIN)], 0
            )
            term = split_dot(rows, inner[ci])
            by_row = term if by_row is None else by_row + term
        total = None
        for ri in range(WIN):
            term = split_dot(by_row[ri * HEADS : (ri + 1) * HEADS], outer[ri])
            total = term if total is None else total + term
        table[0] = total
        table_copy(0).start()

    def table_cross():
        x = p // 2
        return pltpu.make_async_remote_copy(
            table.at[bits + 1],
            tables_ref.at[x],
            table_send_sem.at[bits + 1],
            table_recv_sem.at[bits + 1],
            device_id=(across, w),
            device_id_type=MESH,
        )

    def table_step(s):
        table_copy(s).wait_recv()
        table[s + 1] = table[s] + table_recv[s]
        if s < bits:
            table_copy(s + 1).start()
        else:
            tables_ref[p // 2] = table[s + 1]

            @pl.when(jnp.logical_not(upper))
            def _():
                table_cross().start()

    def relay_copy(k):
        return pltpu.make_async_remote_copy(
            relay.at[k],
            second_ref.at[k * PIECE : (k + 1) * PIECE],
            relay_send.at[k],
            relay_recv.at[k],
            device_id=(1, w),
            device_id_type=MESH,
        )

    def clear(j, carry):
        second_ref[pl.ds(pl.multiple_of(j * PIECE, PIECE), PIECE)] = jnp.zeros((PIECE, share), F32)
        return carry

    lax.fori_loop(by_device(p, (HALF // 2, HALF, 0, HALF)), HALF, clear, 0)

    def sent_by(s):
        return pieces - 1 + LAG * (bits - 1 - s) - 3

    def body(t, carry):
        for s in range(bits):
            at = t - LAG * s

            @pl.when((at >= 0) & (at < pieces))
            def _(s=s, at=at):
                take(s, at)
                if s == 0:

                    @pl.when(t + AHEAD < pieces)
                    def _():
                        send_first(t + AHEAD)

        for s in range(1, bits):
            past = t - LAG * s - 3

            @pl.when((past >= 0) & (past < pieces))
            def _(s=s, past=past):
                stage_copy(s, past).wait_send()

        pl.when(t == 2)(vec_start)
        pl.when(t == 4)(table_start)
        for s in range(bits):

            @pl.when(t == 2 * s + 4)
            def _(s=s):
                vec_step(s)

        for s in range(bits + 1):

            @pl.when(t == 2 * s + 6)
            def _(s=s):
                table_step(s)

        @pl.when(upper & (t == RELAY + LAG * (bits - 1)))
        def _():
            pl.semaphore_wait(ready, 2)
            table_cross().start()

            @pl.when(p == 2)
            def _():
                for k in range(RELAY):
                    relay_copy(k).start()

        return carry

    lax.fori_loop(0, pieces + LAG * (bits - 1), body, 0)

    def drain(t, carry):
        @pl.when(t >= pieces - RING)
        def _():
            stage_copy(0, t).wait_send()

        for s in range(1, bits):

            @pl.when(t > sent_by(s))
            def _(s=s):
                stage_copy(s, t).wait_send()

        return carry

    lax.fori_loop(pieces - RING, pieces, drain, 0)
    for s in range(bits):
        vec_copy(s).wait_send()
    for s in range(bits + 1):
        table_copy(s).wait_send()
    table_cross().wait()

    for index in range(4):

        @pl.when(p == index)
        def _(index=index):
            if index < 2:
                token_own(index).wait()
                for target in range(4):
                    if target != index:
                        token_copy(index, target, target).wait_send()
            for source in range(2):
                if source != index:
                    token_copy(source, index, source).wait_recv()
            if index == 2:
                for k in range(RELAY):
                    relay_copy(k).wait_send()
            if index == 1:
                for k in range(RELAY):
                    relay_copy(k).wait_recv()


def reduce_gradients(made, count):
    bits = count.bit_length() - 1
    share = D // count
    anywhere = pl.BlockSpec(memory_space=pl.ANY)
    in_vmem = pl.BlockSpec(memory_space=pltpu.VMEM)
    inner, outer = offset_blocks()
    flat = (HEADS * ROWS, 128)
    operands = {name: made[name] for name in made if name not in ("tokens", "outs")}
    operands["unroll"] = jnp.asarray(unroll_matrix(), BF16)
    operands["inner"] = jnp.asarray(inner, BF16)
    operands["outer"] = jnp.asarray(outer, BF16)
    merged = made["merged"]
    dma = pltpu.SemaphoreType.DMA
    halves = [(2, count // 4)] + [(count >> (s + 1),) for s in range(1, bits)]
    return pl.pallas_call(
        functools.partial(reduce_kernel, bits, tuple(operands)),
        in_specs=[anywhere] * len(operands),
        out_specs=[in_vmem] * 3 + [anywhere] + [in_vmem],
        out_shape=[
            shape_of((share, FF), F32),
            shape_of((FF, share), F32),
            shape_of((share, 128), F32),
            shape_of((2,) + merged.shape[1:], BF16),
            shape_of((2, HEADS, OFFSETS), F32),
        ],
        scratch_shapes=[
            pltpu.VMEM((3, 2 * M, D), BF16),
            pltpu.VMEM((3, 4, count // 4, share, 2 * M), BF16),
            pltpu.VMEM((PIECES, 2 * M, PIECE), BF16),
            pltpu.VMEM((2, 16, D), F32),
            pltpu.VMEM((count, share, 128), F32),
            pltpu.VMEM((RELAY, PIECE, share), F32),
            pltpu.VMEM(flat, F32),
            pltpu.VMEM((2 * M, 2 * M), BF16),
            pltpu.VMEM(inner.shape, BF16),
            pltpu.VMEM(outer.shape, BF16),
            pltpu.VMEM((bits + 2, HEADS, OFFSETS), F32),
            pltpu.VMEM((bits + 1, HEADS, OFFSETS), F32),
            pltpu.VMEM((RING, 2, count // 4, share, PIECE), BF16),
            pltpu.VMEM((RING, 2, count // 4, share, PIECE), F32),
            pltpu.VMEM((4, count // 4, share, PIECE), F32),
            pltpu.VMEM(merged.shape, BF16),
            *[pltpu.VMEM((PIECES,) + half + (share, PIECE), BF16) for half in halves],
            *[pltpu.VMEM((count >> (s + 1), share, 128), F32) for s in range(bits)],
            dma((SLOTS,)),
            dma((bits, PIECES)),
            dma((bits, PIECES)),
            dma((bits,)),
            dma((bits,)),
            dma((bits + 2,)),
            dma((bits + 2,)),
            dma((5,)),
            dma,
            dma((4,)),
            dma((2,)),
            dma((RELAY,)),
            dma((RELAY,)),
            pltpu.SemaphoreType.REGULAR,
        ],
        compiler_params=pltpu.CompilerParams(
            collective_id=0, has_side_effects=True, vmem_limit_bytes=60 * 1024 * 1024
        ),
        name="reduce_gradients",
    )(*operands.values())


def finish_kernel(
    first_in, second_in, vecs_in, outs_in, parts_in, tables_in, order_in, split_in,
    output_ref, tokens_ref, first_out, second_out, gains_ref, biases_ref, tables_out,
    vecs_ref, outs_ref, parts_ref, tables_ref, order_ref, split_ref, first_ref, second_ref, sems,
):
    copies = [
        pltpu.make_async_copy(source, target, sems.at[k])
        for k, (source, target) in enumerate(
            (
                (parts_in, parts_ref),
                (split_in, split_ref),
                (outs_in, outs_ref),
                (order_in, order_ref),
                (tables_in, tables_ref),
                (vecs_in, vecs_ref),
                (first_in, first_ref),
                (second_in, second_ref),
            )
        )
    ]
    for copy in copies:
        copy.start()
    for copy in copies[:6]:
        copy.wait()
    on = []
    for copy, source, target in ((copies[6], first_ref, first_out), (copies[7], second_ref, second_out)):
        copy.wait()
        on.append(pltpu.make_async_copy(source, target, sems.at[8 + len(on)]))
        on[-1].start()
    tables_out[...] = tables_ref[:, :, : SPAN * SPAN]
    vecs = jnp.transpose(vecs_ref[...])
    for row in range(3):
        gains_ref[row] = vecs[row : row + 1]
    for row in range(6):
        biases_ref[row] = vecs[3 + row : 4 + row]
    channels = tokens_ref.shape[-1]
    for crop in range(WINS):
        windows = []
        for half in range(2):
            window = 2 * crop + half
            core, k = window // WINS, window % WINS
            windows.append((core, slice(k * ROWS, (k + 1) * ROWS)))
        rolled = jnp.concatenate([outs_ref[core, rows] for core, rows in windows], 0)
        output_ref[crop] = dot(order_ref[...], rolled).astype(BF16)
        total = None
        for half, (core, rows) in enumerate(windows):
            cells = jnp.concatenate(
                [parts_ref[core, rows, t * channels : (t + 1) * channels] for t in range(4)], 0
            )
            term = dot(split_ref[half], cells)
            total = term if total is None else total + term
        tokens_ref[crop] = total
    for copy in on:
        copy.wait()


def finish(out_parts, first_part, second_part, vec_part, token_parts, table_parts):
    share = first_part.shape[0]
    split = np.transpose(merge_matrix(), (0, 2, 1))
    channels = token_parts.shape[-1] // 4
    return pl.pallas_call(
        finish_kernel,
        in_specs=[ANYWHERE] * 8,
        out_specs=[IN_VMEM] * 2 + [ANYWHERE] * 2 + [IN_VMEM] * 3,
        out_shape=[
            shape_of((WINS, TOK, out_parts.shape[-1]), BF16),
            shape_of((WINS, 4 * TOK, channels), F32),
            shape_of(first_part.shape, F32),
            shape_of(second_part.shape, F32),
            shape_of((3, 1, share), F32),
            shape_of((6, 1, share), F32),
            shape_of((2, HEADS, SPAN * SPAN), F32),
        ],
        scratch_shapes=[
            pltpu.VMEM(vec_part.shape, F32),
            pltpu.VMEM(out_parts.shape, BF16),
            pltpu.VMEM(token_parts.shape, BF16),
            pltpu.VMEM(table_parts.shape, F32),
            pltpu.VMEM((TOK, 2 * ROWS), BF16),
            pltpu.VMEM(split.shape, BF16),
            pltpu.VMEM(first_part.shape, F32),
            pltpu.VMEM(second_part.shape, F32),
            DMA((10,)),
        ],
        compiler_params=pltpu.CompilerParams(vmem_limit_bytes=61 * 1024 * 1024),
        name="finish",
    )(
        first_part,
        second_part,
        vec_part,
        out_parts,
        token_parts,
        table_parts,
        jnp.asarray(output_matrix(), BF16),
        jnp.asarray(split, BF16),
    )


def padded_row(token):
    return (token // AREA) * ROWS + token % AREA


def rolled_source():
    cells = np.arange(TOK)
    rows, columns = cells // GRID_W, cells % GRID_W
    return ((rows + WIN // 2) % GRID_H) * GRID_W + (columns + WIN // 2) % GRID_W


def hop_matrix(inverse):
    source = rolled_source()
    if inverse:
        source = np.argsort(source)
    result = np.zeros((2, M, (WINS + 1) * ROWS), np.float32)
    for core in range(2):
        for k in range(WINS):
            window = WINS * core + k
            crop, part = window // 2, window % 2
            for t in range(AREA):
                token = source[part * AREA + t]
                taken = crop * 2 + token // AREA
                slot = taken - WINS * core
                if not 0 <= slot < WINS:
                    slot = WINS
                result[core, k * ROWS + t, slot * ROWS + token % AREA] = 1.0
    return result


def cotangent_matrix():
    source = rolled_source()
    result = np.zeros((2, M, 4 * 256), np.float32)
    for core in range(2):
        for k in range(WINS):
            window = WINS * core + k
            crop, part = window // 2, window % 2
            for t in range(AREA):
                result[core, k * ROWS + t, crop * 256 + source[part * AREA + t]] = 1.0
    return result


def output_matrix():
    source = rolled_source()
    result = np.zeros((TOK, 2 * ROWS), np.float32)
    for t in range(TOK):
        result[source[t], padded_row(t)] = 1.0
    return result


def offset_matrices():
    span = 2 * WIN - 1
    inner = np.zeros((WIN, 128, WIN, span), np.float32)
    outer = np.zeros((WIN, WIN, span, span, span), np.float32)
    for ci in range(WIN):
        for j in range(AREA):
            inner[ci, j, j // WIN, ci - j % WIN + WIN - 1] = 1.0
    for ri in range(WIN):
        for rj in range(WIN):
            for dc in range(span):
                outer[ri, rj, dc, ri - rj + WIN - 1, dc] = 1.0
    return (
        inner.reshape(WIN * 128, WIN * span),
        outer.reshape(WIN * WIN * span, span * span),
    )


def offset_blocks():
    inner, outer = offset_matrices()
    inner = np.pad(inner.reshape(WIN, 128, WIN * SPAN), ((0, 0), (0, 0), (0, INNER - WIN * SPAN)))
    outer = np.pad(
        outer.reshape(WIN, WIN * SPAN, SPAN * SPAN),
        ((0, 0), (0, INNER - WIN * SPAN), (0, OFFSETS - SPAN * SPAN)),
    )
    return inner, outer


def offset_pack():
    inner, outer = offset_blocks()
    result = np.zeros((WIN // 2, INNER, D), np.float32)
    for k in range(WIN):
        half = k % 2
        result[k // 2, :, half * OFFSETS : (half + 1) * OFFSETS] = outer[k]
        result[k // 2, half * 128 : (half + 1) * 128, 2 * OFFSETS :] = inner[k]
    return result


def unroll_matrix():
    source = rolled_source()
    result = np.zeros((2 * M, 2 * M), np.float32)
    for crop in range(WINS):
        for t in range(TOK):
            start = crop * 2 * ROWS
            result[start + padded_row(t), start + padded_row(source[t])] = 1.0
    return result


def merge_matrix():
    result = np.zeros((2, 4, ROWS, 2 * GRID_W, 2 * GRID_H), np.float32)
    for half in range(2):
        for part in range(4):
            right, down = part // 2, part % 2
            for t in range(AREA):
                result[half, part, t, 2 * (t % WIN) + right, 2 * (half * WIN + t // WIN) + down] = 1.0
    return result.reshape(2, 4 * ROWS, 4 * TOK)


def region_masks():
    cells = np.arange(TOK)
    rows_at, cols_at = cells // GRID_W, cells % GRID_W
    row_band = (rows_at >= GRID_H - WIN).astype(int) + (rows_at >= GRID_H - WIN // 2)
    col_band = (cols_at >= GRID_W - WIN).astype(int) + (cols_at >= GRID_W - WIN // 2)
    rolled = (row_band * 3 + col_band).reshape(2, AREA)
    result = np.zeros((4, ROWS, 128), np.float32)
    for part in range(2):
        result[part, :AREA, :AREA] = 1.0
        result[2 + part, :AREA, :AREA] = rolled[part][:, None] == rolled[part][None, :]
    return result


def key_matrix():
    source = rolled_source()
    result = np.zeros((TOK, 4, 128), np.float32)
    for part in range(2):
        for t in range(AREA):
            result[part * AREA + t, part, t] = 1.0
            result[source[part * AREA + t], 2 + part, t] = 1.0
    return result.reshape(TOK, 4 * 128)


def local(page_tokens, blank, cotangent, first, second, gains, biases, tables):
    count = lax.axis_size("wide")
    made = forward_backward(
        page_tokens, blank, cotangent, first[0], second[0], gains, biases, tables
    )
    output, token_grad, first_grad, second_grad, gain_grad, bias_grad, table_grad = finish(
        made["outs"], *reduce_gradients(made, count)
    )
    crops, rows, columns, channels = page_tokens.shape
    token_grad = token_grad.reshape(crops, columns, rows, channels // 4)
    return (
        output,
        jnp.transpose(token_grad, (0, 2, 1, 3)),
        first_grad[None],
        second_grad[None],
        jnp.transpose(gain_grad, (1, 0, 2)),
        jnp.transpose(bias_grad, (1, 0, 2)),
        table_grad,
    )


def solution(mesh):
    placed = (
        P("wide", None, None, None),
        P("wide", None),
        P("wide", None, None),
        P("pipe", None, None),
        P("pipe", None, None),
        P("pipe", None, None),
        P("pipe", None, None),
        P(),
    )
    return jax.shard_map(
        local,
        mesh=mesh,
        in_specs=placed,
        out_specs=(
            P("wide", None, "pipe"),
            P("wide", None, None, "pipe"),
            P("pipe", "wide", None),
            P("pipe", None, "wide"),
            P("pipe", None, "wide"),
            P("pipe", None, "wide"),
            P(),
        ),
        check_vma=False,
    )
```

```python
import functools
from itertools import zip_longest

import jax
import jax.numpy as jnp
import numpy as np
from jax import lax
from jax.experimental import pallas as pl
from jax.experimental.pallas import tpu as pltpu
from jax.sharding import PartitionSpec as P

HEADS = 32
WIN = 10
GRID_H = 20
GRID_W = 10
AREA = WIN * WIN
TOK = GRID_H * GRID_W
ROWS = 112
WINS = 3
M = ROWS * WINS
D = 1024
FF = 4096
CHUNK = 512
EPSILON = 1e-05
NEGATIVE = -1000000000.0
SCALE = 32 ** (-0.5)
MESH = pl.DeviceIdType.MESH
F32 = jnp.float32
BF16 = jnp.bfloat16


def shape_of(dims, kind):
    return jax.ShapeDtypeStruct(dims, kind)


def dot(left, right):
    return jnp.dot(left, right, preferred_element_type=F32)


def dot_nt(left, right):
    return lax.dot_general(left, right, (((1,), (1,)), ((), ())), preferred_element_type=F32)


def dot_tn(left, right):
    return lax.dot_general(left, right, (((0,), (0,)), ((), ())), preferred_element_type=F32)


def norm_parts(values):
    average = jnp.mean(values, -1, keepdims=True)
    centered = values - average
    inv_std = lax.rsqrt(jnp.mean(centered * centered, -1, keepdims=True) + EPSILON)
    return centered * inv_std, inv_std


def norm_backward(grad_out, values, gain):
    unit, inv_std = norm_parts(values)
    scaled = grad_out * gain
    grad_in = inv_std * (
        scaled
        - jnp.mean(scaled, -1, keepdims=True)
        - unit * jnp.mean(scaled * unit, -1, keepdims=True)
    )
    return (
        grad_in,
        jnp.sum(grad_out * unit, 0, keepdims=True),
        jnp.sum(grad_out, 0, keepdims=True),
    )


def split_dot(left, right, product=dot):
    high = left.astype(BF16)
    low = (left - high.astype(F32)).astype(BF16)
    return product(high, right) + product(low, right)


ANYWHERE = pl.BlockSpec(memory_space=pl.ANY)
IN_VMEM = pl.BlockSpec(memory_space=pltpu.VMEM)
DMA = pltpu.SemaphoreType.DMA
SPAN = 2 * WIN - 1
INNER = 256
OFFSETS = 384
GROUP = 256
GROUP_HEADS = GROUP // 32
STEPS = D // GROUP
CHUNKS = FF // CHUNK
PIECE = 256
HALF = FF // PIECE
PER = D // PIECE
RELAY = 12


class Refs:
    def __init__(self, names, refs):
        self.__dict__.update(zip(names, refs))


def lanes_at(start, size):
    return pl.ds(pl.multiple_of(start, 128), size)


def lane_masks():
    lanes = lax.broadcasted_iota(jnp.int32, (1, 128), 1)
    return [
        jnp.where((lanes >= 32 * h) & (lanes < 32 * h + 32), 1.0, 0.0).astype(BF16)
        for h in range(4)
    ]


def stacked(values, masks, rows):
    if rows > values.shape[0]:
        values = jnp.concatenate(
            [values, jnp.zeros((rows - values.shape[0], values.shape[1]), values.dtype)], 0
        )
    return jnp.concatenate([values * mask for mask in masks], 0)


def beside_ones(values, masks):
    ones = jnp.concatenate([jnp.broadcast_to(mask, (128, 128)) for mask in masks], 0)
    return jnp.concatenate([stacked(values, masks, 128), ones], 1)


def attention_forward(s, vec, weights):
    unit, _ = norm_parts(s.x[...])
    s.normed[...] = (unit * vec[0:1] + vec[3:4]).astype(BF16)
    s.acc[...] = jnp.zeros_like(s.acc)
    masks = lane_masks()

    def step(g, carry):
        weights(g)
        here = lanes_at(g * GROUP, GROUP)
        projected = dot(s.normed[...], s.w_qkv[g])
        query = (projected[:, :GROUP] + vec[4:5, here]).astype(BF16)
        key = projected[:, GROUP : 2 * GROUP].astype(BF16)
        value = (projected[:, 2 * GROUP :] + vec[5:6, here]).astype(BF16)
        for k, values in enumerate((query, key, value)):
            s.qkv[k, :, here] = values
        mixed = []
        for w in range(WINS):
            rows = slice(w * ROWS, (w + 1) * ROWS)
            allowed = s.mask[w] > 0.5
            parts = []
            for part in range(GROUP // 128):
                inside = slice(part * 128, (part + 1) * 128)
                lanes = lanes_at(g * GROUP + part * 128, 128)
                scores = dot_nt(query[rows, inside], stacked(key[rows, inside], masks, 128))
                found = []
                for h in range(4):
                    head = g * GROUP_HEADS + part * 4 + h
                    bias = s.rel[pl.ds(pl.multiple_of(head * ROWS, 8), ROWS)]
                    one = jnp.where(
                        allowed, scores[:, h * 128 : (h + 1) * 128] * SCALE + bias, NEGATIVE
                    )
                    exponent = jnp.exp(one - jnp.max(one, -1, keepdims=True)).astype(BF16)
                    s.exps[w, head] = exponent
                    found.append(exponent)
                sums = dot(jnp.concatenate(found, 1), beside_ones(value[rows, inside], masks))
                scale = 1.0 / sums[:, 128:]
                s.inverse[rows, lanes] = scale
                parts.append((sums[:, :128] * scale).astype(BF16))
            mixed.append(jnp.concatenate(parts, 1))
        mixed = jnp.concatenate(mixed, 0)
        s.mixed[:, here] = mixed
        s.acc[...] += dot(mixed, s.w_out[g])
        return carry

    lax.fori_loop(0, STEPS, step, 0)
    return s.x[...] + (s.acc[...] + vec[6:7])


def attention_backward(s, vec, right, vecs):
    masks = lane_masks()
    s.acc[...] = jnp.zeros_like(s.acc)

    def step(g, carry):
        here = lanes_at(g * GROUP, GROUP)
        mixed_grad = dot_nt(s.grad_a[...], s.w_out[g])
        scaled_grad = (mixed_grad * s.inverse[:, here]).astype(BF16)
        spread = (scaled_grad.astype(F32) * s.mixed[:, here].astype(F32)).astype(BF16)
        query, key, value = [s.qkv[k, :, here] for k in range(3)]
        made = []
        for w in range(WINS):
            rows = slice(w * ROWS, (w + 1) * ROWS)
            parts = []
            for part in range(GROUP // 128):
                inside = slice(part * 128, (part + 1) * 128)
                grad_here = scaled_grad[rows, inside]
                prob_grad = dot_nt(
                    jnp.concatenate([grad_here, -spread[rows, inside]], 1),
                    beside_ones(value[rows, inside], masks),
                )
                found = []
                draws = []
                for h in range(4):
                    head = g * GROUP_HEADS + part * 4 + h
                    exponent = s.exps[w, head]
                    score_grad = exponent.astype(F32) * prob_grad[:, h * 128 : (h + 1) * 128]
                    at = pl.ds(pl.multiple_of(head * ROWS, 8), ROWS)
                    if w == 0:
                        s.rel[at] = score_grad
                    else:
                        s.rel[at] += score_grad
                    found.append(exponent)
                    draws.append((score_grad * SCALE).astype(BF16))
                query_grad = dot(jnp.concatenate(draws, 1), stacked(key[rows, inside], masks, 128))
                key_grad = dot_tn(jnp.concatenate(draws, 0), stacked(query[rows, inside], masks, ROWS))
                value_grad = dot_tn(jnp.concatenate(found, 0), stacked(grad_here, masks, ROWS))
                parts.append([t[:ROWS].astype(BF16) for t in (query_grad, key_grad, value_grad)])
            made.append([jnp.concatenate([part[k] for part in parts], 1) for k in range(3)])
        made = [jnp.concatenate([window[k] for window in made], 0) for k in range(3)]
        for k in range(3):
            right[k, :, here] = made[k]
        s.acc[...] += dot_nt(jnp.concatenate(made, 1), s.w_qkv[g])
        return carry

    lax.fori_loop(0, STEPS, step, 0)
    grad_in, gain_grad, shift_grad = norm_backward(s.acc[...], s.x[...], vec[0:1])
    wide = s.grad_a[...].astype(F32)
    vecs[0:1] = gain_grad
    vecs[1:3] = jnp.zeros((2, D), F32)
    vecs[3:4] = shift_grad
    vecs[4:5] = jnp.sum(right[0].astype(F32), 0, keepdims=True)
    vecs[5:6] = jnp.sum(right[2].astype(F32), 0, keepdims=True)
    vecs[6:7] = jnp.sum(wide, 0, keepdims=True)
    vecs[7:16] = jnp.zeros((9, D), F32)
    return wide + grad_in


def gelu_parts(pre):
    cumulative = 0.5 * (1.0 + lax.erf(pre * 0.7071067811865476))
    density = jnp.exp(-0.5 * pre * pre) * 0.3989422804014327
    return (pre * cumulative).astype(BF16), (cumulative + pre * density).astype(BF16)


def mlp_forward(s, vec, weights):
    x = s.mid[...].astype(F32)
    unit, _ = norm_parts(x)
    s.normed[...] = (unit * vec[0:1] + vec[3:4]).astype(BF16)

    def product(j):
        weights(j)
        start = j % 2 * CHUNK
        bias = vec[4 + j // 2 : 5 + j // 2, start : start + CHUNK]
        s.pre[j % 2] = dot(s.normed[...], s.w1[j]) + bias

    def take(j):
        start = j % 2 * CHUNK
        term = dot(s.hidden[j // 2, :, start : start + CHUNK], s.w2[j])
        if j == 0:
            s.acc[...] = term
        else:
            s.acc[...] += term

    product(0)
    for j in range(CHUNKS):
        start = j % 2 * CHUNK
        if j + 1 < CHUNKS:
            product(j + 1)
        if j > 0:
            take(j - 1)
        values, slopes = gelu_parts(s.pre[j % 2])
        s.hidden[j // 2, :, start : start + CHUNK] = values
        s.slope[j // 2, :, start : start + CHUNK] = slopes
    take(CHUNKS - 1)
    return s.mid[...].astype(F32) + s.acc[...] + vec[8:9]


def mlp_backward(s, vec, vecs):
    def product(j):
        here = slice(j % 2 * CHUNK, (j % 2 + 1) * CHUNK)
        pre_grad = dot_nt(s.grad_m[...], s.w2[j]) * s.slope[j // 2, :, here].astype(F32)
        vecs[4 + j // 2 : 5 + j // 2, here] = jnp.sum(pre_grad, 0, keepdims=True)
        s.slope[j // 2, :, here] = pre_grad.astype(BF16)

    def take(j):
        here = slice(j % 2 * CHUNK, (j % 2 + 1) * CHUNK)
        term = dot_nt(s.slope[j // 2, :, here], s.w1[j])
        if j == 0:
            s.acc[...] = term
        else:
            s.acc[...] += term

    product(0)
    for j in range(CHUNKS):
        if j + 1 < CHUNKS:
            product(j + 1)
        take(j)
    grad_in, gain_grad, shift_grad = norm_backward(s.acc[...], s.mid[...].astype(F32), vec[0:1])
    wide = s.grad_m[...].astype(F32)
    vecs[0:1] = gain_grad
    vecs[1:3] = jnp.zeros((2, D), F32)
    vecs[3:4] = shift_grad
    vecs[8:9] = jnp.sum(wide, 0, keepdims=True)
    vecs[9:16] = jnp.zeros((7, D), F32)
    return wide + grad_in


def main_kernel(ins, outs, scratch, *refs):
    first = len(ins)
    second = first + len(outs)
    i, o, s = Refs(ins, refs[:first]), Refs(outs, refs[first:second]), Refs(scratch, refs[second:])
    p = lax.axis_index("pipe")
    w_at = lax.axis_index("wide")
    side, c = p // 2, lax.rem(p, 2)
    lower, upper = side == 0, side == 1
    pair = (p + 1 - 2 * c, w_at)
    across = (lax.rem(p + 2, 4), w_at)

    def local(source, target, sem):
        return pltpu.make_async_copy(source, target, sem)

    def remote(source, target, sent, got, to):
        return pltpu.make_async_remote_copy(
            source, target, sent, got, device_id=to, device_id_type=MESH
        )

    consts = [local(i.pack.at[k], s.hidden.at[k, :INNER], s.const_sem.at[k]) for k in range(4)]
    consts.append(local(i.pack.at[4], s.slope.at[0, :INNER], s.const_sem.at[4]))
    consts.append(local(i.roll.at[side, c], s.roll, s.const_sem.at[5]))
    picks = []
    for half in range(2):
        for source, target in (
            (i.pick.at[half, : 3 * ROWS], s.slope.at[1 + half]),
            (i.pick.at[half, 3 * ROWS :], s.slope.at[3, half * ROWS : (half + 1) * ROWS]),
        ):
            picks.append(local(source, target, s.pick_sem.at[len(picks)]))
    cot = local(i.cot.at[c], s.mixed, s.const_sem.at[6])

    def token_copy(k):
        return local(i.tokens.at[(c * WINS + k) // 2], s.tokens.at[k % 2], s.token_sem.at[k % 2])

    def cotangent_copy(k):
        return local(i.cotangent.at[k], s.cotangent, s.token_sem.at[0])

    for copy in consts:
        copy.start()

    @pl.when(lower)
    def _():
        token_copy(0).start()
        token_copy(1).start()
        for copy in picks:
            copy.start()

    @pl.when(upper)
    def _():
        cotangent_copy(0).start()
        cot.start()

    for row in range(3):
        s.vec[c, row : row + 1] = i.gains[row]
    for row in range(6):
        s.vec[c, 3 + row : 4 + row] = i.biases[row]
    s.vec[c, 9:16] = jnp.zeros((7, D), F32)
    barrier = pltpu.get_barrier_semaphore()
    for step in range(1, 4):
        pl.semaphore_signal(
            barrier, inc=1, device_id=(lax.rem(p + step, 4), w_at), device_id_type=MESH
        )
    beside = []
    for b in range(2):
        bit = lax.rem(w_at // (1 << b), 2)
        beside.append((pair[0], w_at + (1 << b) * (1 - 2 * bit)))
        pl.semaphore_signal(barrier, inc=1, device_id=beside[b], device_id_type=MESH)
    pl.semaphore_wait(barrier, 5)
    vec_copy = remote(s.vec.at[c], s.vec.at[c], s.vec_sem.at[0], s.vec_sem.at[1], pair)
    vec_copy.start()

    attention_parts = []
    for g in range(STEPS):
        for k in range(3):
            start = k * D + g * GROUP
            attention_parts.append(
                (i.first.at[:, start : start + GROUP], s.w_qkv.at[g, :, k * GROUP : (k + 1) * GROUP])
            )
        attention_parts.append((i.first.at[g * GROUP : (g + 1) * GROUP, 3 * D :], s.w_out.at[g]))
    mlp_parts = []
    for j in range(CHUNKS):
        here = slice(j * CHUNK, (j + 1) * CHUNK)
        mlp_parts.append((i.first.at[:, here], s.w1.at[j]))
        mlp_parts.append((i.second.at[here], s.w2.at[j]))
    merge_parts = []
    for g in range(STEPS):
        here = slice(g * GROUP, (g + 1) * GROUP)
        merge_parts.append((i.second.at[: 2 * D, here], s.w_merge.at[:, here]))

    def load(parts, got):
        for k, (source, target) in enumerate(parts):
            local(source, target, got.at[k]).start()

    def gifts(parts, got):
        found = []
        for k, (source, target) in enumerate(parts):
            over = k % 4 == 3 if parts is attention_parts else k % 8 in (5, 7)
            to = beside[k // 8] if over else pair
            found.append(remote(source, target, s.give_sem.at[k], got.at[k], to))
        return found

    def give(parts, got):
        for copy in gifts(parts, got):
            copy.start()

    def merge_gifts():
        return [
            remote(source, target, s.merge_sem.at[1, k], s.merge_sem.at[0, k], pair)
            for k, (source, target) in enumerate(merge_parts)
        ]

    mine = pl.ds(pl.multiple_of(c * M, 16), M)

    class Delivery:
        def __init__(self, section, item, source, target):
            self.here = c == section
            self.ends = source, target
            self.sems = s.give_out.at[section, item], s.give_in.at[section, item]

        def local(self):
            return local(*self.ends, self.sems[0])

        def remote(self):
            return remote(*self.ends, *self.sems, pair)

        def start(self):
            pl.when(self.here)(lambda: self.local().start())
            pl.when(jnp.logical_not(self.here))(lambda: self.remote().start())

        def wait(self):
            pl.when(self.here)(lambda: self.local().wait())
            pl.when(jnp.logical_not(self.here))(lambda: self.remote().wait_send())

        def wait_recv(self):
            pl.when(self.here)(lambda: self.remote().wait_recv())

    def deliver_rows(section, item, source):
        target = (o.left, o.left_b, o.right_b)[item]
        return Delivery(section, item, source, target.at[mine])

    def deliver_vecs(section, source):
        return Delivery(section, 3, source, o.vecs.at[c])

    def deliver_right(section, source, where=range(4)):
        return [Delivery(section, 4 + k, source.at[k], o.right.at[k, mine]) for k in where]

    def deliver_hidden(section, source, where):
        return [Delivery(section, 8 + k, source.at[k], o.hidden.at[k, mine]) for k in where]

    def start_all(copies):
        for copy in copies:
            copy.start()

    def wait_all(copies):
        for copy in copies:
            copy.wait()

    @pl.when(c == 0)
    def _():
        @pl.when(lower)
        def _():
            start_all(merge_gifts())
            for k, (source, target) in enumerate(merge_parts):
                local(source, target, s.merge_sem.at[0, k]).start()

        @pl.when(upper)
        def _():
            give(attention_parts, s.attention_sem)

        load(attention_parts, s.attention_sem)

    @pl.when(c == 1)
    def _():
        give(mlp_parts, s.mlp_sem)
        load(mlp_parts, s.mlp_sem)

    def arrived(target, sem):
        local(target, target, sem).wait()

    def attention_weights(g):
        for k in range(3):
            arrived(s.w_qkv.at[g, :, k * GROUP : (k + 1) * GROUP], s.attention_sem.at[4 * g + k])
        arrived(s.w_out.at[g], s.attention_sem.at[4 * g + 3])

    def mlp_weights(j):
        arrived(s.w1.at[j], s.mlp_sem.at[2 * j])
        arrived(s.w2.at[j], s.mlp_sem.at[2 * j + 1])

    for copy in consts:
        copy.wait()

    def outer(ri):
        block = s.hidden.at[ri // 2] if ri < 8 else s.slope.at[0]
        return block[:INNER, ri % 2 * OFFSETS : (ri % 2 + 1) * OFFSETS]

    def inner(ci):
        block = s.hidden.at[ci // 2] if ci < 8 else s.slope.at[0]
        return block[ci % 2 * 128 : (ci % 2 + 1) * 128, 2 * OFFSETS :]

    s.table[...] = jnp.zeros_like(s.table)
    s.table[:, : SPAN * SPAN] = jnp.where(lower, i.tables[0], i.tables[1])
    table = s.table[...]
    wide = jnp.concatenate([split_dot(table, outer(ri), dot_nt) for ri in range(WIN)], 0)
    s.rel[...] = jnp.zeros_like(s.rel)
    for ci in range(WIN):
        rows = split_dot(wide, inner(ci), dot_nt)
        for ri in range(WIN):
            s.rel[pl.ds(ri * WIN + ci, HEADS, stride=ROWS), :] = rows[ri * HEADS : (ri + 1) * HEADS]

    @pl.when(lower & (c == 0))
    def _():
        give(attention_parts, s.attention_sem)

    closed = dot(i.blank[...].astype(F32).astype(BF16), i.keys[...])
    at_row = lax.broadcasted_iota(jnp.int32, (ROWS, 128), 0)
    at_lane = lax.broadcasted_iota(jnp.int32, (ROWS, 128), 1)
    own = jnp.where(at_row == at_lane, 1.0, 0.0)
    for k in range(WINS):
        found = []
        for rolled in range(2):
            for core in range(2):
                crop, part = (WINS * core + k) // 2, (WINS * core + k) % 2
                start = (2 * rolled + part) * 128
                found.append((closed[crop : crop + 1, start : start + 128], i.regions[2 * rolled + part]))
        near = [[jnp.where(c == 0, found[2 * t][u], found[2 * t + 1][u]) for u in range(2)] for t in range(2)]
        row, region = [jnp.where(lower, near[0][u], near[1][u]) for u in range(2)]
        s.mask[k] = region * jnp.maximum(1.0 - row, own)

    @pl.when(upper)
    def _():
        cot.wait()
        for crop in range(WINS):
            cotangent_copy(crop).wait()
            term = dot(s.mixed[:, crop * 256 : crop * 256 + TOK], s.cotangent[...])
            if crop == 0:
                s.acc[...] = term
            else:
                s.acc[...] += term
            if crop + 1 < WINS:
                cotangent_copy(crop + 1).start()
        s.grad_m[...] = s.acc[...].astype(BF16)
        deliver_rows(1, 2, s.grad_m).start()

    arrived(s.vec.at[1 - c], s.vec_sem.at[1])
    vec_a, vec_m = s.vec.at[0], s.vec.at[1]

    def merge_saved():
        return [local(s.hidden.at[k], o.tokens.at[k], s.save_sem.at[k]) for k in range(4)]

    @pl.when(lower)
    def _():
        for copy in picks:
            copy.wait()
        gain = jnp.concatenate([vec_a[1:2], vec_a[2:3]], 1)
        shift = jnp.concatenate([vec_a[7:8], vec_a[8:9]], 1)
        area = 4 * TOK
        for k in range(WINS):
            rows = slice(k * ROWS, (k + 1) * ROWS)
            half = lax.rem(c + k, 2)
            token_copy(k).wait()
            picked = dot(s.slope[1 + half, :, :area], s.tokens[k % 2])
            last = s.slope[3, pl.ds(pl.multiple_of(half * ROWS, 16), ROWS), :area]
            picked = [picked[t * ROWS : (t + 1) * ROWS] for t in range(3)] + [dot(last, s.tokens[k % 2])]
            if k + 2 < WINS:
                token_copy(k + 2).start()
            merged = jnp.concatenate(picked, 1)
            s.hidden[2, rows] = merged[:, :D].astype(BF16)
            s.hidden[3, rows] = merged[:, D:].astype(BF16)
            unit, _ = norm_parts(merged)
            normed = (unit * gain + shift).astype(BF16)
            s.hidden[0, rows] = normed[:, :D]
            s.hidden[1, rows] = normed[:, D:]
        start_all(merge_saved())

        for g in range(STEPS):
            here = slice(g * GROUP, (g + 1) * GROUP)
            arrived(s.w_merge.at[:, here], s.merge_sem.at[0, g])
            s.x[:, here] = dot(s.hidden[0], s.w_merge[:D, here]) + dot(s.hidden[1], s.w_merge[D:, here])

    shared = pl.ds(pl.multiple_of((1 - c) * (WINS - 1) * ROWS, 16), ROWS)
    shared_copy = remote(
        s.hop_out.at[shared], s.hop_out.at[M:], s.hop_sem.at[0], s.hop_sem.at[1], pair
    )

    early = pl.ds(pl.multiple_of(c * ROWS, 16), 2 * ROWS)
    late = pl.ds(pl.multiple_of((1 - c) * 2 * ROWS, 16), ROWS)

    def hop_copies(target):
        return [
            remote(s.grad_a.at[rows], target.at[rows], s.hop_sem.at[2 * k], s.hop_sem.at[2 * k + 1], across)
            for k, rows in ((1, early), (2, late))
        ]

    def hop(target):
        first, last = hop_copies(target)
        shared_copy.start()
        s.grad_a[early] = dot(s.roll[early, :M], s.hop_out[:M]).astype(BF16)
        first.start()
        near = dot(s.roll[late, :M], s.hop_out[:M])
        shared_copy.wait_recv()
        s.grad_a[late] = (near + dot(s.roll[late, M:], s.hop_out[M:])).astype(BF16)
        last.start()
        shared_copy.wait_send()

    @pl.when(upper)
    def _():
        for copy in hop_copies(s.grad_a):
            copy.wait_recv()
        s.x[...] = s.grad_a[...].astype(F32)

    s.mid[...] = attention_forward(s, vec_a, attention_weights).astype(BF16)
    normed_out = deliver_rows(0, 0, s.normed)
    mixed_out = deliver_rows(0, 1, s.mixed)

    @pl.when(lower)
    def _():
        aside = local(s.normed, o.tokens.at[4], s.save_sem.at[4])
        aside.start()
        wait_all(merge_saved())
        aside.wait()

    @pl.when(upper)
    def _():
        normed_out.start()
        normed_out.wait()

    s.hop_out[:M] = mlp_forward(s, vec_m, mlp_weights).astype(BF16)
    mixed_out.start()
    normed_out = deliver_rows(1, 0, s.normed)

    over = range(RELAY // PER)

    def hidden_over(k, core):
        rows = pl.ds(pl.multiple_of(core * M, 16), M)
        return remote(
            s.hidden.at[k], o.hidden.at[k, rows], s.over_sem.at[k], s.over_in.at[core, k], (2, w_at)
        )

    def output_copy(owner):
        wide = D // 4
        source = s.hop_out.at[:M, owner * wide : (owner + 1) * wide]
        return (
            local(source, o.outs.at[c], s.piece_sem.at[owner]),
            remote(source, o.outs.at[c], s.piece_sem.at[owner], s.outs_in.at[c], (owner, w_at)),
        )

    hidden_upper = deliver_hidden(1, s.hidden, range(4))
    hidden_lower = deliver_hidden(1, s.hidden, range(RELAY // PER, 4))
    grad_m_out = deliver_rows(1, 2, s.grad_m)

    @pl.when(lower)
    def _():
        hop(s.grad_a)
        start_all(hidden_lower)
        for copy in hop_copies(s.grad_a):
            copy.wait_send()
        for k in over:
            hidden_over(k, c).start()
        normed_out.start()
        normed_out.wait()

        def bring(at, buffer):
            back = local(o.tokens.at[at], buffer, s.save_sem.at[at])
            back.start()
            back.wait()

        late = [Delivery(0, 8 + k, b, o.hidden.at[k, mine]) for k, b in enumerate((s.normed, s.grad_a))]
        for k, copy in enumerate(late):
            bring(k, (s.normed, s.grad_a)[k])
            copy.start()
        wait_all(late)
        bring(4, s.normed)
        copy = deliver_rows(0, 0, s.normed)
        copy.start()
        copy.wait()
        for copy in hop_copies(s.grad_m):
            copy.wait_recv()
        grad_m_out.start()

    @pl.when(upper)
    def _():
        normed_out.start()
        start_all(hidden_upper)
        for owner in range(4):
            here, there = output_copy(owner)
            pl.when(p == owner)(here.start)
            pl.when(p != owner)(there.start)

    s.grad_a[...] = mlp_backward(s, vec_m, s.vecs_m).astype(BF16)
    right_m_out = deliver_right(1, s.slope)
    vecs_m_out = deliver_vecs(1, s.vecs_m)
    start_all(right_m_out)
    vecs_m_out.start()

    @pl.when(lower)
    def _():
        wait_all(hidden_lower)
        for k in over:
            hidden_over(k, c).wait_send()

    @pl.when(upper)
    def _():
        wait_all(hidden_upper)

    grad_a_out = Delivery(0, 4 + 3, s.grad_a, o.right.at[3, mine])
    grad_a_out.start()
    grad_out = attention_backward(s, vec_a, s.hidden, s.vecs_a)
    grad_a_out.wait()

    @pl.when(upper)
    def _():
        for owner in range(4):
            here, there = output_copy(owner)
            pl.when(p == owner)(here.wait)
            pl.when(p != owner)(there.wait_send)

    s.hop_out[:M] = grad_out.astype(BF16)
    table_out = local(s.rel, o.table, s.out_sem.at[3])
    right_a_out = [deliver_rows(0, 2, s.hop_out.at[:M])] + deliver_right(0, s.hidden, range(3))
    vecs_a_out = deliver_vecs(0, s.vecs_a)

    def merged_copy(owner):
        return local(s.slope.at[owner, :, : D // 2], o.merged.at[owner], s.piece_sem.at[owner])

    @pl.when(upper)
    def _():
        hop(s.grad_m)
        start_all(right_a_out)
        table_out.start()
        vecs_a_out.start()
        for copy in hop_copies(s.grad_m):
            copy.wait_send()

    @pl.when(lower)
    def _():
        saved = [
            local(o.tokens.at[2 + k], s.qkv.at[k], s.out_sem.at[1 + k]) for k in range(2)
        ]
        start_all(saved)
        start_all(right_a_out)
        table_out.start()
        wait_all(right_m_out)
        halves = [s.acc, s.inverse]
        for k in range(4):
            rows = slice(k * CHUNK, (k + 1) * CHUNK)
            here = slice(k % 2 * CHUNK, (k % 2 + 1) * CHUNK)
            halves[k // 2][:, here] = dot_nt(s.hop_out[:M], s.w_merge[rows])
        wait_all(saved)
        gain = jnp.concatenate([vec_a[1:2], vec_a[2:3]], 1)
        values = jnp.concatenate([s.qkv[0], s.qkv[1]], 1).astype(F32)
        grad_in, gain_grad, shift_grad = norm_backward(
            jnp.concatenate([s.acc[...], s.inverse[...]], 1), values, gain
        )
        wide = D // 8
        for owner in range(4):
            for part in range(4):
                start = part * (D // 2) + owner * wide
                s.slope[owner, :, part * wide : (part + 1) * wide] = grad_in[
                    :, start : start + wide
                ].astype(BF16)
            merged_copy(owner).start()
        s.vecs_a[1:2] = gain_grad[:, :D]
        s.vecs_a[2:3] = gain_grad[:, D:]
        s.vecs_a[7:8] = shift_grad[:, :D]
        s.vecs_a[8:9] = shift_grad[:, D:]
        vecs_a_out.start()
        for owner in range(4):
            merged_copy(owner).wait()

    @pl.when(upper)
    def _():
        wait_all(right_m_out)

    wait_all(right_a_out + [table_out, vecs_a_out, vecs_m_out, mixed_out, grad_m_out])
    pl.when(upper)(normed_out.wait)
    given = [deliver_rows(0, 0, s.normed), mixed_out, vecs_a_out, grad_a_out] + right_a_out
    given += [normed_out, grad_m_out, vecs_m_out] + right_m_out
    for copy in given:
        copy.wait_recv()

    @pl.when(lower)
    def _():
        for copy in deliver_hidden(0, s.hidden, range(2)) + hidden_lower:
            copy.wait_recv()

    @pl.when(upper)
    def _():
        for copy in hidden_upper:
            copy.wait_recv()

    @pl.when(p == 2)
    def _():
        for k in over:
            for core in range(2):
                hidden_over(k, core).wait_recv()

    for source in (2, 3):

        @pl.when(p != source)
        def _(source=source):
            wide = D // 4
            remote(
                s.hop_out.at[:M, :wide], o.outs.at[source % 2], s.piece_sem.at[0], s.outs_in.at[source % 2], (source, w_at)
            ).wait_recv()

    vec_copy.wait_send()

    @pl.when(c == 0)
    def _():
        for copy in gifts(attention_parts, s.attention_sem):
            copy.wait_send()

        @pl.when(lower)
        def _():
            for copy in merge_gifts():
                copy.wait_send()

    @pl.when(c == 1)
    def _():
        for copy in gifts(mlp_parts, s.mlp_sem):
            copy.wait_send()


def forward_backward(page_tokens, blank, cotangent, first, second, gains, biases, tables):
    channels = page_tokens.shape[-1]
    crops = blank.shape[0]
    rolls = np.stack([hop_matrix(False), hop_matrix(True)])
    operands = {
        "tokens": jnp.transpose(page_tokens, (0, 2, 1, 3)).reshape(crops, 4 * TOK, channels),
        "cotangent": cotangent,
        "first": first,
        "second": second,
        "pack": jnp.asarray(offset_pack(), BF16),
        "roll": jnp.asarray(rolls, BF16),
        "pick": jnp.asarray(np.pad(merge_matrix(), ((0, 0), (0, 0), (0, D - 4 * TOK))), BF16),
        "cot": jnp.asarray(cotangent_matrix(), BF16),
        "gains": jnp.transpose(gains, (1, 0, 2)),
        "biases": jnp.transpose(biases, (1, 0, 2)),
        "blank": blank,
        "tables": tables,
        "keys": jnp.asarray(key_matrix(), BF16),
        "regions": jnp.asarray(region_masks(), F32),
    }
    in_vmem = ("gains", "biases", "blank", "tables", "keys", "regions")
    four = (4, M, D)
    outs = {
        "left": ((2 * M, D), BF16),
        "left_b": ((2 * M, D), BF16),
        "right_b": ((2 * M, D), BF16),
        "right": ((4, 2 * M, D), BF16),
        "hidden": ((4, 2 * M, D), BF16),
        "vecs": ((2, 16, D), F32),
        "table": ((HEADS * ROWS, 128), F32),
        "outs": ((2, M, D // 4), BF16),
        "merged": ((4, M, D // 2), BF16),
        "tokens": ((5, M, D), BF16),
    }
    scratch = {
        "w_qkv": pltpu.VMEM((STEPS, D, 3 * GROUP), BF16),
        "w_out": pltpu.VMEM((STEPS, GROUP, D), BF16),
        "w1": pltpu.VMEM((CHUNKS, D, CHUNK), BF16),
        "w2": pltpu.VMEM((CHUNKS, CHUNK, D), BF16),
        "w_merge": pltpu.VMEM((2 * D, D), BF16),
        "x": pltpu.VMEM((M, D), F32),
        "normed": pltpu.VMEM((M, D), BF16),
        "mixed": pltpu.VMEM((M, D), BF16),
        "qkv": pltpu.VMEM((3, M, D), BF16),
        "exps": pltpu.VMEM((WINS, HEADS, ROWS, 128), BF16),
        "inverse": pltpu.VMEM((M, D), F32),
        "mid": pltpu.VMEM((M, D), BF16),
        "hidden": pltpu.VMEM(four, BF16),
        "slope": pltpu.VMEM(four, BF16),
        "pre": pltpu.VMEM((2, M, CHUNK), F32),
        "acc": pltpu.VMEM((M, D), F32),
        "hop_out": pltpu.VMEM((M + ROWS, D), BF16),
        "grad_m": pltpu.VMEM((M, D), BF16),
        "grad_a": pltpu.VMEM((M, D), BF16),
        "rel": pltpu.VMEM((HEADS * ROWS, 128), F32),
        "mask": pltpu.VMEM((WINS, ROWS, 128), F32),
        "vec": pltpu.VMEM((2, 16, D), F32),
        "vecs_a": pltpu.VMEM((16, D), F32),
        "vecs_m": pltpu.VMEM((16, D), F32),
        "tokens": pltpu.VMEM((2, 4 * TOK, channels), BF16),
        "table": pltpu.VMEM((HEADS, OFFSETS), F32),
        "cotangent": pltpu.VMEM((TOK, D), BF16),
        "roll": pltpu.VMEM((M, M + ROWS), BF16),
        "const_sem": DMA((7,)),
        "pick_sem": DMA((4,)),
        "token_sem": DMA((2,)),
        "vec_sem": DMA((2,)),
        "attention_sem": DMA((4 * STEPS,)),
        "mlp_sem": DMA((2 * CHUNKS,)),
        "merge_sem": DMA((2, STEPS)),
        "give_sem": DMA((16,)),
        "out_sem": DMA((4,)),
        "give_out": DMA((2, 12)),
        "give_in": DMA((2, 12)),
        "save_sem": DMA((5,)),
        "over_sem": DMA((4,)),
        "over_in": DMA((2, 4)),
        "outs_in": DMA((2,)),
        "piece_sem": DMA((4,)),
        "hop_sem": DMA((6,)),
    }
    found = pl.pallas_call(
        functools.partial(main_kernel, tuple(operands), tuple(outs), tuple(scratch)),
        in_specs=[IN_VMEM if k in in_vmem else ANYWHERE for k in operands],
        out_specs=[ANYWHERE] * len(outs),
        out_shape=[shape_of(*value) for value in outs.values()],
        scratch_shapes=list(scratch.values()),
        compiler_params=pltpu.CompilerParams(
            collective_id=1, has_side_effects=True, vmem_limit_bytes=61 * 1024 * 1024
        ),
        name="forward_backward",
    )(*operands.values())
    return dict(zip(outs, found))


PIECES = 2 * HALF
AHEAD = 3
RING = AHEAD + 2
LAG = 2
LEFT = PIECES
SLOTS = PIECES + 4
OWN_PIECES = (HALF + HALF // 2, 2 * HALF - RELAY, HALF + RELAY, 2 * HALF)
EARLY = AHEAD + 1


def bit_reversed(index, bits):
    return sum(((index >> b) & 1) << (bits - 1 - b) for b in range(bits))


def by_device(p, values):
    found = values[-1]
    for index in range(len(values) - 2, -1, -1):
        found = jnp.where(p == index, values[index], found)
    return found


def reduce_kernel(bits, names, *refs):
    refs = list(refs)
    count = 1 << bits
    share = D // count
    quarter = count // 4
    i = Refs(names, refs[: len(names)])
    refs = refs[len(names) :]
    first_ref, second_ref, vecs_ref, tokens_ref, tables_ref = refs[:5]
    refs = refs[5:]
    lhs_in, lhs, rhs, vec_in, vec_own, relay, score, unroll, inner, outer, table, table_recv, send, keep, whole, merged = refs[:16]
    refs = refs[16:]
    recv = refs[:bits]
    vec_recv = refs[bits : 2 * bits]
    (
        row_sem,
        stage_send,
        stage_recv,
        vec_send_sem,
        vec_recv_sem,
        table_send_sem,
        table_recv_sem,
        const_sem,
        cross_local,
        cross_send,
        cross_recv,
        relay_send,
        relay_recv,
        ready,
    ) = refs[2 * bits :]

    p = lax.axis_index("pipe")
    w = lax.axis_index("wide")
    c = lax.rem(p, 2)
    upper = p >= 2
    pair = p + 1 - 2 * c
    across = lax.rem(p + 2, 4)
    partner = []
    mine = []
    for s in range(bits):
        bit = lax.rem(w // (1 << s), 2)
        mine.append(bit)
        partner.append(w + (1 << s) * (1 - 2 * bit))

    barrier = pltpu.get_barrier_semaphore()
    pl.semaphore_signal(barrier, inc=1, device_id=(pair, w), device_id_type=MESH)
    for s in range(bits):
        pl.semaphore_signal(barrier, inc=1, device_id=(p, partner[s]), device_id_type=MESH)

    @pl.when(upper)
    def _():
        for other in (0, 1):
            pl.semaphore_signal(barrier, inc=1, device_id=(other, w), device_id_type=MESH)
        pl.semaphore_wait(barrier, 1 + bits)

    @pl.when(jnp.logical_not(upper))
    def _():
        pl.semaphore_wait(barrier, 3 + bits)
        for other in (2, 3):
            pl.semaphore_signal(ready, inc=1, device_id=(other, w), device_id_type=MESH)

    pieces = by_device(p, OWN_PIECES)

    def columns(ref, j):
        return ref.at[j // PER, :, j % PER * PIECE : (j % PER + 1) * PIECE]

    def sources(index):
        found = [(LEFT, i.left, lhs_in.at[0])]
        found += [(j, columns(i.right, j), rhs.at[j]) for j in range(HALF)]
        if index % 2 == 0:
            found.insert(AHEAD + 1, (LEFT + 1, i.left_b, lhs_in.at[1]))
        where = ((0, HALF // 2), (RELAY, HALF), (0, RELAY), (0, HALF))[index]
        more = [(LEFT + 2, i.right_b, lhs_in.at[2])]
        more += [(HALF + j, columns(i.hidden, j), rhs.at[HALF + j]) for j in range(*where)]
        return more + found if index == 2 else found + more

    def issue(early):
        part = slice(0, EARLY) if early else slice(EARLY, None)
        for index in range(4):

            @pl.when(p == index)
            def _(index=index):
                for slot, source, target in sources(index)[part]:
                    pltpu.make_async_copy(source, target, row_sem.at[slot]).start()

    issue(True)
    pltpu.make_async_copy(i.vecs, vec_in, row_sem.at[LEFT + 3]).start()
    pltpu.make_async_copy(i.table, score, const_sem.at[0]).start()
    pltpu.make_async_copy(i.inner, inner, const_sem.at[1]).start()
    pltpu.make_async_copy(i.outer, outer, const_sem.at[2]).start()

    @pl.when(p == 2)
    def _():
        pltpu.make_async_copy(i.unroll, unroll, const_sem.at[3]).start()

    def token_copy(source, target, to):
        return pltpu.make_async_remote_copy(
            merged.at[target],
            tokens_ref.at[source],
            cross_send.at[target],
            cross_recv.at[source],
            device_id=(to, w),
            device_id_type=MESH,
        )

    def token_own(index):
        return pltpu.make_async_copy(merged.at[index], tokens_ref.at[index], cross_local)

    merged_in = pltpu.make_async_copy(i.merged, merged, const_sem.at[4])

    @pl.when(jnp.logical_not(upper))
    def _():
        merged_in.start()

    def rows_wait(slot, target):
        pltpu.make_async_copy(target, target, row_sem.at[slot]).wait()

    def turn(k, unrolled):
        rows_wait(LEFT + k, lhs_in.at[k])
        if unrolled:
            pltpu.make_async_copy(i.unroll, unroll, const_sem.at[3]).wait()
        per = max(1, 128 // share)
        at_row = lax.broadcasted_iota(jnp.int32, (128, 128), 0)
        at_lane = lax.broadcasted_iota(jnp.int32, (128, 128), 1)
        unit = jnp.where(at_row == at_lane, 1.0, 0.0).astype(BF16)
        for block in range(D // 128):
            flipped = dot_nt(unit, lhs_in[k, :, block * 128 : (block + 1) * 128]).astype(BF16)
            if unrolled:
                flipped = dot(flipped, unroll[...]).astype(BF16)
            if share >= 128:
                at = bit_reversed(block * 128 // share, bits)
                start = block * 128 % share
                lhs[k, at // quarter, at % quarter, start : start + 128] = flipped
            else:
                for q in range(per):
                    at = bit_reversed(block * per + q, bits)
                    lhs[k, at // quarter, at % quarter] = flipped[q * share : (q + 1) * share]

    def swapped(t):
        return (4 - lax.rem(t, 4)) // 4

    def stage_of(s, t):
        if s >= 2:
            return mine[s], partner[s]
        odd = swapped(t)
        return (
            mine[s] + odd * (mine[1 - s] - mine[s]),
            partner[s] + odd * (partner[1 - s] - partner[s]),
        )

    def stage_copy(s, t):
        j = piece(t)
        half, to = stage_of(s, t)
        if s == 0:
            source = send.at[lax.rem(t, RING)]
        elif s == 1:
            source = recv[0].at[j, 1 - half]
        else:
            width = count >> (s + 1)
            source = recv[s - 1].at[j, pl.ds((1 - half) * width, width)]
        return pltpu.make_async_remote_copy(
            source,
            recv[s].at[j],
            stage_send.at[s, j],
            stage_recv.at[s, j],
            device_id=(p, to),
            device_id_type=MESH,
        )

    def send_first(t):
        j = piece(t)
        slot = lax.rem(t, RING)

        @pl.when((j == 0) & (p == 2))
        def _():
            turn(0, False)

        @pl.when((j == HALF - PER) & (c == 0))
        def _():
            turn(1, False)

        @pl.when(j == by_device(p, (HALF, HALF + RELAY, PIECES, HALF)))
        def _():
            turn(2, False)

        @pl.when(t >= RING)
        def _():
            stage_copy(0, t - RING).wait_send()

        rows_wait(j, rhs.at[j])
        odd = swapped(t)
        sel = jnp.where(j < HALF - PER, 0, jnp.where(j < HALF, 1 - c, 2))
        product = dot(lhs[sel].reshape(D, 2 * M), rhs[j])
        for high in range(2):
            for low in range(2):
                bit = (1 - odd) * high + odd * low
                part = (1 - odd) * low + odd * high
                keeps = 1 - (bit - mine_first(odd)) * (bit - mine_first(odd))
                rows = (2 * high + low) * (D // 4)
                whole[2 * keeps + part] = product[rows : rows + D // 4].reshape(quarter, share, PIECE)
        send[slot] = whole[:2].astype(BF16)
        keep[slot] = whole[2:]
        stage_copy(0, t).start()

    def mine_first(odd):
        return mine[0] + odd * (mine[1] - mine[0])

    def store_out(j, values):
        @pl.when(j < HALF)
        def _():
            first_ref[:, pl.ds(pl.multiple_of(j * PIECE, PIECE), PIECE)] = values

        @pl.when(j >= HALF)
        def _():
            turned = jnp.transpose(values)

            @pl.when(p == 2)
            def _():
                relay[j - HALF] = turned

            @pl.when(p != 2)
            def _():
                second_ref[pl.ds(pl.multiple_of((j - HALF) * PIECE, PIECE), PIECE)] = turned

    def take(s, t):
        j = piece(t)
        stage_copy(s, t).wait_recv()
        half, _ = stage_of(s, t)
        if s == 0:
            kept = keep[lax.rem(t, RING)]
        elif s == 1:
            kept = recv[0][j, half].astype(F32)
        else:
            width = count >> (s + 1)
            kept = recv[s - 1][j, pl.ds(half * width, width)].astype(F32)
        total = kept + recv[s][j].astype(F32)
        if s == bits - 1:
            store_out(j, total[0])
        else:
            recv[s][j] = total.astype(BF16)
            stage_copy(s + 1, t).start()

    def piece(t):
        return by_device(
            p,
            (
                t,
                jnp.where(t < HALF, t, t + RELAY),
                jnp.where(t < RELAY, t + HALF, t - RELAY),
                t,
            ),
        )

    @pl.when(p == 2)
    def _():
        turn(2, True)

    @pl.when(p != 2)
    def _():
        turn(0, False)

    lax.fori_loop(0, AHEAD, lambda t, _: (send_first(t), 0)[1], 0)
    issue(False)

    for index in range(2):

        @pl.when(p == index)
        def _(index=index):
            merged_in.wait()
            token_own(index).start()
            for target in range(4):
                if target != index:
                    token_copy(index, target, target).start()

    def vec_copy(s):
        width = count >> (s + 1)
        held = vec_own if s == 0 else vec_recv[s - 1]
        return pltpu.make_async_remote_copy(
            held.at[pl.ds((1 - mine[s]) * width, width)],
            vec_recv[s],
            vec_send_sem.at[s],
            vec_recv_sem.at[s],
            device_id=(p, partner[s]),
            device_id_type=MESH,
        )

    def vec_start():
        rows_wait(LEFT + 3, vec_in)
        both = jnp.concatenate([vec_in[0] + vec_in[1], jnp.zeros((112, D), F32)], 0)
        per = max(1, 128 // share)
        for block in range(D // 128):
            flipped = jnp.transpose(both[:, block * 128 : (block + 1) * 128])
            if share >= 128:
                at = bit_reversed(block * 128 // share, bits)
                inside = block * 128 % share
                vec_own[at, inside : inside + 128] = flipped
            else:
                for q in range(per):
                    at = bit_reversed(block * per + q, bits)
                    vec_own[at] = flipped[q * share : (q + 1) * share]
        vec_copy(0).start()

    def vec_step(s):
        width = count >> (s + 1)
        vec_copy(s).wait_recv()
        held = vec_own if s == 0 else vec_recv[s - 1]
        total = held[pl.ds(mine[s] * width, width)] + vec_recv[s][...]
        if s == bits - 1:
            vecs_ref[...] = total[0]
        else:
            vec_recv[s][...] = total
            vec_copy(s + 1).start()

    def table_copy(s):
        to = (pair, w) if s == 0 else (p, partner[s - 1])
        return pltpu.make_async_remote_copy(
            table.at[s],
            table_recv.at[s],
            table_send_sem.at[s],
            table_recv_sem.at[s],
            device_id=to,
            device_id_type=MESH,
        )

    def table_start():
        pltpu.make_async_copy(i.table, score, const_sem.at[0]).wait()
        pltpu.make_async_copy(i.inner, inner, const_sem.at[1]).wait()
        pltpu.make_async_copy(i.outer, outer, const_sem.at[2]).wait()
        by_row = None
        for ci in range(WIN):
            rows = jnp.concatenate(
                [score[pl.ds(ri * WIN + ci, HEADS, stride=ROWS), :] for ri in range(WIN)], 0
            )
            term = split_dot(rows, inner[ci])
            by_row = term if by_row is None else by_row + term
        total = None
        for ri in range(WIN):
            term = split_dot(by_row[ri * HEADS : (ri + 1) * HEADS], outer[ri])
            total = term if total is None else total + term
        table[0] = total
        table_copy(0).start()

    def table_cross():
        x = p // 2
        return pltpu.make_async_remote_copy(
            table.at[bits + 1],
            tables_ref.at[x],
            table_send_sem.at[bits + 1],
            table_recv_sem.at[bits + 1],
            device_id=(across, w),
            device_id_type=MESH,
        )

    def table_step(s):
        table_copy(s).wait_recv()
        table[s + 1] = table[s] + table_recv[s]
        if s < bits:
            table_copy(s + 1).start()
        else:
            tables_ref[p // 2] = table[s + 1]

            @pl.when(jnp.logical_not(upper))
            def _():
                table_cross().start()

    def relay_copy(k):
        return pltpu.make_async_remote_copy(
            relay.at[k],
            second_ref.at[k * PIECE : (k + 1) * PIECE],
            relay_send.at[k],
            relay_recv.at[k],
            device_id=(1, w),
            device_id_type=MESH,
        )

    def clear(j, carry):
        second_ref[pl.ds(pl.multiple_of(j * PIECE, PIECE), PIECE)] = jnp.zeros((PIECE, share), F32)
        return carry

    lax.fori_loop(by_device(p, (HALF // 2, HALF, 0, HALF)), HALF, clear, 0)

    def sent_by(s):
        return pieces - 1 + LAG * (bits - 1 - s) - 3

    def body(t, carry):
        for s in range(bits):
            at = t - LAG * s

            @pl.when((at >= 0) & (at < pieces))
            def _(s=s, at=at):
                take(s, at)
                if s == 0:

                    @pl.when(t + AHEAD < pieces)
                    def _():
                        send_first(t + AHEAD)

        for s in range(1, bits):
            past = t - LAG * s - 3

            @pl.when((past >= 0) & (past < pieces))
            def _(s=s, past=past):
                stage_copy(s, past).wait_send()

        pl.when(t == 2)(vec_start)
        pl.when(t == 4)(table_start)
        for s in range(bits):

            @pl.when(t == 2 * s + 4)
            def _(s=s):
                vec_step(s)

        for s in range(bits + 1):

            @pl.when(t == 2 * s + 6)
            def _(s=s):
                table_step(s)

        @pl.when(upper & (t == RELAY + LAG * (bits - 1)))
        def _():
            pl.semaphore_wait(ready, 2)
            table_cross().start()

            @pl.when(p == 2)
            def _():
                for k in range(RELAY):
                    relay_copy(k).start()

        return carry

    lax.fori_loop(0, pieces + LAG * (bits - 1), body, 0)

    def drain(t, carry):
        @pl.when(t >= pieces - RING)
        def _():
            stage_copy(0, t).wait_send()

        for s in range(1, bits):

            @pl.when(t > sent_by(s))
            def _(s=s):
                stage_copy(s, t).wait_send()

        return carry

    lax.fori_loop(pieces - RING, pieces, drain, 0)
    for s in range(bits):
        vec_copy(s).wait_send()
    for s in range(bits + 1):
        table_copy(s).wait_send()
    table_cross().wait()

    for index in range(4):

        @pl.when(p == index)
        def _(index=index):
            if index < 2:
                token_own(index).wait()
                for target in range(4):
                    if target != index:
                        token_copy(index, target, target).wait_send()
            for source in range(2):
                if source != index:
                    token_copy(source, index, source).wait_recv()
            if index == 2:
                for k in range(RELAY):
                    relay_copy(k).wait_send()
            if index == 1:
                for k in range(RELAY):
                    relay_copy(k).wait_recv()


def reduce_gradients(made, count):
    bits = count.bit_length() - 1
    share = D // count
    anywhere = pl.BlockSpec(memory_space=pl.ANY)
    in_vmem = pl.BlockSpec(memory_space=pltpu.VMEM)
    inner, outer = offset_blocks()
    flat = (HEADS * ROWS, 128)
    operands = {name: made[name] for name in made if name not in ("tokens", "outs")}
    operands["unroll"] = jnp.asarray(unroll_matrix(), BF16)
    operands["inner"] = jnp.asarray(inner, BF16)
    operands["outer"] = jnp.asarray(outer, BF16)
    merged = made["merged"]
    dma = pltpu.SemaphoreType.DMA
    halves = [(2, count // 4)] + [(count >> (s + 1),) for s in range(1, bits)]
    return pl.pallas_call(
        functools.partial(reduce_kernel, bits, tuple(operands)),
        in_specs=[anywhere] * len(operands),
        out_specs=[in_vmem] * 3 + [anywhere] + [in_vmem],
        out_shape=[
            shape_of((share, FF), F32),
            shape_of((FF, share), F32),
            shape_of((share, 128), F32),
            shape_of((2,) + merged.shape[1:], BF16),
            shape_of((2, HEADS, OFFSETS), F32),
        ],
        scratch_shapes=[
            pltpu.VMEM((3, 2 * M, D), BF16),
            pltpu.VMEM((3, 4, count // 4, share, 2 * M), BF16),
            pltpu.VMEM((PIECES, 2 * M, PIECE), BF16),
            pltpu.VMEM((2, 16, D), F32),
            pltpu.VMEM((count, share, 128), F32),
            pltpu.VMEM((RELAY, PIECE, share), F32),
            pltpu.VMEM(flat, F32),
            pltpu.VMEM((2 * M, 2 * M), BF16),
            pltpu.VMEM(inner.shape, BF16),
            pltpu.VMEM(outer.shape, BF16),
            pltpu.VMEM((bits + 2, HEADS, OFFSETS), F32),
            pltpu.VMEM((bits + 1, HEADS, OFFSETS), F32),
            pltpu.VMEM((RING, 2, count // 4, share, PIECE), BF16),
            pltpu.VMEM((RING, 2, count // 4, share, PIECE), F32),
            pltpu.VMEM((4, count // 4, share, PIECE), F32),
            pltpu.VMEM(merged.shape, BF16),
            *[pltpu.VMEM((PIECES,) + half + (share, PIECE), BF16) for half in halves],
            *[pltpu.VMEM((count >> (s + 1), share, 128), F32) for s in range(bits)],
            dma((SLOTS,)),
            dma((bits, PIECES)),
            dma((bits, PIECES)),
            dma((bits,)),
            dma((bits,)),
            dma((bits + 2,)),
            dma((bits + 2,)),
            dma((5,)),
            dma,
            dma((4,)),
            dma((2,)),
            dma((RELAY,)),
            dma((RELAY,)),
            pltpu.SemaphoreType.REGULAR,
        ],
        compiler_params=pltpu.CompilerParams(
            collective_id=0, has_side_effects=True, vmem_limit_bytes=60 * 1024 * 1024
        ),
        name="reduce_gradients",
    )(*operands.values())


def finish_kernel(
    first_in, second_in, vecs_in, outs_in, parts_in, tables_in, order_in, split_in,
    output_ref, tokens_ref, first_out, second_out, gains_ref, biases_ref, tables_out,
    vecs_ref, outs_ref, parts_ref, tables_ref, order_ref, split_ref, first_ref, second_ref, sems,
):
    copies = [
        pltpu.make_async_copy(source, target, sems.at[k])
        for k, (source, target) in enumerate(
            (
                (parts_in, parts_ref),
                (split_in, split_ref),
                (outs_in, outs_ref),
                (order_in, order_ref),
                (tables_in, tables_ref),
                (vecs_in, vecs_ref),
                (first_in, first_ref),
                (second_in, second_ref),
            )
        )
    ]
    for copy in copies:
        copy.start()
    for copy in copies[:6]:
        copy.wait()
    on = []
    for copy, source, target in ((copies[6], first_ref, first_out), (copies[7], second_ref, second_out)):
        copy.wait()
        on.append(pltpu.make_async_copy(source, target, sems.at[8 + len(on)]))
        on[-1].start()
    tables_out[...] = tables_ref[:, :, : SPAN * SPAN]
    vecs = jnp.transpose(vecs_ref[...])
    for row in range(3):
        gains_ref[row] = vecs[row : row + 1]
    for row in range(6):
        biases_ref[row] = vecs[3 + row : 4 + row]
    channels = tokens_ref.shape[-1]
    for crop in range(WINS):
        windows = []
        for half in range(2):
            window = 2 * crop + half
            core, k = window // WINS, window % WINS
            windows.append((core, slice(k * ROWS, (k + 1) * ROWS)))
        rolled = jnp.concatenate([outs_ref[core, rows] for core, rows in windows], 0)
        output_ref[crop] = dot(order_ref[...], rolled).astype(BF16)
        total = None
        for half, (core, rows) in enumerate(windows):
            cells = jnp.concatenate(
                [parts_ref[core, rows, t * channels : (t + 1) * channels] for t in range(4)], 0
            )
            term = dot(split_ref[half], cells)
            total = term if total is None else total + term
        tokens_ref[crop] = total
    for copy in on:
        copy.wait()


def finish(out_parts, first_part, second_part, vec_part, token_parts, table_parts):
    share = first_part.shape[0]
    split = np.transpose(merge_matrix(), (0, 2, 1))
    channels = token_parts.shape[-1] // 4
    return pl.pallas_call(
        finish_kernel,
        in_specs=[ANYWHERE] * 8,
        out_specs=[IN_VMEM] * 2 + [ANYWHERE] * 2 + [IN_VMEM] * 3,
        out_shape=[
            shape_of((WINS, TOK, out_parts.shape[-1]), BF16),
            shape_of((WINS, 4 * TOK, channels), F32),
            shape_of(first_part.shape, F32),
            shape_of(second_part.shape, F32),
            shape_of((3, 1, share), F32),
            shape_of((6, 1, share), F32),
            shape_of((2, HEADS, SPAN * SPAN), F32),
        ],
        scratch_shapes=[
            pltpu.VMEM(vec_part.shape, F32),
            pltpu.VMEM(out_parts.shape, BF16),
            pltpu.VMEM(token_parts.shape, BF16),
            pltpu.VMEM(table_parts.shape, F32),
            pltpu.VMEM((TOK, 2 * ROWS), BF16),
            pltpu.VMEM(split.shape, BF16),
            pltpu.VMEM(first_part.shape, F32),
            pltpu.VMEM(second_part.shape, F32),
            DMA((10,)),
        ],
        compiler_params=pltpu.CompilerParams(vmem_limit_bytes=61 * 1024 * 1024),
        name="finish",
    )(
        first_part,
        second_part,
        vec_part,
        out_parts,
        token_parts,
        table_parts,
        jnp.asarray(output_matrix(), BF16),
        jnp.asarray(split, BF16),
    )


def padded_row(token):
    return (token // AREA) * ROWS + token % AREA


def rolled_source():
    cells = np.arange(TOK)
    rows, columns = cells // GRID_W, cells % GRID_W
    return ((rows + WIN // 2) % GRID_H) * GRID_W + (columns + WIN // 2) % GRID_W


def hop_matrix(inverse):
    source = rolled_source()
    if inverse:
        source = np.argsort(source)
    result = np.zeros((2, M, (WINS + 1) * ROWS), np.float32)
    for core in range(2):
        for k in range(WINS):
            window = WINS * core + k
            crop, part = window // 2, window % 2
            for t in range(AREA):
                token = source[part * AREA + t]
                taken = crop * 2 + token // AREA
                slot = taken - WINS * core
                if not 0 <= slot < WINS:
                    slot = WINS
                result[core, k * ROWS + t, slot * ROWS + token % AREA] = 1.0
    return result


def cotangent_matrix():
    source = rolled_source()
    result = np.zeros((2, M, 4 * 256), np.float32)
    for core in range(2):
        for k in range(WINS):
            window = WINS * core + k
            crop, part = window // 2, window % 2
            for t in range(AREA):
                result[core, k * ROWS + t, crop * 256 + source[part * AREA + t]] = 1.0
    return result


def output_matrix():
    source = rolled_source()
    result = np.zeros((TOK, 2 * ROWS), np.float32)
    for t in range(TOK):
        result[source[t], padded_row(t)] = 1.0
    return result


def offset_matrices():
    span = 2 * WIN - 1
    inner = np.zeros((WIN, 128, WIN, span), np.float32)
    outer = np.zeros((WIN, WIN, span, span, span), np.float32)
    for ci in range(WIN):
        for j in range(AREA):
            inner[ci, j, j // WIN, ci - j % WIN + WIN - 1] = 1.0
    for ri in range(WIN):
        for rj in range(WIN):
            for dc in range(span):
                outer[ri, rj, dc, ri - rj + WIN - 1, dc] = 1.0
    return (
        inner.reshape(WIN * 128, WIN * span),
        outer.reshape(WIN * WIN * span, span * span),
    )


def offset_blocks():
    inner, outer = offset_matrices()
    inner = np.pad(inner.reshape(WIN, 128, WIN * SPAN), ((0, 0), (0, 0), (0, INNER - WIN * SPAN)))
    outer = np.pad(
        outer.reshape(WIN, WIN * SPAN, SPAN * SPAN),
        ((0, 0), (0, INNER - WIN * SPAN), (0, OFFSETS - SPAN * SPAN)),
    )
    return inner, outer


def offset_pack():
    inner, outer = offset_blocks()
    result = np.zeros((WIN // 2, INNER, D), np.float32)
    for k in range(WIN):
        half = k % 2
        result[k // 2, :, half * OFFSETS : (half + 1) * OFFSETS] = outer[k]
        result[k // 2, half * 128 : (half + 1) * 128, 2 * OFFSETS :] = inner[k]
    return result


def unroll_matrix():
    source = rolled_source()
    result = np.zeros((2 * M, 2 * M), np.float32)
    for crop in range(WINS):
        for t in range(TOK):
            start = crop * 2 * ROWS
            result[start + padded_row(t), start + padded_row(source[t])] = 1.0
    return result


def merge_matrix():
    result = np.zeros((2, 4, ROWS, 2 * GRID_W, 2 * GRID_H), np.float32)
    for half in range(2):
        for part in range(4):
            right, down = part // 2, part % 2
            for t in range(AREA):
                result[half, part, t, 2 * (t % WIN) + right, 2 * (half * WIN + t // WIN) + down] = 1.0
    return result.reshape(2, 4 * ROWS, 4 * TOK)


def region_masks():
    cells = np.arange(TOK)
    rows_at, cols_at = cells // GRID_W, cells % GRID_W
    row_band = (rows_at >= GRID_H - WIN).astype(int) + (rows_at >= GRID_H - WIN // 2)
    col_band = (cols_at >= GRID_W - WIN).astype(int) + (cols_at >= GRID_W - WIN // 2)
    rolled = (row_band * 3 + col_band).reshape(2, AREA)
    result = np.zeros((4, ROWS, 128), np.float32)
    for part in range(2):
        result[part, :AREA, :AREA] = 1.0
        result[2 + part, :AREA, :AREA] = rolled[part][:, None] == rolled[part][None, :]
    return result


def key_matrix():
    source = rolled_source()
    result = np.zeros((TOK, 4, 128), np.float32)
    for part in range(2):
        for t in range(AREA):
            result[part * AREA + t, part, t] = 1.0
            result[source[part * AREA + t], 2 + part, t] = 1.0
    return result.reshape(TOK, 4 * 128)


def local(page_tokens, blank, cotangent, first, second, gains, biases, tables):
    count = lax.axis_size("wide")
    made = forward_backward(
        page_tokens, blank, cotangent, first[0], second[0], gains, biases, tables
    )
    output, token_grad, first_grad, second_grad, gain_grad, bias_grad, table_grad = finish(
        made["outs"], *reduce_gradients(made, count)
    )
    crops, rows, columns, channels = page_tokens.shape
    token_grad = token_grad.reshape(crops, columns, rows, channels // 4)
    return (
        output,
        jnp.transpose(token_grad, (0, 2, 1, 3)),
        first_grad[None],
        second_grad[None],
        jnp.transpose(gain_grad, (1, 0, 2)),
        jnp.transpose(bias_grad, (1, 0, 2)),
        table_grad,
    )


def solution(mesh):
    placed = (
        P("wide", None, None, None),
        P("wide", None),
        P("wide", None, None),
        P("pipe", None, None),
        P("pipe", None, None),
        P("pipe", None, None),
        P("pipe", None, None),
        P(),
    )
    return jax.shard_map(
        local,
        mesh=mesh,
        in_specs=placed,
        out_specs=(
            P("wide", None, "pipe"),
            P("wide", None, None, "pipe"),
            P("pipe", "wide", None),
            P("pipe", None, "wide"),
            P("pipe", None, "wide"),
            P("pipe", None, "wide"),
            P(),
        ),
        check_vma=False,
    )
```
